32 devices in a mesh: runs: 2 (over x), tp: 8 (over z, y), dp: 2 (over core).
Axes of the slice: x: 2, y: 2, z: 4, core: 2. Of those that a mesh axis runs over, the one named last changes fastest.
Arguments:
- grad_out: bfloat16 [4, 256, 4096], P(('runs', 'dp'), 'tp'), parts along dimension 0, may hold values from -1 to 1
- hidden: bfloat16 [4, 256, 3584], P(('runs', 'dp'), None, 'tp'), parts along dimension 0, may hold values from -6 to 6
- feedback: bfloat16 [4, 3584, 4096], P(('runs', 'dp'), 'tp'), parts along dimension 0, may hold values from -100 to 100
- right_factor: float32 [64, 4096], replicated, may hold values from -6 to 6
Outputs:
- new_feedback: bfloat16 [4, 3584, 4096], P(('runs', 'dp'), 'tp'), parts along dimension 0
- new_factor: float32 [128, 4096], P('runs'), parts along dimension 0
The draws below stay inside these ranges and needn't reach their ends.
There are 2 independent parts, one for each index of `runs`. The reference program is written for one: setup_inputs(seed, part) draws one part's arguments, and reference() takes and returns one part's arrays. A program takes and returns all parts, laid end to end along the dimension named above; an argument that names none is the same for every part. Nothing has to cross between parts.
All inputs are finite; a program needn't handle non-finite values.
Results may differ from the reference program's by a relative error of at most 0.0004.
Values may be sent and summed in bfloat16 or wider, within the bound.
No kernel may reach another device: no remote copies, remote signals or barrier semaphores. Data moves between devices by JAX's collectives and lax.ppermute only.
A program may use at most 64 MiB of HBM per device.

```python
import math
import jax
import jax.numpy as jnp
from jax import lax

D = 4096
RANK = 64
FF = 3584
TOK = 256
N_DP = 2


def draw_feedback(key, part):
    key = jax.random.fold_in(key, 7)
    key_rows, key_cols, key_base = jax.random.split(key, 3)
    row_scale = jnp.exp(jax.random.uniform(key_rows, (N_DP, FF, 1), jnp.float32) * math.log(10.0))
    trend = 1.0 + 2.0 * jnp.arange(FF, dtype=jnp.float32) / FF
    row_scale = row_scale * trend[None, :, None]
    col_scale = jnp.exp(jax.random.uniform(key_cols, (N_DP, 1, D), jnp.float32) * math.log(10.0))
    base = jnp.clip(jax.random.normal(key_base, (N_DP, FF, D), jnp.float32), -6.0, 6.0)
    values = 0.05 * row_scale * col_scale * base
    return values.astype(jnp.bfloat16)


def block_scale(key, shape, shards, smallest, high):
    level = 1.0
    for position, parts in shards:
        steps = jax.random.uniform(jax.random.fold_in(jax.random.fold_in(key, 6), position), (parts,), jnp.float32, smallest / len(shards), high / len(shards))
        level = level * jnp.repeat(jnp.exp(steps), shape[position] // parts).reshape((-1,) + (1,) * (len(shape) - 1 - position))
    return level


def gaussian(stream_key, dims, spread, limit, pieces=(), kind=jnp.bfloat16):
    factor_of = block_scale(stream_key, dims, pieces, -0.22, 0.18) if pieces else 1.0
    result = jax.random.normal(stream_key, dims, jnp.float32) * spread * factor_of
    return jnp.minimum(jnp.maximum(result, -limit), limit).astype(kind)


def setup_inputs(seed: int = 0, part: int = 0) -> dict:
    arg_keys = jax.random.split(jax.random.key(seed), 5)
    own_keys = jax.random.split(jax.random.fold_in(arg_keys[4], part), 5)
    grad_out = gaussian(own_keys[0], (N_DP, TOK, D), (TOK ** -0.5), 1.0, ((0, 2), (1, 8)))
    hidden = gaussian(own_keys[1], (N_DP, TOK, FF), 1.0, 6.0, ((0, 2), (2, 8)))
    feedback = draw_feedback(jax.random.fold_in(jax.random.fold_in(arg_keys[4], part), 71), part)
    right_factor = gaussian(arg_keys[3], (RANK, D), 1.0, 6.0, (), jnp.float32)
    return {"grad_out": grad_out, "hidden": hidden, "feedback": feedback, "right_factor": right_factor}


def reference(grad_out, hidden, feedback, right_factor):
    highest = lax.Precision.HIGHEST
    merged_list = []
    for replica in range(N_DP):
        product = jnp.dot(hidden[replica].T.astype(jnp.float32), grad_out[replica].astype(jnp.float32), preferred_element_type=jnp.float32)
        merged_list.append(product + feedback[replica].astype(jnp.float32))
    left_sum = jnp.zeros((FF, RANK), jnp.float32)
    for merged in merged_list:
        left_sum = left_sum + jnp.dot(merged, right_factor.T, precision=highest)
    gram_matrix = jnp.dot(left_sum.T, left_sum, precision=highest)
    lower_factor = jnp.linalg.cholesky(gram_matrix)
    left_orth = lax.linalg.triangular_solve(lower_factor, left_sum, left_side=False, lower=True, transpose_a=True)
    new_factor = jnp.zeros((RANK, D), jnp.float32)
    for merged in merged_list:
        new_factor = new_factor + jnp.dot(left_orth.T, merged, precision=highest)
    new_factor = new_factor / N_DP
    approx = jnp.dot(left_orth, new_factor, precision=highest)
    new_feedback = jnp.stack([(merged - approx).astype(jnp.bfloat16) for merged in merged_list])
    return (new_feedback, new_factor)
```

```python
import functools

import jax
import jax.numpy as jnp
import numpy as np
from jax import lax
from jax.experimental import pallas as pl
from jax.experimental.pallas import tpu as pltpu
from jax.sharding import PartitionSpec as P

F32 = jnp.float32
BF16 = jnp.bfloat16
HIGHEST = lax.Precision.HIGHEST
VMEM_LIMIT = 40 * 1024 * 1024


def split3(value):
    high = value.astype(BF16)
    rest = value - high.astype(F32)
    middle = rest.astype(BF16)
    low = (rest - middle.astype(F32)).astype(BF16)
    return high, middle, low


def fold3(stacked):
    rank = stacked.shape[0] // 3
    return stacked[:rank] + stacked[rank : 2 * rank] + stacked[2 * rank :]


def nn(a, b):
    return lax.dot_general(a, b, (((1,), (0,)), ((), ())), preferred_element_type=F32)


def nt(a, b):
    return lax.dot_general(a, b, (((1,), (1,)), ((), ())), preferred_element_type=F32)


def params(semantics=None):
    return pltpu.CompilerParams(vmem_limit_bytes=VMEM_LIMIT, dimension_semantics=semantics)


def whole(shape):
    return pl.BlockSpec(shape, lambda *_: (0,) * len(shape))


def residue_kernel(right, feedback, terms, left_t, total):
    step = pl.program_id(0)
    stacked = jnp.concatenate(split3(right[...]), axis=0)
    terms[...] = stacked
    part = nt(stacked, feedback[...])

    @pl.when(step == 0)
    def _():
        total[...] = part

    @pl.when(step > 0)
    def _():
        total[...] += part

    @pl.when(step == pl.num_programs(0) - 1)
    def _():
        left_t[...] = fold3(total[...])


def residue_left(right, feedback):
    rank, width = right.shape
    rows = feedback.shape[0]
    steps = 4
    cols = width // steps
    return pl.pallas_call(
        residue_kernel,
        grid=(steps,),
        in_specs=[
            pl.BlockSpec((rank, cols), lambda j: (0, j)),
            pl.BlockSpec((rows, cols), lambda j: (0, j)),
        ],
        out_specs=[pl.BlockSpec((3 * rank, cols), lambda j: (0, j)), whole((rank, rows))],
        out_shape=[
            jax.ShapeDtypeStruct((3 * rank, width), BF16),
            jax.ShapeDtypeStruct((rank, rows), F32),
        ],
        scratch_shapes=[pltpu.VMEM((3 * rank, rows), F32)],
        compiler_params=params(("arbitrary",)),
        name="residue_left",
    )(right, feedback)


def left_kernel(places, *refs):
    count = places.shape[1]
    pieces, (terms, residue_t, hidden_t, tokens, left_t) = refs[:count], refs[count:]
    here = lax.axis_index("tp")
    for index, piece in enumerate(pieces):
        size = piece.shape[0]
        tokens[pl.ds(pl.multiple_of(places[here, index] * size, size), size), :] = piece[...]
    projected = fold3(nt(terms[...], tokens[...]))
    stacked = jnp.concatenate(split3(projected), axis=0)
    left_t[...] = residue_t[...] + fold3(nt(stacked, hidden_t[...]))


def left_factor(places, pieces, terms, residue_t, hidden_t):
    rows, count = hidden_t.shape
    width = terms.shape[1]
    operands = [*pieces, terms, residue_t, hidden_t]
    return pl.pallas_call(
        left_kernel,
        in_specs=[pl.BlockSpec(memory_space=pltpu.SMEM)]
        + [pl.BlockSpec(memory_space=pltpu.VMEM)] * len(operands),
        out_specs=[pl.BlockSpec(memory_space=pltpu.VMEM)] * 2,
        out_shape=[
            jax.ShapeDtypeStruct((count, width), BF16),
            jax.ShapeDtypeStruct(residue_t.shape, F32),
        ],
        compiler_params=params(),
        name="left_factor",
    )(jnp.asarray(places), *operands)


def right_kernel(here_l, other_l, hidden_t, feedback, tokens, keep, give, gram, left_sum, lhs, rhs):
    step = pl.program_id(0)
    chip, core = lax.axis_index("tp"), lax.axis_index("dp")
    half = keep.shape[2]

    @pl.when(step == 0)
    def _():
        left_t = here_l[...] + other_l[...]
        left_sum[...] = left_t
        gram[...] = lax.dot_general(
            left_t, left_t, (((1,), (1,)), ((), ())), precision=HIGHEST, preferred_element_type=F32
        )
        stacked = jnp.concatenate(split3(left_t), axis=0)
        lhs[...] = stacked
        seen_t = fold3(nn(stacked, hidden_t[...]))
        rhs[...] = jnp.concatenate(split3(seen_t), axis=0)

    block = fold3(nn(lhs[...], feedback[...]) + nn(rhs[...], tokens[...]))
    first, second = block[:, :half], block[:, half:]
    place = step ^ chip
    keep[place] = jnp.where(core == 0, first, second)
    give[place] = jnp.where(core == 0, second, first)


def right_factor_terms(here_l, other_l, hidden_t, feedback, tokens, chips):
    rank, rows = here_l.shape
    count, width = tokens.shape
    cols = width // chips
    half = cols // 2
    return pl.pallas_call(
        right_kernel,
        grid=(chips,),
        in_specs=[
            whole((rank, rows)),
            whole((rank, rows)),
            whole((rows, count)),
            pl.BlockSpec((rows, cols), lambda j: (0, j)),
            pl.BlockSpec((count, cols), lambda j: (0, j)),
        ],
        out_specs=[
            whole((chips, rank, half)),
            whole((chips, rank, half)),
            whole((rank, rank)),
            whole((rank, rows)),
        ],
        out_shape=[
            jax.ShapeDtypeStruct((chips, rank, half), F32),
            jax.ShapeDtypeStruct((chips, rank, half), F32),
            jax.ShapeDtypeStruct((rank, rank), F32),
            jax.ShapeDtypeStruct((rank, rows), F32),
        ],
        scratch_shapes=[pltpu.VMEM((3 * rank, rows), BF16), pltpu.VMEM((3 * rank, count), BF16)],
        compiler_params=params(("arbitrary",)),
        name="right_terms",
    )(here_l, other_l, hidden_t, feedback, tokens)


def message_kernel(keep, got, gram, *messages):
    chips, rank, half = keep.shape
    blocks = half // rank
    rows = rank // blocks
    for index, message in enumerate(messages):
        message[:rank, :] = keep[index] + got[index]
        for block in range(blocks):
            message[rank:, block * rank : (block + 1) * rank] = gram[block * rows : (block + 1) * rows, :]


def messages_for(keep, got, gram):
    chips, rank, half = keep.shape
    rows = rank + rank // (half // rank)
    return pl.pallas_call(
        message_kernel,
        in_specs=[pl.BlockSpec(memory_space=pltpu.VMEM)] * 3,
        out_specs=[pl.BlockSpec(memory_space=pltpu.VMEM)] * chips,
        out_shape=[jax.ShapeDtypeStruct((rows, half), F32)] * chips,
        compiler_params=params(),
        name="messages",
    )(keep, got, gram)


def sum_kernel(*refs):
    messages, (share, gram) = refs[:-2], refs[-2:]
    parts = [message[...] for message in messages]
    while len(parts) > 1:
        parts = [a + b for a, b in zip(parts[::2], parts[1::2])]
    total = parts[0]
    rank, half = share.shape
    blocks = half // rank
    rows = rank // blocks
    share[...] = total[:rank]
    for block in range(blocks):
        gram[block * rows : (block + 1) * rows, :] = total[rank:, block * rank : (block + 1) * rank]


def summed(messages, rank):
    half = messages[0].shape[1]
    return pl.pallas_call(
        sum_kernel,
        in_specs=[pl.BlockSpec(memory_space=pltpu.VMEM)] * len(messages),
        out_specs=[pl.BlockSpec(memory_space=pltpu.VMEM)] * 2,
        out_shape=[jax.ShapeDtypeStruct((rank, half), F32), jax.ShapeDtypeStruct((rank, rank), F32)],
        compiler_params=params(),
        name="sum_messages",
    )(*messages)


def inverse_kernel(gram, inverse):
    rank = gram.shape[0]
    row = lax.broadcasted_iota(jnp.int32, (rank, 2 * rank), 0)
    lane = lax.broadcasted_iota(jnp.int32, (rank, 2 * rank), 1)
    eye = (lane[:, rank:] == row[:, rank:] + rank).astype(F32)
    table = jnp.concatenate([gram[...], eye], axis=1)
    scale = jnp.zeros((rank, 1), F32)
    for pivot in range(rank):
        line = table[pivot : pivot + 1, :]
        column = table[:, pivot : pivot + 1]
        top = line[:, pivot : pivot + 1]
        scale = jnp.where(row[:, :1] == pivot, lax.rsqrt(top), scale)
        if pivot + 1 < rank:
            factor = jnp.where(row[:, :1] > pivot, column / top, 0.0)
            table = table - factor * line
    inverse[...] = table[:, rank:] * scale


def cholesky_inverse(gram):
    return pl.pallas_call(
        inverse_kernel,
        in_specs=[pl.BlockSpec(memory_space=pltpu.VMEM)],
        out_specs=pl.BlockSpec(memory_space=pltpu.VMEM),
        out_shape=jax.ShapeDtypeStruct(gram.shape, F32),
        compiler_params=params(),
        name="cholesky_inverse",
    )(gram)


def final_kernel(replicas, mine, theirs, inverse, left_sum, hidden_t, feedback, tokens, out, factor, lhs, rhs):
    step = pl.program_id(0)
    chip, core = lax.axis_index("tp"), lax.axis_index("dp")
    rows, count = hidden_t.shape
    rank = inverse.shape[0]

    @pl.when(step == 0)
    def _():
        orth_t = jnp.dot(inverse[...], left_sum[...], precision=HIGHEST, preferred_element_type=F32)
        high, middle, low = split3(-orth_t.T)
        lhs[:, :count] = hidden_t[...]
        for place, term in enumerate((high, high, high, middle, middle, low)):
            lhs[:, count + place * rank : count + (place + 1) * rank] = term

    place = step ^ chip
    here, there = mine[place], theirs[place]
    block = jnp.concatenate(
        [jnp.where(core == 0, here, there), jnp.where(core == 0, there, here)], axis=1
    )
    new = jnp.dot(inverse[...], block, precision=HIGHEST, preferred_element_type=F32) * (1.0 / replicas)
    factor[...] = new
    high, middle, low = split3(new)
    rhs[:count, :] = tokens[...]
    for place, term in enumerate((high, middle, low, high, middle, high)):
        rhs[count + place * rank : count + (place + 1) * rank, :] = term
    out[...] = (nn(lhs[...], rhs[...]) + feedback[...].astype(F32)).astype(BF16)


def finish(mine, theirs, inverse, left_sum, hidden_t, feedback, tokens, replicas):
    chips, rank, half = mine.shape
    rows, count = hidden_t.shape
    width = tokens.shape[1]
    cols = width // chips
    depth = count + 6 * rank
    return pl.pallas_call(
        functools.partial(final_kernel, replicas),
        grid=(chips,),
        in_specs=[
            whole(mine.shape),
            whole(mine.shape),
            whole((rank, rank)),
            whole((rank, rows)),
            whole((rows, count)),
            pl.BlockSpec((rows, cols), lambda j: (0, j)),
            pl.BlockSpec((count, cols), lambda j: (0, j)),
        ],
        out_specs=[
            pl.BlockSpec((rows, cols), lambda j: (0, j)),
            pl.BlockSpec((rank, cols), lambda j: (0, j)),
        ],
        out_shape=[
            jax.ShapeDtypeStruct((rows, width), BF16),
            jax.ShapeDtypeStruct((rank, width), F32),
        ],
        scratch_shapes=[pltpu.VMEM((rows, depth), BF16), pltpu.VMEM((depth, cols), BF16)],
        compiler_params=params(("arbitrary",)),
        name="finish",
    )(mine, theirs, inverse, left_sum, hidden_t, feedback, tokens)


def ring_order(chips):
    if chips == 8:
        return [0, 1, 3, 5, 7, 6, 4, 2]
    return list(range(chips))


def ring_gather(shard, chips):
    order = ring_order(chips)
    position = {chip: place for place, chip in enumerate(order)}
    right = [(order[i], order[(i + 1) % chips]) for i in range(chips)]
    left = [(b, a) for a, b in right]
    size = shard.shape[0] // 2
    halves = [shard[:size], shard[size:]]
    pieces = list(halves)
    origin = [(0, 0), (0, 1)]
    going = {(way, half): halves[half] for way in (1, -1) for half in (0, 1)}
    far = chips // 2
    for hop in range(1, far + 1):
        for way, pairs in ((1, right), (-1, left)):
            for half in (0, 1):
                if hop == far and (half == 0) != (way == 1):
                    continue
                going[way, half] = lax.ppermute(going[way, half], "tp", pairs)
                pieces.append(going[way, half])
                origin.append((-way * hop, half))
    places = np.zeros((chips, len(pieces)), np.int32)
    for chip in range(chips):
        for index, (shift, half) in enumerate(origin):
            places[chip, index] = 2 * order[(position[chip] + shift) % chips] + half
    return pieces, places


def swap(value):
    return lax.ppermute(value, "dp", [(0, 1), (1, 0)])


def local(grad_out, hidden, feedback, right_factor):
    shard, residue = grad_out[0], feedback[0]
    hidden_t = hidden[0].T
    chips, replicas = lax.axis_size("tp"), lax.axis_size("dp")
    rank = right_factor.shape[0]
    pairs = [[(i, i ^ k) for i in range(chips)] for k in range(chips)]

    pieces, places = ring_gather(shard, chips)
    terms, residue_t = residue_left(right_factor, residue)
    tokens, left_t = left_factor(places, pieces, terms, residue_t, hidden_t)
    keep, give, gram, left_sum = right_factor_terms(
        left_t, swap(left_t), hidden_t, residue, tokens, chips
    )
    messages = messages_for(keep, swap(give), gram)
    received = [messages[0]] + [lax.ppermute(messages[k], "tp", pairs[k]) for k in range(1, chips)]
    share, gram_matrix = summed(received, rank)
    shares = [share] + [lax.ppermute(share, "tp", pairs[k]) for k in range(1, chips)]
    inverse = cholesky_inverse(gram_matrix)
    mine = jnp.stack(shares)
    new_feedback, new_factor = finish(
        mine, swap(mine), inverse, left_sum, hidden_t, residue, tokens, replicas
    )
    return new_feedback[None], new_factor


def solution(mesh):
    return jax.shard_map(
        local,
        mesh=mesh,
        in_specs=(
            P(("runs", "dp"), "tp", None),
            P(("runs", "dp"), None, "tp"),
            P(("runs", "dp"), "tp", None),
            P(),
        ),
        out_specs=(P(("runs", "dp"), "tp", None), P("runs", None)),
        check_vma=False,
    )
```

```python
import functools

import jax
import jax.numpy as jnp
import numpy as np
from jax import lax
from jax.experimental import pallas as pl
from jax.experimental.pallas import tpu as pltpu
from jax.sharding import PartitionSpec as P

F32 = jnp.float32
BF16 = jnp.bfloat16
HIGHEST = lax.Precision.HIGHEST
VMEM_LIMIT = 40 * 1024 * 1024
GROUP = 2


def split3(value):
    high = value.astype(BF16)
    rest = value - high.astype(F32)
    middle = rest.astype(BF16)
    low = (rest - middle.astype(F32)).astype(BF16)
    return high, middle, low


def split2(value):
    high = value.astype(BF16)
    return high, (value - high.astype(F32)).astype(BF16)


def fold3(stacked):
    rank = stacked.shape[0] // 3
    return stacked[:rank] + stacked[rank : 2 * rank] + stacked[2 * rank :]


def nn(a, b):
    return lax.dot_general(a, b, (((1,), (0,)), ((), ())), preferred_element_type=F32)


def nt(a, b):
    return lax.dot_general(a, b, (((1,), (1,)), ((), ())), preferred_element_type=F32)


def params(semantics=None, limit=VMEM_LIMIT):
    return pltpu.CompilerParams(vmem_limit_bytes=limit, dimension_semantics=semantics)


def cost(microseconds):
    return pl.CostEstimate(flops=int(microseconds * 1.15e9), bytes_accessed=0, transcendentals=0)


def whole(shape):
    return pl.BlockSpec(shape, lambda *_: (0,) * len(shape))


def residue_kernel(right, feedback, terms, left_t, right_here, feedback_here, sems):
    width = right.shape[1]
    steps = sems.shape[0]
    cols = width // steps
    copies = []
    for step in range(steps):
        span = slice(step * cols, (step + 1) * cols)
        copies.append(
            [
                pltpu.make_async_copy(right.at[:, span], right_here.at[:, span], sems.at[step, 0]),
                pltpu.make_async_copy(feedback.at[:, span], feedback_here.at[:, span], sems.at[step, 1]),
            ]
        )
    for pair in copies:
        for copy in pair:
            copy.start()
    total = None
    for step, pair in enumerate(copies):
        span = slice(step * cols, (step + 1) * cols)
        for copy in pair:
            copy.wait()
        stacked = jnp.concatenate(split3(right_here[:, span]), axis=0)
        terms[:, span] = stacked
        part = nt(stacked, feedback_here[:, span])
        total = part if total is None else total + part
    left_t[...] = fold3(total)


def residue_left(right, feedback):
    rank, width = right.shape
    rows = feedback.shape[0]
    return pl.pallas_call(
        residue_kernel,
        in_specs=[pl.BlockSpec(memory_space=pltpu.HBM)] * 2,
        out_specs=[pl.BlockSpec(memory_space=pltpu.VMEM)] * 2,
        out_shape=[
            jax.ShapeDtypeStruct((3 * rank, width), BF16),
            jax.ShapeDtypeStruct((rank, rows), F32),
        ],
        scratch_shapes=[
            pltpu.VMEM((rank, width), F32),
            pltpu.VMEM((rows, width), BF16),
            pltpu.SemaphoreType.DMA((4, 2)),
        ],
        compiler_params=params(),
        cost_estimate=cost(2.2),
        name="residue_left",
    )(right, feedback)


def left_kernel(places, *refs):
    count = places.shape[1]
    pieces, (terms, residue_t, hidden_t, tokens, left_t) = refs[:count], refs[count:]
    here = lax.axis_index("tp")
    for index, piece in enumerate(pieces):
        size = piece.shape[0]
        tokens[pl.ds(pl.multiple_of(places[here, index] * size, size), size), :] = piece[...]
    projected = fold3(nt(terms[...], tokens[...]))
    stacked = jnp.concatenate(split3(projected), axis=0)
    left_t[...] = residue_t[...] + fold3(nt(stacked, hidden_t[...]))


def left_factor(places, pieces, terms, residue_t, hidden_t):
    rows, count = hidden_t.shape
    width = terms.shape[1]
    operands = [*pieces, terms, residue_t, hidden_t]
    return pl.pallas_call(
        left_kernel,
        in_specs=[pl.BlockSpec(memory_space=pltpu.SMEM)]
        + [pl.BlockSpec(memory_space=pltpu.VMEM)] * len(operands),
        out_specs=[pl.BlockSpec(memory_space=pltpu.VMEM)] * 2,
        out_shape=[
            jax.ShapeDtypeStruct((count, width), BF16),
            jax.ShapeDtypeStruct(residue_t.shape, F32),
        ],
        compiler_params=params(),
        cost_estimate=cost(1.8),
        name="left_factor",
    )(jnp.asarray(places), *operands)


def core_of(place):
    return (place >> 1) & 1


def index_of(place):
    return (place >> 2) * 2 + (place & 1)


def right_kernel(here_l, other_l, hidden_t, feedback, tokens, keep, give, gram, left_sum, lhs, rhs):
    step = pl.program_id(0)
    chip, core = lax.axis_index("tp"), lax.axis_index("dp")
    cols = keep.shape[2]

    @pl.when(step == 0)
    def _():
        left_t = here_l[...] + other_l[...]
        left_sum[...] = left_t
        gram[...] = lax.dot_general(
            left_t, left_t, (((1,), (1,)), ((), ())), precision=HIGHEST, preferred_element_type=F32
        )
        stacked = jnp.concatenate(split3(left_t), axis=0)
        lhs[...] = stacked
        seen_t = fold3(nn(stacked, hidden_t[...]))
        rhs[...] = jnp.concatenate(split3(seen_t), axis=0)

    block = fold3(nn(lhs[...], feedback[...]) + nn(rhs[...], tokens[...]))
    for part in range(GROUP):
        value = block[:, part * cols : (part + 1) * cols]
        place = (GROUP * step + part) ^ chip
        ours = core_of(place) == core

        @pl.when(ours)
        def _():
            keep[index_of(place)] = value

        @pl.when(jnp.logical_not(ours))
        def _():
            give[index_of(place)] = value


def right_factor_terms(here_l, other_l, hidden_t, feedback, tokens, chips):
    rank, rows = here_l.shape
    count, width = tokens.shape
    cols = width // chips
    return pl.pallas_call(
        right_kernel,
        grid=(chips // GROUP,),
        in_specs=[
            whole((rank, rows)),
            whole((rank, rows)),
            whole((rows, count)),
            pl.BlockSpec((rows, GROUP * cols), lambda j: (0, j)),
            pl.BlockSpec((count, GROUP * cols), lambda j: (0, j)),
        ],
        out_specs=[
            whole((chips // 2, rank, cols)),
            whole((chips // 2, rank, cols)),
            whole((rank, rank)),
            whole((rank, rows)),
        ],
        out_shape=[
            jax.ShapeDtypeStruct((chips // 2, rank, cols), F32),
            jax.ShapeDtypeStruct((chips // 2, rank, cols), F32),
            jax.ShapeDtypeStruct((rank, rank), F32),
            jax.ShapeDtypeStruct((rank, rows), F32),
        ],
        scratch_shapes=[pltpu.VMEM((3 * rank, rows), BF16), pltpu.VMEM((3 * rank, count), BF16)],
        compiler_params=params(("arbitrary",)),
        cost_estimate=cost(2.8),
        name="right_terms",
    )(here_l, other_l, hidden_t, feedback, tokens)


def message_kernel(keep, got, gram, *messages):
    rank, cols = keep.shape[1:]
    blocks = cols // rank
    rows = rank // blocks
    for index, message in enumerate(messages):
        message[:rank, :] = keep[index] + got[index]
        for block in range(blocks):
            message[rank:, block * rank : (block + 1) * rank] = gram[block * rows : (block + 1) * rows, :]


def messages_for(keep, got, gram):
    places, rank, cols = keep.shape
    rows = rank + rank // (cols // rank)
    return pl.pallas_call(
        message_kernel,
        in_specs=[pl.BlockSpec(memory_space=pltpu.VMEM)] * 3,
        out_specs=[pl.BlockSpec(memory_space=pltpu.VMEM)] * places,
        out_shape=[jax.ShapeDtypeStruct((rows, cols), F32)] * places,
        compiler_params=params(),
        cost_estimate=cost(0.3),
        name="messages",
    )(keep, got, gram)


def core_sum_kernel(own, second, *refs):
    messages, total = refs[:-1], refs[-1]
    first = jnp.where(lax.axis_index("dp") == 0, own[...], second[...])
    parts = [first + messages[0][...]] + [message[...] for message in messages[1:]]
    while len(parts) > 1:
        parts = [a + b for a, b in zip(parts[::2], parts[1::2])]
    total[...] = parts[0]


def core_sum(own, first, second, across):
    operands = [own, first, second, *across]
    return pl.pallas_call(
        core_sum_kernel,
        in_specs=[pl.BlockSpec(memory_space=pltpu.VMEM)] * len(operands),
        out_specs=pl.BlockSpec(memory_space=pltpu.VMEM),
        out_shape=jax.ShapeDtypeStruct(own.shape, F32),
        compiler_params=params(),
        cost_estimate=cost(0.3),
        name="core_sum",
    )(*operands)


def chip_sum_kernel(here, other, share, gram):
    total = here[...] + other[...]
    rank, cols = share.shape
    blocks = cols // rank
    rows = rank // blocks
    share[...] = total[:rank]
    for block in range(blocks):
        gram[block * rows : (block + 1) * rows, :] = total[rank:, block * rank : (block + 1) * rank]


def chip_sum(here, other, rank):
    return pl.pallas_call(
        chip_sum_kernel,
        in_specs=[pl.BlockSpec(memory_space=pltpu.VMEM)] * 2,
        out_specs=[pl.BlockSpec(memory_space=pltpu.VMEM)] * 2,
        out_shape=[
            jax.ShapeDtypeStruct((rank, here.shape[1]), F32),
            jax.ShapeDtypeStruct((rank, rank), F32),
        ],
        compiler_params=params(),
        cost_estimate=cost(0.3),
        name="chip_sum",
    )(here, other)


def inverse_kernel(gram, inverse):
    rank = gram.shape[0]
    row = lax.broadcasted_iota(jnp.int32, (rank, 2 * rank), 0)
    lane = lax.broadcasted_iota(jnp.int32, (rank, 2 * rank), 1)
    eye = (lane[:, rank:] == row[:, rank:] + rank).astype(F32)
    table = jnp.concatenate([gram[...], eye], axis=1)
    scale = jnp.zeros((rank, 1), F32)
    for pivot in range(rank):
        line = table[pivot : pivot + 1, :]
        column = table[:, pivot : pivot + 1]
        top = line[:, pivot : pivot + 1]
        scale = jnp.where(row[:, :1] == pivot, lax.rsqrt(top), scale)
        if pivot + 1 < rank:
            factor = jnp.where(row[:, :1] > pivot, column / top, 0.0)
            table = table - factor * line
    inverse[...] = table[:, rank:] * scale


def cholesky_inverse(gram):
    return pl.pallas_call(
        inverse_kernel,
        in_specs=[pl.BlockSpec(memory_space=pltpu.VMEM)],
        out_specs=pl.BlockSpec(memory_space=pltpu.VMEM),
        out_shape=jax.ShapeDtypeStruct(gram.shape, F32),
        compiler_params=params(),
        cost_estimate=cost(5.0),
        name="cholesky_inverse",
    )(gram)


def spread(target, rows, start, value):
    rank = value.shape[1]
    high, low = split2(value)
    for place, term in enumerate((high, high, low, low)):
        target[rows, start + place * rank : start + (place + 1) * rank] = term


def operand_kernel(replicas, inverse, left_sum, hidden_t, lhs):
    rank = inverse.shape[0]
    rows, count = hidden_t.shape
    orth_t = jnp.dot(inverse[...], left_sum[...], precision=HIGHEST, preferred_element_type=F32)
    share = inverse[...] * (1.0 / replicas)
    weight_t = lax.dot_general(
        share, orth_t, (((0,), (0,)), ((), ())), precision=HIGHEST, preferred_element_type=F32
    )
    lhs[:rows, :count] = hidden_t[...]
    lhs[rows:, :count] = jnp.zeros((rank, count), BF16)
    spread(lhs, slice(0, rows), count, -weight_t.T)
    spread(lhs, slice(rows, rows + rank), count, share)


def last_operand(inverse, left_sum, hidden_t, replicas):
    rank = inverse.shape[0]
    rows, count = hidden_t.shape
    return pl.pallas_call(
        functools.partial(operand_kernel, replicas),
        in_specs=[pl.BlockSpec(memory_space=pltpu.VMEM)] * 3,
        out_specs=pl.BlockSpec(memory_space=pltpu.VMEM),
        out_shape=jax.ShapeDtypeStruct((rows + rank, count + 4 * rank), BF16),
        compiler_params=params(),
        cost_estimate=cost(1.5),
        name="last_operand",
    )(inverse, left_sum, hidden_t)


def final_kernel(mine, theirs, lhs, feedback, tokens, out, factor, rhs):
    step = pl.program_id(0)
    chip, core = lax.axis_index("tp"), lax.axis_index("dp")
    count = tokens.shape[0]
    rows = feedback.shape[0]
    rank, width = mine.shape[1:]
    rhs[:count, :] = tokens[...]
    for part in range(GROUP):
        place = (GROUP * step + part) ^ chip
        index = index_of(place)
        high, low = split2(jnp.where(core_of(place) == core, mine[index], theirs[index]))
        cols = slice(part * width, (part + 1) * width)
        for order, term in enumerate((high, low, high, low)):
            rhs[count + order * rank : count + (order + 1) * rank, cols] = term
    product = nn(lhs[...], rhs[...])
    factor[...] = product[rows:]
    out[...] = (product[:rows] + feedback[...].astype(F32)).astype(BF16)


def finish(mine, theirs, lhs, feedback, tokens):
    rank = mine.shape[1]
    count, width = tokens.shape
    rows = feedback.shape[0]
    cols = GROUP * mine.shape[2]
    return pl.pallas_call(
        final_kernel,
        grid=(width // cols,),
        in_specs=[
            whole(mine.shape),
            whole(mine.shape),
            whole(lhs.shape),
            pl.BlockSpec((rows, cols), lambda j: (0, j)),
            pl.BlockSpec((count, cols), lambda j: (0, j)),
        ],
        out_specs=[
            pl.BlockSpec((rows, cols), lambda j: (0, j)),
            pl.BlockSpec((rank, cols), lambda j: (0, j)),
        ],
        out_shape=[
            jax.ShapeDtypeStruct((rows, width), BF16),
            jax.ShapeDtypeStruct((rank, width), F32),
        ],
        scratch_shapes=[pltpu.VMEM((lhs.shape[1], cols), BF16)],
        compiler_params=params(("arbitrary",)),
        cost_estimate=cost(4.4),
        name="finish",
    )(mine, theirs, lhs, feedback, tokens)


def ring_order(chips):
    if chips == 8:
        return [0, 1, 3, 5, 7, 6, 4, 2]
    return list(range(chips))


def ring_gather(shard, chips, beside):
    order = ring_order(chips)
    position = {chip: place for place, chip in enumerate(order)}
    right = [(order[i], order[(i + 1) % chips]) for i in range(chips)]
    left = [(b, a) for a, b in right]
    size = shard.shape[0] // 2
    halves = [shard[:size], shard[size:]]
    pieces = list(halves)
    origin = [(0, 0), (0, 1)]
    going = {(way, half): halves[half] for way in (1, -1) for half in (0, 1)}
    far = chips // 2
    for hop in range(1, far + 1):
        for way, pairs in ((1, right), (-1, left)):
            for half in (0, 1):
                if hop == far and (half == 0) != (way == 1):
                    continue
                going[way, half] = lax.ppermute(going[way, half], "tp", pairs)
                if hop == 1 and (way, half) == (1, 0):
                    going[way, half], beside = lax.optimization_barrier((going[way, half], beside))
                pieces.append(going[way, half])
                origin.append((-way * hop, half))
    places = np.zeros((chips, len(pieces)), np.int32)
    for chip in range(chips):
        for index, (shift, half) in enumerate(origin):
            places[chip, index] = 2 * order[(position[chip] + shift) % chips] + half
    return pieces, places, beside


def swap(value):
    return lax.ppermute(value, "dp", [(0, 1), (1, 0)])


def local(grad_out, hidden, feedback, right_factor):
    shard, residue = grad_out[0], feedback[0]
    hidden_t = hidden[0].T
    chips, replicas = lax.axis_size("tp"), lax.axis_size("dp")
    rank = right_factor.shape[0]

    half = chips // 2

    def exchange(value, index, place=None):
        pairs = []
        for chip in range(chips):
            for core in range(2):
                to = (index >> 1) * 4 + core * 2 + (index & 1) if place is None else place
                if to:
                    pairs.append((2 * chip + core, 2 * (chip ^ to) + core))
        return lax.ppermute(value, ("tp", "dp"), pairs)

    pieces, places, (terms, residue_t) = ring_gather(shard, chips, residue_left(right_factor, residue))
    tokens, left_t = left_factor(places, pieces, terms, residue_t, hidden_t)
    keep, give, gram, left_sum = right_factor_terms(
        left_t, swap(left_t), hidden_t, residue, tokens, chips
    )

    messages = messages_for(keep, swap(give), gram)
    passed = [exchange(messages[index + 1], index + 1, 1) for index in range(2, half, 2)]
    beside = exchange(messages[1], 1), exchange(messages[0], 0)
    across = [exchange(messages[2 * i + 2] + value, 2 * i + 2) for i, value in enumerate(passed)]
    partial = core_sum(messages[0], beside[1], beside[0], across)
    share, gram_matrix = chip_sum(partial, swap(partial), rank)

    across = [exchange(share, index) for index in range(2, half, 2)]
    beside = exchange(share, 1), exchange(share, 0)
    inverse = cholesky_inverse(gram_matrix)
    across[0], inverse = lax.optimization_barrier((across[0], inverse))
    passed = [exchange(value, 2 * i + 3, 1) for i, value in enumerate(across)]
    lhs = last_operand(inverse, left_sum, hidden_t, replicas)
    first = jnp.where(lax.axis_index("dp") == 0, share, beside[1])
    mine = jnp.stack([first, beside[0]] + [value for pair in zip(across, passed) for value in pair])
    mine, lhs = lax.optimization_barrier((mine, lhs))
    new_feedback, new_factor = finish(mine, swap(mine), lhs, residue, tokens)
    return new_feedback[None], new_factor


def solution(mesh):
    return jax.shard_map(
        local,
        mesh=mesh,
        in_specs=(
            P(("runs", "dp"), "tp", None),
            P(("runs", "dp"), None, "tp"),
            P(("runs", "dp"), "tp", None),
            P(),
        ),
        out_specs=(P(("runs", "dp"), "tp", None), P("runs", None)),
        check_vma=False,
    )
```

```python
import functools

import jax
import jax.numpy as jnp
import numpy as np
from jax import lax
from jax.experimental import pallas as pl
from jax.experimental.pallas import tpu as pltpu
from jax.sharding import PartitionSpec as P

F32 = jnp.float32
BF16 = jnp.bfloat16
HIGHEST = lax.Precision.HIGHEST
VMEM_LIMIT = 32 * 1024 * 1024
STEPS = 4


def split3(value):
    high = value.astype(BF16)
    rest = value - high.astype(F32)
    middle = rest.astype(BF16)
    low = (rest - middle.astype(F32)).astype(BF16)
    return high, middle, low


def split2(value):
    high = value.astype(BF16)
    return high, (value - high.astype(F32)).astype(BF16)


def fold3(stacked):
    rank = stacked.shape[0] // 3
    return stacked[:rank] + stacked[rank : 2 * rank] + stacked[2 * rank :]


def nn(a, b):
    return lax.dot_general(a, b, (((1,), (0,)), ((), ())), preferred_element_type=F32)


def nt(a, b):
    return lax.dot_general(a, b, (((1,), (1,)), ((), ())), preferred_element_type=F32)


def params(semantics=None, limit=VMEM_LIMIT):
    return pltpu.CompilerParams(vmem_limit_bytes=limit, dimension_semantics=semantics)


def cost(microseconds):
    return pl.CostEstimate(flops=int(microseconds * 1.15e9), bytes_accessed=0, transcendentals=0)


def whole(shape):
    return pl.BlockSpec(shape, lambda *_: (0,) * len(shape))


def halves_kernel(shard, first, second):
    size = first.shape[0]
    first[...] = shard[:size, :]
    second[...] = shard[size:, :]


def halves_of(shard):
    half = jax.ShapeDtypeStruct((shard.shape[0] // 2, shard.shape[1]), BF16)
    return pl.pallas_call(
        halves_kernel,
        in_specs=[pl.BlockSpec(memory_space=pltpu.VMEM)],
        out_specs=[pl.BlockSpec(memory_space=pltpu.VMEM)] * 2,
        out_shape=[half, half],
        compiler_params=params(),
        cost_estimate=cost(4.0),
        name="halves",
    )(shard)


def residue_kernel(right, feedback, terms, left_t):
    cols = right.shape[1] // STEPS
    total = None
    for step in range(STEPS):
        span = slice(step * cols, (step + 1) * cols)
        stacked = jnp.concatenate(split3(right[:, span]), axis=0)
        terms[:, span] = stacked
        part = nt(stacked, feedback[:, span])
        total = part if total is None else total + part
    left_t[...] = fold3(total)


def residue_left(right, feedback):
    rank, width = right.shape
    rows = feedback.shape[0]
    return pl.pallas_call(
        residue_kernel,
        in_specs=[pl.BlockSpec(memory_space=pltpu.VMEM)] * 2,
        out_specs=[pl.BlockSpec(memory_space=pltpu.VMEM)] * 2,
        out_shape=[
            jax.ShapeDtypeStruct((3 * rank, width), BF16),
            jax.ShapeDtypeStruct((rank, rows), F32),
        ],
        compiler_params=params(),
        cost_estimate=cost(2.2),
        name="residue_left",
    )(right, feedback)


def early_kernel(places, *refs):
    pieces, (terms, residue_t, hidden_t, tokens, hidden, left_t) = refs[:-6], refs[-6:]
    here = lax.axis_index("tp")
    size = pieces[0].shape[0]
    for index in range(len(pieces) + 2):
        rows = pl.ds(pl.multiple_of(places[here, index] * size, size), size)
        if index < len(pieces):
            tokens[rows, :] = pieces[index][...]
        else:
            tokens[rows, :] = jnp.zeros((size, tokens.shape[1]), BF16)
    projected = fold3(nt(terms[...], tokens[...]))
    stacked = jnp.concatenate(split3(projected), axis=0)
    left_t[...] = residue_t[...] + fold3(nt(stacked, hidden_t[...]))
    hidden[...] = hidden_t[...].T


def early_left(places, pieces, terms, residue_t, hidden_t):
    rows, count = hidden_t.shape
    width = terms.shape[1]
    operands = [*pieces, terms, residue_t, hidden_t]
    return pl.pallas_call(
        early_kernel,
        in_specs=[pl.BlockSpec(memory_space=pltpu.SMEM)]
        + [pl.BlockSpec(memory_space=pltpu.VMEM)] * len(operands),
        out_specs=[pl.BlockSpec(memory_space=pltpu.VMEM)] * 3,
        out_shape=[
            jax.ShapeDtypeStruct((count, width), BF16),
            jax.ShapeDtypeStruct((count, rows), BF16),
            jax.ShapeDtypeStruct(residue_t.shape, F32),
        ],
        compiler_params=params(),
        cost_estimate=cost(2.0),
        name="early_left",
    )(places, *operands)


def late_kernel(places, first, second, terms, hidden, early_t, _, tokens, left_t):
    here = lax.axis_index("tp")
    size = first.shape[0]
    count = places.shape[1]
    seen = []
    for index, piece in enumerate((first, second)):
        rows = pl.ds(pl.multiple_of(places[here, count - 2 + index] * size, size), size)
        tokens[rows, :] = piece[...]
        seen.append(hidden[rows, :])
    projected = fold3(nt(terms[...], jnp.concatenate([first[...], second[...]], axis=0)))
    stacked = jnp.concatenate(split3(projected), axis=0)
    left_t[...] = early_t[...] + fold3(nn(stacked, jnp.concatenate(seen, axis=0)))


def late_left(places, pieces, terms, hidden, early_t, tokens):
    operands = [*pieces, terms, hidden, early_t, tokens]
    return pl.pallas_call(
        late_kernel,
        in_specs=[pl.BlockSpec(memory_space=pltpu.SMEM)]
        + [pl.BlockSpec(memory_space=pltpu.VMEM)] * len(operands),
        out_specs=[pl.BlockSpec(memory_space=pltpu.VMEM)] * 2,
        out_shape=[
            jax.ShapeDtypeStruct(tokens.shape, BF16),
            jax.ShapeDtypeStruct(early_t.shape, F32),
        ],
        input_output_aliases={len(operands): 0},
        compiler_params=params(),
        cost_estimate=cost(1.0),
        name="late_left",
    )(places, *operands)


def core_of(place):
    return (place >> 1) & 1


def index_of(place):
    return (place >> 2) * 2 + (place & 1)


def place_of(core, index):
    return (index >> 1) * 4 + core * 2 + (index & 1)


def columns_of(place, cols):
    shard = lax.axis_index("tp") ^ place
    return pl.ds(pl.multiple_of(shard * cols, cols), cols)


def give_kernel(here_l, other_l, hidden_t, feedback, tokens, give, left_sum, lhs, rhs):
    left_t = here_l[...] + other_l[...]
    left_sum[...] = left_t
    lhs[...] = jnp.concatenate(split3(left_t), axis=0)
    seen_t = fold3(nn(lhs[...], hidden_t[...]))
    rhs[...] = jnp.concatenate(split3(seen_t), axis=0)
    other = 1 - lax.axis_index("dp")
    for index in range(give.shape[0]):
        span = columns_of(place_of(other, index), give.shape[2])
        give[index] = fold3(nn(lhs[...], feedback[:, span]) + nn(rhs[...], tokens[:, span]))


def given_terms(here_l, other_l, hidden_t, feedback, tokens, chips):
    rank, rows = here_l.shape
    count, width = tokens.shape
    return pl.pallas_call(
        give_kernel,
        in_specs=[pl.BlockSpec(memory_space=pltpu.VMEM)] * 5,
        out_specs=[pl.BlockSpec(memory_space=pltpu.VMEM)] * 4,
        out_shape=[
            jax.ShapeDtypeStruct((chips // 2, rank, width // chips), F32),
            jax.ShapeDtypeStruct((rank, rows), F32),
            jax.ShapeDtypeStruct((3 * rank, rows), BF16),
            jax.ShapeDtypeStruct((3 * rank, count), BF16),
        ],
        compiler_params=params(),
        cost_estimate=cost(1.8),
        name="given_terms",
    )(here_l, other_l, hidden_t, feedback, tokens)


def keep_kernel(left_sum, lhs, rhs, feedback, tokens, keep, gram):
    core = lax.axis_index("dp")
    for index in range(keep.shape[0]):
        span = columns_of(place_of(core, index), keep.shape[2])
        keep[index] = fold3(nn(lhs[...], feedback[:, span]) + nn(rhs[...], tokens[:, span]))
    left_t = left_sum[...]
    gram[...] = lax.dot_general(
        left_t, left_t, (((1,), (1,)), ((), ())), precision=HIGHEST, preferred_element_type=F32
    )


def kept_terms(left_sum, lhs, rhs, feedback, tokens, chips):
    rank = left_sum.shape[0]
    return pl.pallas_call(
        keep_kernel,
        in_specs=[pl.BlockSpec(memory_space=pltpu.VMEM)] * 5,
        out_specs=[pl.BlockSpec(memory_space=pltpu.VMEM)] * 2,
        out_shape=[
            jax.ShapeDtypeStruct((chips // 2, rank, tokens.shape[1] // chips), F32),
            jax.ShapeDtypeStruct((rank, rank), F32),
        ],
        compiler_params=params(),
        cost_estimate=cost(1.8),
        name="kept_terms",
    )(left_sum, lhs, rhs, feedback, tokens)


def merged_kernel(hidden_t, feedback, tokens, merged):
    cols = tokens.shape[1] // STEPS
    for step in range(STEPS):
        span = slice(step * cols, (step + 1) * cols)
        merged[:, span] = nn(hidden_t[...], tokens[:, span]) + feedback[:, span].astype(F32)


def merged_sum(hidden_t, feedback, tokens):
    return pl.pallas_call(
        merged_kernel,
        in_specs=[pl.BlockSpec(memory_space=pltpu.VMEM)] * 3,
        out_specs=pl.BlockSpec(memory_space=pltpu.VMEM),
        out_shape=jax.ShapeDtypeStruct(feedback.shape, F32),
        compiler_params=params(),
        cost_estimate=cost(2.0),
        name="merged",
    )(hidden_t, feedback, tokens)


def message_kernel(keep, got, gram, *messages):
    rank, cols = keep.shape[1:]
    blocks = cols // rank
    rows = rank // blocks
    for index, message in enumerate(messages):
        message[:rank, :] = keep[index] + got[index]
        for block in range(blocks):
            message[rank:, block * rank : (block + 1) * rank] = gram[block * rows : (block + 1) * rows, :]


def messages_for(keep, got, gram):
    places, rank, cols = keep.shape
    rows = rank + rank // (cols // rank)
    return pl.pallas_call(
        message_kernel,
        in_specs=[pl.BlockSpec(memory_space=pltpu.VMEM)] * 3,
        out_specs=[pl.BlockSpec(memory_space=pltpu.VMEM)] * places,
        out_shape=[jax.ShapeDtypeStruct((rows, cols), F32)] * places,
        compiler_params=params(),
        cost_estimate=cost(0.3),
        name="messages",
    )(keep, got, gram)


def core_sum_kernel(own, second, *refs):
    messages, total = refs[:-1], refs[-1]
    first = jnp.where(lax.axis_index("dp") == 0, own[...], second[...])
    parts = [first + messages[0][...]] + [message[...] for message in messages[1:]]
    while len(parts) > 1:
        parts = [a + b for a, b in zip(parts[::2], parts[1::2])]
    total[...] = parts[0]


def core_sum(own, first, second, across):
    operands = [own, first, second, *across]
    return pl.pallas_call(
        core_sum_kernel,
        in_specs=[pl.BlockSpec(memory_space=pltpu.VMEM)] * len(operands),
        out_specs=pl.BlockSpec(memory_space=pltpu.VMEM),
        out_shape=jax.ShapeDtypeStruct(own.shape, F32),
        compiler_params=params(),
        cost_estimate=cost(0.3),
        name="core_sum",
    )(*operands)


def chip_sum_kernel(here, other, share, gram):
    total = here[...] + other[...]
    rank, cols = share.shape
    blocks = cols // rank
    rows = rank // blocks
    share[...] = total[:rank]
    for block in range(blocks):
        gram[block * rows : (block + 1) * rows, :] = total[rank:, block * rank : (block + 1) * rank]


def chip_sum(here, other, rank):
    return pl.pallas_call(
        chip_sum_kernel,
        in_specs=[pl.BlockSpec(memory_space=pltpu.VMEM)] * 2,
        out_specs=[pl.BlockSpec(memory_space=pltpu.VMEM)] * 2,
        out_shape=[
            jax.ShapeDtypeStruct((rank, here.shape[1]), F32),
            jax.ShapeDtypeStruct((rank, rank), F32),
        ],
        compiler_params=params(),
        cost_estimate=cost(0.3),
        name="chip_sum",
    )(here, other)


def inverse_kernel(gram, inverse):
    rank = gram.shape[0]
    row = lax.broadcasted_iota(jnp.int32, (rank, 2 * rank), 0)
    lane = lax.broadcasted_iota(jnp.int32, (rank, 2 * rank), 1)
    eye = (lane[:, rank:] == row[:, rank:] + rank).astype(F32)
    table = jnp.concatenate([gram[...], eye], axis=1)
    scale = jnp.zeros((rank, 1), F32)
    for pivot in range(rank):
        line = table[pivot : pivot + 1, :]
        column = table[:, pivot : pivot + 1]
        top = line[:, pivot : pivot + 1]
        scale = jnp.where(row[:, :1] == pivot, lax.rsqrt(top), scale)
        if pivot + 1 < rank:
            factor = jnp.where(row[:, :1] > pivot, column / top, 0.0)
            table = table - factor * line
    inverse[...] = table[:, rank:] * scale


def cholesky_inverse(gram):
    return pl.pallas_call(
        inverse_kernel,
        in_specs=[pl.BlockSpec(memory_space=pltpu.VMEM)],
        out_specs=pl.BlockSpec(memory_space=pltpu.VMEM),
        out_shape=jax.ShapeDtypeStruct(gram.shape, F32),
        compiler_params=params(),
        cost_estimate=cost(5.0),
        name="cholesky_inverse",
    )(gram)


def spread(target, rows, value):
    rank = value.shape[1]
    high, low = split2(value)
    for place, term in enumerate((high, high, low, low)):
        target[rows, place * rank : (place + 1) * rank] = term


def operand_kernel(replicas, inverse, left_sum, lhs):
    rank, rows = left_sum.shape
    orth_t = jnp.dot(inverse[...], left_sum[...], precision=HIGHEST, preferred_element_type=F32)
    share = inverse[...] * (1.0 / replicas)
    weight_t = lax.dot_general(
        share, orth_t, (((0,), (0,)), ((), ())), precision=HIGHEST, preferred_element_type=F32
    )
    spread(lhs, slice(0, rows), -weight_t.T)
    spread(lhs, slice(rows, rows + rank), share)


def last_operand(inverse, left_sum, replicas):
    rank, rows = left_sum.shape
    return pl.pallas_call(
        functools.partial(operand_kernel, replicas),
        in_specs=[pl.BlockSpec(memory_space=pltpu.VMEM)] * 2,
        out_specs=pl.BlockSpec(memory_space=pltpu.VMEM),
        out_shape=jax.ShapeDtypeStruct((rows + rank, 4 * rank), BF16),
        compiler_params=params(),
        cost_estimate=cost(1.5),
        name="last_operand",
    )(inverse, left_sum)


def final_kernel(mine, theirs, lhs, merged, out, factor, rhs, out_here, factor_here, sems):
    chip, core = lax.axis_index("tp"), lax.axis_index("dp")
    rows = merged.shape[0]
    rank, cols = mine.shape[1:]
    group = 2 * mine.shape[0] // STEPS
    copies = []
    for step in range(STEPS):
        for part in range(group):
            place = (group * step + part) ^ chip
            index = index_of(place)
            high, low = split2(jnp.where(core_of(place) == core, mine[index], theirs[index]))
            span = slice(part * cols, (part + 1) * cols)
            for order, term in enumerate((high, low, high, low)):
                rhs[step % 2, order * rank : (order + 1) * rank, span] = term
        span = slice(step * group * cols, (step + 1) * group * cols)
        product = nn(lhs[...], rhs[step % 2])
        factor_here[:, span] = product[rows:]
        out_here[:, span] = (merged[:, span] + product[:rows]).astype(BF16)
        for index, (source, target) in enumerate(((out_here, out), (factor_here, factor))):
            copies.append(pltpu.make_async_copy(source.at[:, span], target.at[:, span], sems.at[step, index]))
            copies[-1].start()
    for copy in copies:
        copy.wait()


def finish(mine, theirs, lhs, merged):
    rank = mine.shape[1]
    rows, width = merged.shape
    return pl.pallas_call(
        final_kernel,
        in_specs=[pl.BlockSpec(memory_space=pltpu.VMEM)] * 4,
        out_specs=[pl.BlockSpec(memory_space=pl.ANY)] * 2,
        out_shape=[
            jax.ShapeDtypeStruct((rows, width), BF16),
            jax.ShapeDtypeStruct((rank, width), F32),
        ],
        scratch_shapes=[
            pltpu.VMEM((2, lhs.shape[1], width // STEPS), BF16),
            pltpu.VMEM((rows, width), BF16),
            pltpu.VMEM((rank, width), F32),
            pltpu.SemaphoreType.DMA((STEPS, 2)),
        ],
        compiler_params=params(),
        cost_estimate=cost(3.0),
        name="finish",
    )(mine, theirs, lhs, merged)


def ring_order(chips):
    if chips == 8:
        return [0, 1, 3, 5, 7, 6, 4, 2]
    return list(range(chips))


def ring_gather(shard, chips, beside):
    order = ring_order(chips)
    position = {chip: place for place, chip in enumerate(order)}
    right = [(order[i], order[(i + 1) % chips]) for i in range(chips)]
    left = [(b, a) for a, b in right]
    halves = halves_of(shard)
    pieces = list(halves)
    origin = [(0, 0), (0, 1)]
    going = {(way, half): halves[half] for way in (1, -1) for half in (0, 1)}
    far = chips // 2
    for hop in range(1, far + 1):
        for way, pairs in ((1, right), (-1, left)):
            for half in (0, 1):
                if hop == far and (half == 0) != (way == 1):
                    continue
                going[way, half] = lax.ppermute(going[way, half], "tp", pairs)
                if hop == 1 and (way, half) == (-1, 0):
                    going[way, half], beside = lax.optimization_barrier((going[way, half], beside))
                pieces.append(going[way, half])
                origin.append((-way * hop, half))
    places = np.zeros((chips, len(pieces)), np.int32)
    for chip in range(chips):
        for index, (shift, half) in enumerate(origin):
            places[chip, index] = 2 * order[(position[chip] + shift) % chips] + half
    return pieces, places, beside


def swap(value):
    return lax.ppermute(value, "dp", [(0, 1), (1, 0)])


def local(grad_out, hidden, feedback, right_factor):
    shard, residue = grad_out[0], feedback[0]
    hidden_t = hidden[0].T
    chips, replicas = lax.axis_size("tp"), lax.axis_size("dp")
    rank = right_factor.shape[0]

    half = chips // 2

    def exchange(value, index, place=None):
        pairs = []
        for chip in range(chips):
            for core in range(2):
                to = (index >> 1) * 4 + core * 2 + (index & 1) if place is None else place
                if to:
                    pairs.append((2 * chip + core, 2 * (chip ^ to) + core))
        return lax.ppermute(value, ("tp", "dp"), pairs)

    pieces, places, (terms, residue_t) = ring_gather(shard, chips, residue_left(right_factor, residue))
    places = jnp.asarray(places)
    tokens, hidden_rows, left_t = early_left(places, pieces[:-2], terms, residue_t, hidden_t)
    tokens, left_t = late_left(places, pieces[-2:], terms, hidden_rows, left_t, tokens)
    give, left_sum, lhs, rhs = given_terms(left_t, swap(left_t), hidden_t, residue, tokens, chips)
    got = swap(give)
    keep, gram = kept_terms(left_sum, lhs, rhs, residue, tokens, chips)

    messages = messages_for(keep, got, gram)
    passed = [exchange(messages[index + 1], index + 1, 1) for index in range(2, half, 2)]
    across = [messages[2 * i + 2] + value for i, value in enumerate(passed)]
    across = [exchange(value, 2 * i + 2) for i, value in enumerate(across)]
    merged = merged_sum(hidden_t, residue, tokens)
    own, beside, passed, merged = lax.optimization_barrier((messages[0], messages[1], passed, merged))
    beside = exchange(beside, 1), exchange(own, 0)
    partial = core_sum(own, beside[1], beside[0], across)
    share, gram_matrix = chip_sum(partial, swap(partial), rank)

    across = [exchange(share, index) for index in range(2, half, 2)]
    beside = exchange(share, 1), exchange(share, 0)
    inverse = cholesky_inverse(gram_matrix)
    across[0], inverse = lax.optimization_barrier((across[0], inverse))
    passed = [exchange(value, 2 * i + 3, 1) for i, value in enumerate(across)]
    lhs = last_operand(inverse, left_sum, replicas)
    first = jnp.where(lax.axis_index("dp") == 0, share, beside[1])
    mine = jnp.stack([first, beside[0]] + [value for pair in zip(across, passed) for value in pair])
    mine, lhs = lax.optimization_barrier((mine, lhs))
    new_feedback, new_factor = finish(mine, swap(mine), lhs, merged)
    return new_feedback[None], new_factor


def solution(mesh):
    return jax.shard_map(
        local,
        mesh=mesh,
        in_specs=(
            P(("runs", "dp"), "tp", None),
            P(("runs", "dp"), None, "tp"),
            P(("runs", "dp"), "tp", None),
            P(),
        ),
        out_specs=(P(("runs", "dp"), "tp", None), P("runs", None)),
        check_vma=False,
    )
```

```python
import functools

import jax
import jax.numpy as jnp
import numpy as np
from jax import lax
from jax.experimental import pallas as pl
from jax.experimental.pallas import tpu as pltpu
from jax.sharding import PartitionSpec as P

F32 = jnp.float32
BF16 = jnp.bfloat16
HIGHEST = lax.Precision.HIGHEST
VMEM_LIMIT = 24 * 1024 * 1024
STEPS = 4
SMALL = 0.05
PIVOTS = 8


def split3(value):
    high = value.astype(BF16)
    rest = value - high.astype(F32)
    middle = rest.astype(BF16)
    low = (rest - middle.astype(F32)).astype(BF16)
    return high, middle, low


def split2(value):
    high = value.astype(BF16)
    return high, (value - high.astype(F32)).astype(BF16)


def fold3(stacked):
    rank = stacked.shape[0] // 3
    return stacked[:rank] + stacked[rank : 2 * rank] + stacked[2 * rank :]


def nn(a, b):
    return lax.dot_general(a, b, (((1,), (0,)), ((), ())), preferred_element_type=F32)


def nt(a, b):
    return lax.dot_general(a, b, (((1,), (1,)), ((), ())), preferred_element_type=F32)


def params(semantics=None, limit=VMEM_LIMIT):
    return pltpu.CompilerParams(vmem_limit_bytes=limit, dimension_semantics=semantics)


def cost(microseconds):
    return pl.CostEstimate(flops=int(microseconds * 1.15e9), bytes_accessed=0, transcendentals=0)


def whole(shape):
    return pl.BlockSpec(shape, lambda *_: (0,) * len(shape))


def halves_kernel(shard, first, second):
    size = first.shape[0]
    first[...] = shard[:size, :]
    second[...] = shard[size:, :]


def halves_of(shard):
    half = jax.ShapeDtypeStruct((shard.shape[0] // 2, shard.shape[1]), BF16)
    return pl.pallas_call(
        halves_kernel,
        in_specs=[pl.BlockSpec(memory_space=pltpu.VMEM)],
        out_specs=[pl.BlockSpec(memory_space=pltpu.VMEM)] * 2,
        out_shape=[half, half],
        compiler_params=params(),
        cost_estimate=cost(4.0),
        name="halves",
    )(shard)


def residue_kernel(right, feedback, terms, left_t):
    cols = right.shape[1] // STEPS
    total = None
    for step in range(STEPS):
        span = slice(step * cols, (step + 1) * cols)
        stacked = jnp.concatenate(split3(right[:, span]), axis=0)
        terms[:, span] = stacked
        part = nt(stacked, feedback[:, span])
        total = part if total is None else total + part
    left_t[...] = fold3(total)


def residue_left(right, feedback):
    rank, width = right.shape
    rows = feedback.shape[0]
    return pl.pallas_call(
        residue_kernel,
        in_specs=[pl.BlockSpec(memory_space=pltpu.VMEM)] * 2,
        out_specs=[pl.BlockSpec(memory_space=pltpu.VMEM)] * 2,
        out_shape=[
            jax.ShapeDtypeStruct((3 * rank, width), BF16),
            jax.ShapeDtypeStruct((rank, rows), F32),
        ],
        compiler_params=params(),
        cost_estimate=cost(2.2),
        name="residue_left",
    )(right, feedback)


def early_kernel(places, *refs):
    pieces, (terms, residue_t, hidden_t, tokens, hidden, left_t) = refs[:-6], refs[-6:]
    here = lax.axis_index("tp")
    size = pieces[0].shape[0]
    for index in range(len(pieces) + 2):
        rows = pl.ds(pl.multiple_of(places[here, index] * size, size), size)
        if index < len(pieces):
            tokens[rows, :] = pieces[index][...]
        else:
            tokens[rows, :] = jnp.zeros((size, tokens.shape[1]), BF16)
    projected = fold3(nt(terms[...], tokens[...]))
    stacked = jnp.concatenate(split3(projected), axis=0)
    left_t[...] = residue_t[...] + fold3(nt(stacked, hidden_t[...]))
    hidden[...] = hidden_t[...].T


def early_left(places, pieces, terms, residue_t, hidden_t):
    rows, count = hidden_t.shape
    width = terms.shape[1]
    operands = [*pieces, terms, residue_t, hidden_t]
    return pl.pallas_call(
        early_kernel,
        in_specs=[pl.BlockSpec(memory_space=pltpu.SMEM)]
        + [pl.BlockSpec(memory_space=pltpu.VMEM)] * len(operands),
        out_specs=[pl.BlockSpec(memory_space=pltpu.VMEM)] * 3,
        out_shape=[
            jax.ShapeDtypeStruct((count, width), BF16),
            jax.ShapeDtypeStruct((count, rows), BF16),
            jax.ShapeDtypeStruct(residue_t.shape, F32),
        ],
        compiler_params=params(),
        cost_estimate=cost(2.0),
        name="early_left",
    )(places, *operands)


def late_kernel(places, first, second, terms, hidden, early_t, _, tokens, left_t):
    here = lax.axis_index("tp")
    size = first.shape[0]
    count = places.shape[1]
    seen = []
    for index, piece in enumerate((first, second)):
        rows = pl.ds(pl.multiple_of(places[here, count - 2 + index] * size, size), size)
        tokens[rows, :] = piece[...]
        seen.append(hidden[rows, :])
    projected = fold3(nt(terms[...], jnp.concatenate([first[...], second[...]], axis=0)))
    stacked = jnp.concatenate(split3(projected), axis=0)
    left_t[...] = early_t[...] + fold3(nn(stacked, jnp.concatenate(seen, axis=0)))


def late_left(places, pieces, terms, hidden, early_t, tokens):
    operands = [*pieces, terms, hidden, early_t, tokens]
    return pl.pallas_call(
        late_kernel,
        in_specs=[pl.BlockSpec(memory_space=pltpu.SMEM)]
        + [pl.BlockSpec(memory_space=pltpu.VMEM)] * len(operands),
        out_specs=[pl.BlockSpec(memory_space=pltpu.VMEM)] * 2,
        out_shape=[
            jax.ShapeDtypeStruct(tokens.shape, BF16),
            jax.ShapeDtypeStruct(early_t.shape, F32),
        ],
        input_output_aliases={len(operands): 0},
        compiler_params=params(),
        cost_estimate=cost(1.0),
        name="late_left",
    )(places, *operands)


def core_of(place):
    return (place >> 1) & 1


def index_of(place):
    return (place >> 2) * 2 + (place & 1)


def place_of(core, index):
    return (index >> 1) * 4 + core * 2 + (index & 1)


def columns_of(place, cols):
    shard = lax.axis_index("tp") ^ place
    return pl.ds(pl.multiple_of(shard * cols, cols), cols)


def block_sum(lhs, rhs, feedback, tokens, core, index, cols):
    span = columns_of(place_of(core, index), cols)
    return fold3(nn(lhs[...], feedback[:, span]) + nn(rhs[...], tokens[:, span]))


def give_far_kernel(here_l, other_l, hidden_t, feedback, tokens, give, left_sum, lhs, rhs):
    left_t = here_l[...] + other_l[...]
    left_sum[...] = left_t
    lhs[...] = jnp.concatenate(split3(left_t), axis=0)
    seen_t = fold3(nn(lhs[...], hidden_t[...]))
    rhs[...] = jnp.concatenate(split3(seen_t), axis=0)
    other = 1 - lax.axis_index("dp")
    for index in range(give.shape[0]):
        give[index] = block_sum(lhs, rhs, feedback, tokens, other, index + 2, give.shape[2])


def given_far(here_l, other_l, hidden_t, feedback, tokens, chips):
    rank, rows = here_l.shape
    count, width = tokens.shape
    return pl.pallas_call(
        give_far_kernel,
        in_specs=[pl.BlockSpec(memory_space=pltpu.VMEM)] * 5,
        out_specs=[pl.BlockSpec(memory_space=pltpu.VMEM)] * 4,
        out_shape=[
            jax.ShapeDtypeStruct((chips // 2 - 2, rank, width // chips), F32),
            jax.ShapeDtypeStruct((rank, rows), F32),
            jax.ShapeDtypeStruct((3 * rank, rows), BF16),
            jax.ShapeDtypeStruct((3 * rank, count), BF16),
        ],
        compiler_params=params(),
        cost_estimate=cost(SMALL),
        name="given_far",
    )(here_l, other_l, hidden_t, feedback, tokens)


def keep_far_kernel(left_sum, lhs, rhs, feedback, tokens, keep, gram):
    core = lax.axis_index("dp")
    for index in range(keep.shape[0]):
        keep[index] = block_sum(lhs, rhs, feedback, tokens, core, index + 2, keep.shape[2])
    left_t = left_sum[...]
    gram[...] = lax.dot_general(
        left_t, left_t, (((1,), (1,)), ((), ())), precision=HIGHEST, preferred_element_type=F32
    )


def kept_far(left_sum, lhs, rhs, feedback, tokens, chips):
    rank = left_sum.shape[0]
    return pl.pallas_call(
        keep_far_kernel,
        in_specs=[pl.BlockSpec(memory_space=pltpu.VMEM)] * 5,
        out_specs=[pl.BlockSpec(memory_space=pltpu.VMEM)] * 2,
        out_shape=[
            jax.ShapeDtypeStruct((chips // 2 - 2, rank, tokens.shape[1] // chips), F32),
            jax.ShapeDtypeStruct((rank, rank), F32),
        ],
        compiler_params=params(),
        cost_estimate=cost(SMALL),
        name="kept_far",
    )(left_sum, lhs, rhs, feedback, tokens)


def near_kernel(lhs, rhs, feedback, tokens, give, keep):
    core = lax.axis_index("dp")
    for target, owner in ((give, 1 - core), (keep, core)):
        for index in range(2):
            target[index] = block_sum(lhs, rhs, feedback, tokens, owner, index, target.shape[2])


def near_terms(lhs, rhs, feedback, tokens, chips):
    block = jax.ShapeDtypeStruct((2, lhs.shape[0] // 3, tokens.shape[1] // chips), F32)
    return pl.pallas_call(
        near_kernel,
        in_specs=[pl.BlockSpec(memory_space=pltpu.VMEM)] * 4,
        out_specs=[pl.BlockSpec(memory_space=pltpu.VMEM)] * 2,
        out_shape=[block, block],
        compiler_params=params(),
        cost_estimate=cost(SMALL),
        name="near_terms",
    )(lhs, rhs, feedback, tokens)


def merged_kernel(hidden_t, feedback, tokens, merged):
    cols = tokens.shape[1] // STEPS
    for step in range(STEPS):
        span = slice(step * cols, (step + 1) * cols)
        merged[:, span] = nn(hidden_t[...], tokens[:, span]) + feedback[:, span].astype(F32)


def merged_sum(hidden_t, feedback, tokens):
    return pl.pallas_call(
        merged_kernel,
        in_specs=[pl.BlockSpec(memory_space=pltpu.VMEM)] * 3,
        out_specs=pl.BlockSpec(memory_space=pltpu.VMEM),
        out_shape=jax.ShapeDtypeStruct(feedback.shape, F32),
        compiler_params=params(),
        cost_estimate=cost(SMALL),
        name="merged",
    )(hidden_t, feedback, tokens)


def message_kernel(keep, got, gram, *messages):
    rank, cols = keep.shape[1:]
    blocks = cols // rank
    rows = rank // blocks
    for index, message in enumerate(messages):
        message[:rank, :] = keep[index] + got[index]
        for block in range(blocks):
            message[rank:, block * rank : (block + 1) * rank] = gram[block * rows : (block + 1) * rows, :]


def messages_for(keep, got, gram):
    places, rank, cols = keep.shape
    rows = rank + rank // (cols // rank)
    return pl.pallas_call(
        message_kernel,
        in_specs=[pl.BlockSpec(memory_space=pltpu.VMEM)] * 3,
        out_specs=[pl.BlockSpec(memory_space=pltpu.VMEM)] * places,
        out_shape=[jax.ShapeDtypeStruct((rows, cols), F32)] * places,
        compiler_params=params(),
        cost_estimate=cost(SMALL),
        name="messages",
    )(keep, got, gram)


def add_kernel(a, b, total):
    total[...] = a[...] + b[...]


def added(a, b):
    return pl.pallas_call(
        add_kernel,
        in_specs=[pl.BlockSpec(memory_space=pltpu.VMEM)] * 2,
        out_specs=pl.BlockSpec(memory_space=pltpu.VMEM),
        out_shape=jax.ShapeDtypeStruct(a.shape, a.dtype),
        compiler_params=params(),
        cost_estimate=cost(SMALL),
        name="added",
    )(a, b)


def join_kernel(share, second, first, *refs):
    across, mine = refs[:-1], refs[-1]
    mine[0] = jnp.where(lax.axis_index("dp") == 0, share[...], second[...])
    mine[1] = first[...]
    for index, value in enumerate(across):
        mine[index + 2] = value[...]


def joined(share, second, first, across):
    operands = [share, second, first, *across]
    return pl.pallas_call(
        join_kernel,
        in_specs=[pl.BlockSpec(memory_space=pltpu.VMEM)] * len(operands),
        out_specs=pl.BlockSpec(memory_space=pltpu.VMEM),
        out_shape=jax.ShapeDtypeStruct((len(operands) - 1, *share.shape), F32),
        compiler_params=params(),
        cost_estimate=cost(SMALL),
        name="joined",
    )(*operands)


def core_sum_kernel(own, second, *refs):
    messages, total = refs[:-1], refs[-1]
    first = jnp.where(lax.axis_index("dp") == 0, own[...], second[...])
    parts = [first + messages[0][...]] + [message[...] for message in messages[1:]]
    while len(parts) > 1:
        parts = [a + b for a, b in zip(parts[::2], parts[1::2])]
    total[...] = parts[0]


def core_sum(own, first, second, across):
    operands = [own, first, second, *across]
    return pl.pallas_call(
        core_sum_kernel,
        in_specs=[pl.BlockSpec(memory_space=pltpu.VMEM)] * len(operands),
        out_specs=pl.BlockSpec(memory_space=pltpu.VMEM),
        out_shape=jax.ShapeDtypeStruct(own.shape, F32),
        compiler_params=params(),
        cost_estimate=cost(SMALL),
        name="core_sum",
    )(*operands)


def chip_sum_kernel(here, other, share, gram):
    total = here[...] + other[...]
    rank, cols = share.shape
    blocks = cols // rank
    rows = rank // blocks
    share[...] = total[:rank]
    for block in range(blocks):
        gram[block * rows : (block + 1) * rows, :] = total[rank:, block * rank : (block + 1) * rank]


def chip_sum(here, other, rank):
    return pl.pallas_call(
        chip_sum_kernel,
        in_specs=[pl.BlockSpec(memory_space=pltpu.VMEM)] * 2,
        out_specs=[pl.BlockSpec(memory_space=pltpu.VMEM)] * 2,
        out_shape=[
            jax.ShapeDtypeStruct((rank, here.shape[1]), F32),
            jax.ShapeDtypeStruct((rank, rank), F32),
        ],
        compiler_params=params(),
        cost_estimate=cost(SMALL),
        name="chip_sum",
    )(here, other)


def inverse_kernel(gram, inverse):
    rank = gram.shape[0]
    row = lax.broadcasted_iota(jnp.int32, (rank, 2 * rank), 0)
    lane = lax.broadcasted_iota(jnp.int32, (rank, 2 * rank), 1)
    eye = (lane[:, rank:] == row[:, rank:] + rank).astype(F32)
    table = jnp.concatenate([gram[...], eye], axis=1)
    done = []
    for start in range(0, rank, PIVOTS):
        below = row[start:]
        each = range(PIVOTS)
        lines = [table[k : k + 1, :] for k in each]
        columns = [jnp.broadcast_to(table[:, start + k : start + k + 1], table.shape) for k in each]
        change = None
        for k in each:
            top = columns[k][k : k + 1, :]
            reciprocal = 1.0 / top
            factor = jnp.where(below > start + k, columns[k] * reciprocal, 0.0)
            for m in range(k + 1, PIVOTS):
                entry = columns[m][k : k + 1, :]
                lines[m] = lines[m] - (entry * reciprocal) * lines[k]
                columns[m] = columns[m] - factor * entry
            done.append(lines[k] * lax.rsqrt(top))
            part = factor * lines[k]
            change = part if change is None else change + part
        table = (table - change)[PIVOTS:]
    inverse[...] = jnp.concatenate(done, axis=0)[:, rank:]


def cholesky_inverse(gram):
    return pl.pallas_call(
        inverse_kernel,
        in_specs=[pl.BlockSpec(memory_space=pltpu.VMEM)],
        out_specs=pl.BlockSpec(memory_space=pltpu.VMEM),
        out_shape=jax.ShapeDtypeStruct(gram.shape, F32),
        compiler_params=params(),
        cost_estimate=cost(SMALL),
        name="cholesky_inverse",
    )(gram)


def spread(target, rows, value):
    rank = value.shape[1]
    high, low = split2(value)
    for place, term in enumerate((high, high, low, low)):
        target[rows, place * rank : (place + 1) * rank] = term


def operand_kernel(replicas, inverse, left_sum, lhs):
    rank, rows = left_sum.shape
    orth_t = jnp.dot(inverse[...], left_sum[...], precision=HIGHEST, preferred_element_type=F32)
    share = inverse[...] * (1.0 / replicas)
    weight_t = lax.dot_general(
        share, orth_t, (((0,), (0,)), ((), ())), precision=HIGHEST, preferred_element_type=F32
    )
    spread(lhs, slice(0, rows), -weight_t.T)
    spread(lhs, slice(rows, rows + rank), share)


def last_operand(inverse, left_sum, replicas):
    rank, rows = left_sum.shape
    return pl.pallas_call(
        functools.partial(operand_kernel, replicas),
        in_specs=[pl.BlockSpec(memory_space=pltpu.VMEM)] * 2,
        out_specs=pl.BlockSpec(memory_space=pltpu.VMEM),
        out_shape=jax.ShapeDtypeStruct((rows + rank, 4 * rank), BF16),
        compiler_params=params(),
        cost_estimate=cost(SMALL),
        name="last_operand",
    )(inverse, left_sum)


def final_kernel(side, shares, lhs, merged, *refs):
    out, factor, rhs, out_here, factor_here, sems = refs[-6:]
    owner = lax.axis_index("dp") ^ side
    rows = merged.shape[0]
    count, rank, cols = shares.shape
    copies = []
    for index in range(count):
        span = columns_of(place_of(owner, index), cols)
        high, low = split2(shares[index])
        for place, term in enumerate((high, low, high, low)):
            rhs[index % 2, place * rank : (place + 1) * rank, :] = term
        product = nn(lhs[...], rhs[index % 2])
        factor_here[index] = product[rows:]
        out_here[index] = (merged[:, span] + product[:rows]).astype(BF16)
        for order, (source, target) in enumerate(((out_here, out), (factor_here, factor))):
            copies.append(
                pltpu.make_async_copy(source.at[index], target.at[:, span], sems.at[index, order])
            )
            copies[-1].start()
    for copy in copies:
        copy.wait()


def finish(side, shares, lhs, merged, begun=()):
    count, rank, cols = shares.shape
    rows, width = merged.shape
    return pl.pallas_call(
        functools.partial(final_kernel, side),
        in_specs=[pl.BlockSpec(memory_space=pltpu.VMEM)] * 3
        + [pl.BlockSpec(memory_space=pl.ANY)] * len(begun),
        out_specs=[pl.BlockSpec(memory_space=pl.ANY)] * 2,
        out_shape=[
            jax.ShapeDtypeStruct((rows, width), BF16),
            jax.ShapeDtypeStruct((rank, width), F32),
        ],
        input_output_aliases={3 + index: index for index in range(len(begun))},
        scratch_shapes=[
            pltpu.VMEM((2, lhs.shape[1], cols), BF16),
            pltpu.VMEM((count, rows, cols), BF16),
            pltpu.VMEM((count, rank, cols), F32),
            pltpu.SemaphoreType.DMA((count, 2)),
        ],
        compiler_params=params(),
        cost_estimate=cost(1.5),
        name="finish",
    )(shares, lhs, merged, *begun)


def ring_order(chips):
    if chips == 8:
        return [0, 1, 3, 5, 7, 6, 4, 2]
    return list(range(chips))


def ring_gather(shard, chips, beside):
    order = ring_order(chips)
    position = {chip: place for place, chip in enumerate(order)}
    right = [(order[i], order[(i + 1) % chips]) for i in range(chips)]
    left = [(b, a) for a, b in right]
    halves = halves_of(shard)
    pieces = list(halves)
    origin = [(0, 0), (0, 1)]
    far = chips // 2
    *later, beside = lax.optimization_barrier((*halves, beside))
    going = {(1, 0): halves[0], (-1, 1): halves[1], (1, 1): later[1], (-1, 0): later[0]}
    for hop in range(1, far + 1):
        for way, half in ((1, 0), (-1, 1), (1, 1), (-1, 0)):
            if hop == far and (half == 0) != (way == 1):
                continue
            going[way, half] = lax.ppermute(going[way, half], "tp", right if way == 1 else left)
            pieces.append(going[way, half])
            origin.append((-way * hop, half))
    places = np.zeros((chips, len(pieces)), np.int32)
    for chip in range(chips):
        for index, (shift, half) in enumerate(origin):
            places[chip, index] = 2 * order[(position[chip] + shift) % chips] + half
    return pieces, places, beside


def swap(value):
    return lax.ppermute(value, "dp", [(0, 1), (1, 0)])


def local(grad_out, hidden, feedback, right_factor):
    shard, residue = grad_out[0], feedback[0]
    hidden_t = hidden[0].T
    chips, replicas = lax.axis_size("tp"), lax.axis_size("dp")
    rank = right_factor.shape[0]

    half = chips // 2

    def exchange(value, index, place=None):
        pairs = []
        for chip in range(chips):
            for core in range(2):
                to = (index >> 1) * 4 + core * 2 + (index & 1) if place is None else place
                if to:
                    pairs.append((2 * chip + core, 2 * (chip ^ to) + core))
        return lax.ppermute(value, ("tp", "dp"), pairs)

    pieces, places, (terms, residue_t) = ring_gather(shard, chips, residue_left(right_factor, residue))
    places = jnp.asarray(places)
    tokens, hidden_rows, left_t = early_left(places, pieces[:-2], terms, residue_t, hidden_t)
    tokens, left_t = late_left(places, pieces[-2:], terms, hidden_rows, left_t, tokens)
    give, left_sum, lhs, rhs = given_far(left_t, swap(left_t), hidden_t, residue, tokens, chips)
    got = swap(give)
    keep, gram = kept_far(left_sum, lhs, rhs, residue, tokens, chips)
    far = messages_for(keep, got, gram)
    give, keep = near_terms(lhs, rhs, residue, tokens, chips)
    messages = [*messages_for(keep, swap(give), gram), *far]

    passed = [exchange(messages[index + 1], index + 1, 1) for index in range(2, half, 2)]
    second = exchange(messages[0], 0)
    across = [exchange(added(messages[2 * i + 2], value), 2 * i + 2) for i, value in enumerate(passed)]
    tokens, _ = lax.optimization_barrier((tokens, messages[1]))
    merged = merged_sum(hidden_t, residue, tokens)
    beside, passed = lax.optimization_barrier((messages[1], passed))
    first = exchange(beside, 1)
    second, merged = lax.optimization_barrier((second, merged))
    partial = core_sum(messages[0], second, first, across)
    share, gram_matrix = chip_sum(partial, swap(partial), rank)

    across = [exchange(share, index) for index in range(2, half, 2)]
    first, second = exchange(share, 1), exchange(share, 0)
    passed = [exchange(value, 2 * i + 3, 1) for i, value in enumerate(across)]
    gram_matrix, first, second, across[0] = lax.optimization_barrier((gram_matrix, first, second, across[0]))
    lhs = last_operand(cholesky_inverse(gram_matrix), left_sum, replicas)
    passed, lhs = lax.optimization_barrier((passed, lhs))
    mine = joined(share, second, first, [value for pair in zip(across, passed) for value in pair])
    theirs = swap(mine)
    begun = finish(0, mine, lhs, merged)
    new_feedback, new_factor = finish(1, theirs, lhs, merged, begun)
    return new_feedback[None], new_factor


def solution(mesh):
    return jax.shard_map(
        local,
        mesh=mesh,
        in_specs=(
            P(("runs", "dp"), "tp", None),
            P(("runs", "dp"), None, "tp"),
            P(("runs", "dp"), "tp", None),
            P(),
        ),
        out_specs=(P(("runs", "dp"), "tp", None), P("runs", None)),
        check_vma=False,
    )
```

```python
import functools

import jax
import jax.numpy as jnp
import numpy as np
from jax import lax
from jax.experimental import pallas as pl
from jax.experimental.pallas import tpu as pltpu
from jax.sharding import PartitionSpec as P

F32 = jnp.float32
BF16 = jnp.bfloat16
HIGHEST = lax.Precision.HIGHEST
VMEM_LIMIT = 24 * 1024 * 1024
STEPS = 4
SMALL = 0.05
PIVOTS = 8


def split2(value):
    high = value.astype(BF16)
    return high, (value - high.astype(F32)).astype(BF16)


def fold2(stacked):
    rank = stacked.shape[0] // 2
    return stacked[:rank] + stacked[rank:]


def nn(a, b):
    return lax.dot_general(a, b, (((1,), (0,)), ((), ())), preferred_element_type=F32)


def nt(a, b):
    return lax.dot_general(a, b, (((1,), (1,)), ((), ())), preferred_element_type=F32)


def params(semantics=None, limit=VMEM_LIMIT):
    return pltpu.CompilerParams(vmem_limit_bytes=limit, dimension_semantics=semantics)


def cost(microseconds):
    return pl.CostEstimate(flops=int(microseconds * 1.15e9), bytes_accessed=0, transcendentals=0)


def whole(shape):
    return pl.BlockSpec(shape, lambda *_: (0,) * len(shape))


def halves_kernel(shard, first, second):
    size = first.shape[0]
    first[...] = shard[:size, :]
    second[...] = shard[size:, :]


def halves_of(shard):
    half = jax.ShapeDtypeStruct((shard.shape[0] // 2, shard.shape[1]), BF16)
    return pl.pallas_call(
        halves_kernel,
        in_specs=[pl.BlockSpec(memory_space=pltpu.VMEM)],
        out_specs=[pl.BlockSpec(memory_space=pltpu.VMEM)] * 2,
        out_shape=[half, half],
        compiler_params=params(),
        cost_estimate=cost(4.0),
        name="halves",
    )(shard)


def residue_kernel(right, feedback, terms, left_t):
    cols = right.shape[1] // STEPS
    total = None
    for step in range(STEPS):
        span = slice(step * cols, (step + 1) * cols)
        stacked = jnp.concatenate(split2(right[:, span]), axis=0)
        terms[:, span] = stacked
        part = nt(stacked, feedback[:, span])
        total = part if total is None else total + part
    left_t[...] = fold2(total)


def residue_left(right, feedback):
    rank, width = right.shape
    rows = feedback.shape[0]
    return pl.pallas_call(
        residue_kernel,
        in_specs=[pl.BlockSpec(memory_space=pltpu.VMEM)] * 2,
        out_specs=[pl.BlockSpec(memory_space=pltpu.VMEM)] * 2,
        out_shape=[
            jax.ShapeDtypeStruct((2 * rank, width), BF16),
            jax.ShapeDtypeStruct((rank, rows), F32),
        ],
        compiler_params=params(),
        cost_estimate=cost(2.2),
        name="residue_left",
    )(right, feedback)


def early_kernel(places, *refs):
    pieces, (terms, residue_t, hidden_t, tokens, hidden, left_t) = refs[:-6], refs[-6:]
    here = 2 * lax.axis_index("tp") + lax.axis_index("dp")
    size = pieces[0].shape[0]
    for index in range(len(pieces) + 2):
        rows = pl.ds(pl.multiple_of(places[here, index] * size, size), size)
        if index < len(pieces):
            tokens[rows, :] = pieces[index][...]
        else:
            tokens[rows, :] = jnp.zeros((size, tokens.shape[1]), BF16)
    projected = fold2(nt(terms[...], tokens[...]))
    stacked = jnp.concatenate(split2(projected), axis=0)
    left_t[...] = residue_t[...] + fold2(nt(stacked, hidden_t[...]))
    hidden[...] = hidden_t[...].T


def early_left(places, pieces, terms, residue_t, hidden_t):
    rows, count = hidden_t.shape
    width = terms.shape[1]
    operands = [*pieces, terms, residue_t, hidden_t]
    return pl.pallas_call(
        early_kernel,
        in_specs=[pl.BlockSpec(memory_space=pltpu.SMEM)]
        + [pl.BlockSpec(memory_space=pltpu.VMEM)] * len(operands),
        out_specs=[pl.BlockSpec(memory_space=pltpu.VMEM)] * 3,
        out_shape=[
            jax.ShapeDtypeStruct((count, width), BF16),
            jax.ShapeDtypeStruct((count, rows), BF16),
            jax.ShapeDtypeStruct(residue_t.shape, F32),
        ],
        compiler_params=params(),
        cost_estimate=cost(2.0),
        name="early_left",
    )(places, *operands)


def late_kernel(places, first, second, terms, hidden, early_t, _, tokens, left_t):
    here = 2 * lax.axis_index("tp") + lax.axis_index("dp")
    size = first.shape[0]
    count = places.shape[1]
    seen = []
    for index, piece in enumerate((first, second)):
        rows = pl.ds(pl.multiple_of(places[here, count - 2 + index] * size, size), size)
        tokens[rows, :] = piece[...]
        seen.append(hidden[rows, :])
    projected = fold2(nt(terms[...], jnp.concatenate([first[...], second[...]], axis=0)))
    stacked = jnp.concatenate(split2(projected), axis=0)
    left_t[...] = early_t[...] + fold2(nn(stacked, jnp.concatenate(seen, axis=0)))


def late_left(places, pieces, terms, hidden, early_t, tokens):
    operands = [*pieces, terms, hidden, early_t, tokens]
    return pl.pallas_call(
        late_kernel,
        in_specs=[pl.BlockSpec(memory_space=pltpu.SMEM)]
        + [pl.BlockSpec(memory_space=pltpu.VMEM)] * len(operands),
        out_specs=[pl.BlockSpec(memory_space=pltpu.VMEM)] * 2,
        out_shape=[
            jax.ShapeDtypeStruct(tokens.shape, BF16),
            jax.ShapeDtypeStruct(early_t.shape, F32),
        ],
        input_output_aliases={len(operands): 0},
        compiler_params=params(),
        cost_estimate=cost(1.0),
        name="late_left",
    )(places, *operands)


def core_of(place):
    return (place >> 1) & 1


def index_of(place):
    return (place >> 2) * 2 + (place & 1)


def place_of(core, index):
    return (index >> 1) * 4 + core * 2 + (index & 1)


def columns_of(place, cols):
    shard = lax.axis_index("tp") ^ place
    return pl.ds(pl.multiple_of(shard * cols, cols), cols)


def block_sum(lhs, rhs, feedback, tokens, core, index, cols):
    span = columns_of(place_of(core, index), cols)
    return fold2(nn(lhs[...], feedback[:, span]) + nn(rhs[...], tokens[:, span]))


def give_far_kernel(here_l, other_l, hidden_t, feedback, tokens, give, left_sum, lhs, rhs):
    left_t = here_l[...] + other_l[...]
    left_sum[...] = left_t
    lhs[...] = jnp.concatenate(split2(left_t), axis=0)
    seen_t = fold2(nn(lhs[...], hidden_t[...]))
    rhs[...] = jnp.concatenate(split2(seen_t), axis=0)
    other = 1 - lax.axis_index("dp")
    for index in range(give.shape[0]):
        give[index] = block_sum(lhs, rhs, feedback, tokens, other, index + 2, give.shape[2])


def given_far(here_l, other_l, hidden_t, feedback, tokens, chips):
    rank, rows = here_l.shape
    count, width = tokens.shape
    return pl.pallas_call(
        give_far_kernel,
        in_specs=[pl.BlockSpec(memory_space=pltpu.VMEM)] * 5,
        out_specs=[pl.BlockSpec(memory_space=pltpu.VMEM)] * 4,
        out_shape=[
            jax.ShapeDtypeStruct((chips // 2 - 2, rank, width // chips), F32),
            jax.ShapeDtypeStruct((rank, rows), F32),
            jax.ShapeDtypeStruct((2 * rank, rows), BF16),
            jax.ShapeDtypeStruct((2 * rank, count), BF16),
        ],
        compiler_params=params(),
        cost_estimate=cost(SMALL),
        name="given_far",
    )(here_l, other_l, hidden_t, feedback, tokens)


def keep_far_kernel(left_sum, lhs, rhs, feedback, tokens, keep, gram):
    core = lax.axis_index("dp")
    for index in range(keep.shape[0]):
        keep[index] = block_sum(lhs, rhs, feedback, tokens, core, index + 2, keep.shape[2])
    left_t = left_sum[...]
    gram[...] = lax.dot_general(
        left_t, left_t, (((1,), (1,)), ((), ())), precision=HIGHEST, preferred_element_type=F32
    )


def kept_far(left_sum, lhs, rhs, feedback, tokens, chips):
    rank = left_sum.shape[0]
    return pl.pallas_call(
        keep_far_kernel,
        in_specs=[pl.BlockSpec(memory_space=pltpu.VMEM)] * 5,
        out_specs=[pl.BlockSpec(memory_space=pltpu.VMEM)] * 2,
        out_shape=[
            jax.ShapeDtypeStruct((chips // 2 - 2, rank, tokens.shape[1] // chips), F32),
            jax.ShapeDtypeStruct((rank, rank), F32),
        ],
        compiler_params=params(),
        cost_estimate=cost(SMALL),
        name="kept_far",
    )(left_sum, lhs, rhs, feedback, tokens)


def near_kernel(lhs, rhs, feedback, tokens, give, keep):
    core = lax.axis_index("dp")
    for target, owner in ((give, 1 - core), (keep, core)):
        for index in range(2):
            target[index] = block_sum(lhs, rhs, feedback, tokens, owner, index, target.shape[2])


def near_terms(lhs, rhs, feedback, tokens, chips):
    block = jax.ShapeDtypeStruct((2, lhs.shape[0] // 2, tokens.shape[1] // chips), F32)
    return pl.pallas_call(
        near_kernel,
        in_specs=[pl.BlockSpec(memory_space=pltpu.VMEM)] * 4,
        out_specs=[pl.BlockSpec(memory_space=pltpu.VMEM)] * 2,
        out_shape=[block, block],
        compiler_params=params(),
        cost_estimate=cost(SMALL),
        name="near_terms",
    )(lhs, rhs, feedback, tokens)


def merged_kernel(hidden_t, feedback, tokens, merged):
    cols = tokens.shape[1] // STEPS
    for step in range(STEPS):
        span = slice(step * cols, (step + 1) * cols)
        merged[:, span] = nn(hidden_t[...], tokens[:, span]) + feedback[:, span].astype(F32)


def merged_sum(hidden_t, feedback, tokens):
    return pl.pallas_call(
        merged_kernel,
        in_specs=[pl.BlockSpec(memory_space=pltpu.VMEM)] * 3,
        out_specs=pl.BlockSpec(memory_space=pltpu.VMEM),
        out_shape=jax.ShapeDtypeStruct(feedback.shape, F32),
        compiler_params=params(),
        cost_estimate=cost(SMALL),
        name="merged",
    )(hidden_t, feedback, tokens)


def message_kernel(keep, got, gram, *messages):
    rank, cols = keep.shape[1:]
    blocks = cols // rank
    rows = rank // blocks
    for index, message in enumerate(messages):
        message[:rank, :] = keep[index] + got[index]
        for block in range(blocks):
            message[rank:, block * rank : (block + 1) * rank] = gram[block * rows : (block + 1) * rows, :]


def messages_for(keep, got, gram):
    places, rank, cols = keep.shape
    rows = rank + rank // (cols // rank)
    return pl.pallas_call(
        message_kernel,
        in_specs=[pl.BlockSpec(memory_space=pltpu.VMEM)] * 3,
        out_specs=[pl.BlockSpec(memory_space=pltpu.VMEM)] * places,
        out_shape=[jax.ShapeDtypeStruct((rows, cols), F32)] * places,
        compiler_params=params(),
        cost_estimate=cost(SMALL),
        name="messages",
    )(keep, got, gram)


def add_kernel(a, b, total):
    total[...] = a[...] + b[...]


def added(a, b):
    return pl.pallas_call(
        add_kernel,
        in_specs=[pl.BlockSpec(memory_space=pltpu.VMEM)] * 2,
        out_specs=pl.BlockSpec(memory_space=pltpu.VMEM),
        out_shape=jax.ShapeDtypeStruct(a.shape, a.dtype),
        compiler_params=params(),
        cost_estimate=cost(SMALL),
        name="added",
    )(a, b)


def join_kernel(share, second, first, *refs):
    across, mine = refs[:-1], refs[-1]
    mine[0] = jnp.where(lax.axis_index("dp") == 0, share[...], second[...])
    mine[1] = first[...]
    for index, value in enumerate(across):
        mine[index + 2] = value[...]


def joined(share, second, first, across):
    operands = [share, second, first, *across]
    return pl.pallas_call(
        join_kernel,
        in_specs=[pl.BlockSpec(memory_space=pltpu.VMEM)] * len(operands),
        out_specs=pl.BlockSpec(memory_space=pltpu.VMEM),
        out_shape=jax.ShapeDtypeStruct((len(operands) - 1, *share.shape), F32),
        compiler_params=params(),
        cost_estimate=cost(SMALL),
        name="joined",
    )(*operands)


def core_sum_kernel(own, second, *refs):
    messages, total = refs[:-1], refs[-1]
    first = jnp.where(lax.axis_index("dp") == 0, own[...], second[...])
    parts = [first + messages[0][...]] + [message[...] for message in messages[1:]]
    while len(parts) > 1:
        parts = [a + b for a, b in zip(parts[::2], parts[1::2])]
    total[...] = parts[0]


def core_sum(own, first, second, across):
    operands = [own, first, second, *across]
    return pl.pallas_call(
        core_sum_kernel,
        in_specs=[pl.BlockSpec(memory_space=pltpu.VMEM)] * len(operands),
        out_specs=pl.BlockSpec(memory_space=pltpu.VMEM),
        out_shape=jax.ShapeDtypeStruct(own.shape, F32),
        compiler_params=params(),
        cost_estimate=cost(SMALL),
        name="core_sum",
    )(*operands)


def chip_sum_kernel(here, other, share, gram):
    total = here[...] + other[...]
    rank, cols = share.shape
    blocks = cols // rank
    rows = rank // blocks
    share[...] = total[:rank]
    for block in range(blocks):
        gram[block * rows : (block + 1) * rows, :] = total[rank:, block * rank : (block + 1) * rank]


def chip_sum(here, other, rank):
    return pl.pallas_call(
        chip_sum_kernel,
        in_specs=[pl.BlockSpec(memory_space=pltpu.VMEM)] * 2,
        out_specs=[pl.BlockSpec(memory_space=pltpu.VMEM)] * 2,
        out_shape=[
            jax.ShapeDtypeStruct((rank, here.shape[1]), F32),
            jax.ShapeDtypeStruct((rank, rank), F32),
        ],
        compiler_params=params(),
        cost_estimate=cost(SMALL),
        name="chip_sum",
    )(here, other)


def inverse_kernel(gram, inverse):
    rank = gram.shape[0]
    row = lax.broadcasted_iota(jnp.int32, (rank, 2 * rank), 0)
    lane = lax.broadcasted_iota(jnp.int32, (rank, 2 * rank), 1)
    eye = (lane[:, rank:] == row[:, rank:] + rank).astype(F32)
    table = jnp.concatenate([gram[...], eye], axis=1)
    done = []
    for start in range(0, rank, PIVOTS):
        below = row[start:]
        each = range(PIVOTS)
        lines = [table[k : k + 1, :] for k in each]
        columns = [jnp.broadcast_to(table[:, start + k : start + k + 1], table.shape) for k in each]
        change = None
        for k in each:
            top = columns[k][k : k + 1, :]
            reciprocal = 1.0 / top
            factor = jnp.where(below > start + k, columns[k] * reciprocal, 0.0)
            for m in range(k + 1, PIVOTS):
                entry = columns[m][k : k + 1, :]
                lines[m] = lines[m] - (entry * reciprocal) * lines[k]
                columns[m] = columns[m] - factor * entry
            done.append(lines[k] * lax.rsqrt(top))
            part = factor * lines[k]
            change = part if change is None else change + part
        table = (table - change)[PIVOTS:]
    inverse[...] = jnp.concatenate(done, axis=0)[:, rank:]


def cholesky_inverse(gram):
    return pl.pallas_call(
        inverse_kernel,
        in_specs=[pl.BlockSpec(memory_space=pltpu.VMEM)],
        out_specs=pl.BlockSpec(memory_space=pltpu.VMEM),
        out_shape=jax.ShapeDtypeStruct(gram.shape, F32),
        compiler_params=params(),
        cost_estimate=cost(5.0),
        name="cholesky_inverse",
    )(gram)


def spread(target, rows, value):
    rank = value.shape[1]
    high, low = split2(value)
    for place, term in enumerate((high, high, low, low)):
        target[rows, place * rank : (place + 1) * rank] = term


def operand_kernel(replicas, inverse, left_sum, lhs):
    rank, rows = left_sum.shape
    orth_t = jnp.dot(inverse[...], left_sum[...], precision=HIGHEST, preferred_element_type=F32)
    share = inverse[...] * (1.0 / replicas)
    weight_t = lax.dot_general(
        share, orth_t, (((0,), (0,)), ((), ())), precision=HIGHEST, preferred_element_type=F32
    )
    spread(lhs, slice(0, rows), -weight_t.T)
    spread(lhs, slice(rows, rows + rank), share)


def last_operand(inverse, left_sum, replicas):
    rank, rows = left_sum.shape
    return pl.pallas_call(
        functools.partial(operand_kernel, replicas),
        in_specs=[pl.BlockSpec(memory_space=pltpu.VMEM)] * 2,
        out_specs=pl.BlockSpec(memory_space=pltpu.VMEM),
        out_shape=jax.ShapeDtypeStruct((rows + rank, 4 * rank), BF16),
        compiler_params=params(),
        cost_estimate=cost(SMALL),
        name="last_operand",
    )(inverse, left_sum)


def final_kernel(indices, side, shares, lhs, merged, *refs):
    out, factor, rhs, out_here, factor_here, sems = refs[-6:]
    owner = lax.axis_index("dp") ^ side
    rows = merged.shape[0]
    rank, cols = shares.shape[1:]
    copies = []
    for block, index in enumerate(indices):
        span = columns_of(place_of(owner, index), cols)
        high, low = split2(shares[block])
        for place, term in enumerate((high, low, high, low)):
            rhs[block % 2, place * rank : (place + 1) * rank, :] = term
        product = nn(lhs[...], rhs[block % 2])
        factor_here[block] = product[rows:]
        out_here[block] = (merged[:, span] + product[:rows]).astype(BF16)
        for number, (source, target) in enumerate(((out_here, out), (factor_here, factor))):
            copies.append(
                pltpu.make_async_copy(source.at[block], target.at[:, span], sems.at[block, number])
            )
            copies[-1].start()
    for copy in copies:
        copy.wait()


def finish(indices, shares, side, lhs, merged, begun=()):
    rank, cols = shares.shape[1:]
    rows, width = merged.shape
    blocks = len(indices)
    return pl.pallas_call(
        functools.partial(final_kernel, indices, side),
        in_specs=[pl.BlockSpec(memory_space=pltpu.VMEM)] * 3
        + [pl.BlockSpec(memory_space=pl.ANY)] * len(begun),
        out_specs=[pl.BlockSpec(memory_space=pl.ANY)] * 2,
        out_shape=[
            jax.ShapeDtypeStruct((rows, width), BF16),
            jax.ShapeDtypeStruct((rank, width), F32),
        ],
        input_output_aliases={3 + index: index for index in range(len(begun))},
        scratch_shapes=[
            pltpu.VMEM((2, lhs.shape[1], cols), BF16),
            pltpu.VMEM((blocks, rows, cols), BF16),
            pltpu.VMEM((blocks, rank, cols), F32),
            pltpu.SemaphoreType.DMA((blocks, 2)),
        ],
        compiler_params=params(),
        cost_estimate=cost(SMALL),
        name="finish",
    )(shares, lhs, merged, *begun)


def ring_order(chips):
    if chips == 8:
        return [0, 1, 3, 5, 7, 6, 4, 2]
    return list(range(chips))


def ring_gather(shard, chips, beside):
    order = ring_order(chips)
    position = {chip: place for place, chip in enumerate(order)}

    def pairs(way):
        steps = ((0, way), (1, -way))
        return [
            (2 * order[i] + core, 2 * order[(i + step) % chips] + core)
            for i in range(chips)
            for core, step in steps
        ]

    halves = halves_of(shard)
    pieces = list(halves)
    origin = [(0, 0), (0, 1)]
    far = chips // 2
    *later, beside = lax.optimization_barrier((*halves, beside))
    going = {(1, 0): halves[0], (-1, 1): halves[1], (1, 1): later[1], (-1, 0): later[0]}
    for hop in range(1, far + 1):
        for way, half in ((1, 0), (-1, 1), (1, 1), (-1, 0)):
            if hop == far and (half == 0) != (way == 1):
                continue
            going[way, half] = lax.ppermute(going[way, half], ("tp", "dp"), pairs(way))
            pieces.append(going[way, half])
            origin.append((-way * hop, half))
    places = np.zeros((2 * chips, len(pieces)), np.int32)
    for chip in range(chips):
        for core, sign in ((0, 1), (1, -1)):
            for index, (shift, half) in enumerate(origin):
                source = order[(position[chip] + sign * shift) % chips]
                places[2 * chip + core, index] = 2 * source + half
    return pieces, places, beside


def swap(value):
    return lax.ppermute(value, "dp", [(0, 1), (1, 0)])


def local(grad_out, hidden, feedback, right_factor):
    shard, residue = grad_out[0], feedback[0]
    hidden_t = hidden[0].T
    chips, replicas = lax.axis_size("tp"), lax.axis_size("dp")
    rank = right_factor.shape[0]

    half = chips // 2

    def exchange(value, index, place=None):
        pairs = []
        for chip in range(chips):
            for core in range(2):
                to = (index >> 1) * 4 + core * 2 + (index & 1) if place is None else place
                if to:
                    pairs.append((2 * chip + core, 2 * (chip ^ to) + core))
        return lax.ppermute(value, ("tp", "dp"), pairs)

    pieces, places, (terms, residue_t) = ring_gather(shard, chips, residue_left(right_factor, residue))
    places = jnp.asarray(places)
    tokens, hidden_rows, left_t = early_left(places, pieces[:-2], terms, residue_t, hidden_t)
    tokens, left_t = late_left(places, pieces[-2:], terms, hidden_rows, left_t, tokens)
    give, left_sum, lhs, rhs = given_far(left_t, swap(left_t), hidden_t, residue, tokens, chips)
    got = swap(give)
    keep, gram = kept_far(left_sum, lhs, rhs, residue, tokens, chips)
    far = messages_for(keep, got, gram)
    give, keep = near_terms(lhs, rhs, residue, tokens, chips)
    messages = [*messages_for(keep, swap(give), gram), *far]

    passed = [exchange(messages[index + 1], index + 1, 1) for index in range(2, half, 2)]
    second = exchange(messages[0], 0)
    across = [exchange(added(messages[2 * i + 2], value), 2 * i + 2) for i, value in enumerate(passed)]
    tokens, _ = lax.optimization_barrier((tokens, messages[1]))
    merged = merged_sum(hidden_t, residue, tokens)
    beside, passed = lax.optimization_barrier((messages[1], passed))
    first = exchange(beside, 1)
    second, merged = lax.optimization_barrier((second, merged))
    partial = core_sum(messages[0], second, first, across)
    share, gram_matrix = chip_sum(partial, swap(partial), rank)

    across = [exchange(share, index) for index in range(2, half, 2)]
    first, second = exchange(share, 1), exchange(share, 0)
    passed = [exchange(value, 2 * i + 3, 1) for i, value in enumerate(across)]
    passed = [exchange(value, 2 * i + 3, 1) for i, value in enumerate(across)]
    inverse = cholesky_inverse(gram_matrix)
    inverse, first, second, across[0] = lax.optimization_barrier((inverse, first, second, across[0]))
    lhs = last_operand(inverse, left_sum, replicas)
    mine = joined(share, second, first, across)
    begun = finish([0, 1, *range(2, half, 2)], mine, 0, lhs, merged)
    passed, begun = lax.optimization_barrier((passed, begun))
    rest = passed[0][None] if len(passed) == 1 else jnp.stack(passed)
    theirs = swap(jnp.concatenate([mine, rest]))
    begun = finish([*range(3, half, 2)], rest, 0, lhs, merged, begun)
    order = [0, 1, *range(2, half, 2), *range(3, half, 2)]
    new_feedback, new_factor = finish(order, theirs, 1, lhs, merged, begun)
    return new_feedback[None], new_factor


def solution(mesh):
    return jax.shard_map(
        local,
        mesh=mesh,
        in_specs=(
            P(("runs", "dp"), "tp", None),
            P(("runs", "dp"), None, "tp"),
            P(("runs", "dp"), "tp", None),
            P(),
        ),
        out_specs=(P(("runs", "dp"), "tp", None), P("runs", None)),
        check_vma=False,
    )
```

```python
import functools

import jax
import jax.numpy as jnp
import numpy as np
from jax import lax
from jax.experimental import pallas as pl
from jax.experimental.pallas import tpu as pltpu
from jax.sharding import PartitionSpec as P

F32 = jnp.float32
BF16 = jnp.bfloat16
HIGHEST = lax.Precision.HIGHEST
VMEM_LIMIT = 24 * 1024 * 1024
STEPS = 4
SMALL = 0.05
PIVOTS = 8


def split2(value):
    high = value.astype(BF16)
    return high, (value - high.astype(F32)).astype(BF16)


def fold2(stacked):
    rank = stacked.shape[0] // 2
    return stacked[:rank] + stacked[rank:]


def nn(a, b):
    return lax.dot_general(a, b, (((1,), (0,)), ((), ())), preferred_element_type=F32)


def nt(a, b):
    return lax.dot_general(a, b, (((1,), (1,)), ((), ())), preferred_element_type=F32)


def params(semantics=None, limit=VMEM_LIMIT):
    return pltpu.CompilerParams(vmem_limit_bytes=limit, dimension_semantics=semantics)


def cost(microseconds):
    return pl.CostEstimate(flops=int(microseconds * 1.15e9), bytes_accessed=0, transcendentals=0)


def whole(shape):
    return pl.BlockSpec(shape, lambda *_: (0,) * len(shape))


def halves_kernel(shard, first, second):
    size = first.shape[0]
    first[...] = shard[:size, :]
    second[...] = shard[size:, :]


def halves_of(shard):
    half = jax.ShapeDtypeStruct((shard.shape[0] // 2, shard.shape[1]), BF16)
    return pl.pallas_call(
        halves_kernel,
        in_specs=[pl.BlockSpec(memory_space=pltpu.VMEM)],
        out_specs=[pl.BlockSpec(memory_space=pltpu.VMEM)] * 2,
        out_shape=[half, half],
        compiler_params=params(),
        cost_estimate=cost(4.0),
        name="halves",
    )(shard)


def residue_kernel(right, feedback, terms, left_t):
    cols = right.shape[1] // STEPS
    total = None
    for step in range(STEPS):
        span = slice(step * cols, (step + 1) * cols)
        stacked = jnp.concatenate(split2(right[:, span]), axis=0)
        terms[:, span] = stacked
        part = nt(stacked, feedback[:, span])
        total = part if total is None else total + part
    left_t[...] = fold2(total)


def residue_left(right, feedback):
    rank, width = right.shape
    rows = feedback.shape[0]
    return pl.pallas_call(
        residue_kernel,
        in_specs=[pl.BlockSpec(memory_space=pltpu.VMEM)] * 2,
        out_specs=[pl.BlockSpec(memory_space=pltpu.VMEM)] * 2,
        out_shape=[
            jax.ShapeDtypeStruct((2 * rank, width), BF16),
            jax.ShapeDtypeStruct((rank, rows), F32),
        ],
        compiler_params=params(),
        cost_estimate=cost(2.2),
        name="residue_left",
    )(right, feedback)


def early_kernel(places, *refs):
    pieces, (terms, residue_t, hidden_t, tokens, hidden, left_t) = refs[:-6], refs[-6:]
    here = 2 * lax.axis_index("tp") + lax.axis_index("dp")
    size = pieces[0].shape[0]
    for index in range(len(pieces) + 2):
        rows = pl.ds(pl.multiple_of(places[here, index] * size, size), size)
        if index < len(pieces):
            tokens[rows, :] = pieces[index][...]
        else:
            tokens[rows, :] = jnp.zeros((size, tokens.shape[1]), BF16)
    projected = fold2(nt(terms[...], tokens[...]))
    stacked = jnp.concatenate(split2(projected), axis=0)
    left_t[...] = residue_t[...] + fold2(nt(stacked, hidden_t[...]))
    hidden[...] = hidden_t[...].T


def early_left(places, pieces, terms, residue_t, hidden_t):
    rows, count = hidden_t.shape
    width = terms.shape[1]
    operands = [*pieces, terms, residue_t, hidden_t]
    return pl.pallas_call(
        early_kernel,
        in_specs=[pl.BlockSpec(memory_space=pltpu.SMEM)]
        + [pl.BlockSpec(memory_space=pltpu.VMEM)] * len(operands),
        out_specs=[pl.BlockSpec(memory_space=pltpu.VMEM)] * 3,
        out_shape=[
            jax.ShapeDtypeStruct((count, width), BF16),
            jax.ShapeDtypeStruct((count, rows), BF16),
            jax.ShapeDtypeStruct(residue_t.shape, F32),
        ],
        compiler_params=params(),
        cost_estimate=cost(2.0),
        name="early_left",
    )(places, *operands)


def late_kernel(places, first, second, terms, hidden, early_t, _, tokens, left_t):
    here = 2 * lax.axis_index("tp") + lax.axis_index("dp")
    size = first.shape[0]
    count = places.shape[1]
    seen = []
    for index, piece in enumerate((first, second)):
        rows = pl.ds(pl.multiple_of(places[here, count - 2 + index] * size, size), size)
        tokens[rows, :] = piece[...]
        seen.append(hidden[rows, :])
    projected = fold2(nt(terms[...], jnp.concatenate([first[...], second[...]], axis=0)))
    stacked = jnp.concatenate(split2(projected), axis=0)
    left_t[...] = early_t[...] + fold2(nn(stacked, jnp.concatenate(seen, axis=0)))


def late_left(places, pieces, terms, hidden, early_t, tokens):
    operands = [*pieces, terms, hidden, early_t, tokens]
    return pl.pallas_call(
        late_kernel,
        in_specs=[pl.BlockSpec(memory_space=pltpu.SMEM)]
        + [pl.BlockSpec(memory_space=pltpu.VMEM)] * len(operands),
        out_specs=[pl.BlockSpec(memory_space=pltpu.VMEM)] * 2,
        out_shape=[
            jax.ShapeDtypeStruct(tokens.shape, BF16),
            jax.ShapeDtypeStruct(early_t.shape, F32),
        ],
        input_output_aliases={len(operands): 0},
        compiler_params=params(),
        cost_estimate=cost(1.0),
        name="late_left",
    )(places, *operands)


def core_of(place):
    return (place >> 1) & 1


def index_of(place):
    return (place >> 2) * 2 + (place & 1)


def place_of(core, index):
    return (index >> 1) * 4 + core * 2 + (index & 1)


def columns_of(place, cols):
    shard = lax.axis_index("tp") ^ place
    return pl.ds(pl.multiple_of(shard * cols, cols), cols)


def block_sum(lhs, rhs, feedback, tokens, core, index, cols):
    span = columns_of(place_of(core, index), cols)
    return fold2(nn(lhs[...], feedback[:, span]) + nn(rhs[...], tokens[:, span]))


def give_far_kernel(here_l, other_l, hidden_t, feedback, tokens, give, left_sum, lhs, rhs):
    left_t = here_l[...] + other_l[...]
    left_sum[...] = left_t
    lhs[...] = jnp.concatenate(split2(left_t), axis=0)
    seen_t = fold2(nn(lhs[...], hidden_t[...]))
    rhs[...] = jnp.concatenate(split2(seen_t), axis=0)
    other = 1 - lax.axis_index("dp")
    for index in range(give.shape[0]):
        give[index] = block_sum(lhs, rhs, feedback, tokens, other, index + 2, give.shape[2])


def given_far(here_l, other_l, hidden_t, feedback, tokens, chips):
    rank, rows = here_l.shape
    count, width = tokens.shape
    return pl.pallas_call(
        give_far_kernel,
        in_specs=[pl.BlockSpec(memory_space=pltpu.VMEM)] * 5,
        out_specs=[pl.BlockSpec(memory_space=pltpu.VMEM)] * 4,
        out_shape=[
            jax.ShapeDtypeStruct((chips // 2 - 2, rank, width // chips), F32),
            jax.ShapeDtypeStruct((rank, rows), F32),
            jax.ShapeDtypeStruct((2 * rank, rows), BF16),
            jax.ShapeDtypeStruct((2 * rank, count), BF16),
        ],
        compiler_params=params(),
        cost_estimate=cost(SMALL),
        name="given_far",
    )(here_l, other_l, hidden_t, feedback, tokens)


def keep_far_kernel(left_sum, lhs, rhs, feedback, tokens, keep, gram):
    core = lax.axis_index("dp")
    for index in range(keep.shape[0]):
        keep[index] = block_sum(lhs, rhs, feedback, tokens, core, index + 2, keep.shape[2])
    left_t = left_sum[...]
    gram[...] = lax.dot_general(
        left_t, left_t, (((1,), (1,)), ((), ())), precision=HIGHEST, preferred_element_type=F32
    )


def kept_far(left_sum, lhs, rhs, feedback, tokens, chips):
    rank = left_sum.shape[0]
    return pl.pallas_call(
        keep_far_kernel,
        in_specs=[pl.BlockSpec(memory_space=pltpu.VMEM)] * 5,
        out_specs=[pl.BlockSpec(memory_space=pltpu.VMEM)] * 2,
        out_shape=[
            jax.ShapeDtypeStruct((chips // 2 - 2, rank, tokens.shape[1] // chips), F32),
            jax.ShapeDtypeStruct((rank, rank), F32),
        ],
        compiler_params=params(),
        cost_estimate=cost(SMALL),
        name="kept_far",
    )(left_sum, lhs, rhs, feedback, tokens)


def near_kernel(lhs, rhs, feedback, tokens, give, keep):
    core = lax.axis_index("dp")
    for target, owner in ((give, 1 - core), (keep, core)):
        for index in range(2):
            target[index] = block_sum(lhs, rhs, feedback, tokens, owner, index, target.shape[2])


def near_terms(lhs, rhs, feedback, tokens, chips):
    block = jax.ShapeDtypeStruct((2, lhs.shape[0] // 2, tokens.shape[1] // chips), F32)
    return pl.pallas_call(
        near_kernel,
        in_specs=[pl.BlockSpec(memory_space=pltpu.VMEM)] * 4,
        out_specs=[pl.BlockSpec(memory_space=pltpu.VMEM)] * 2,
        out_shape=[block, block],
        compiler_params=params(),
        cost_estimate=cost(SMALL),
        name="near_terms",
    )(lhs, rhs, feedback, tokens)


def merged_kernel(hidden_t, feedback, tokens, merged):
    cols = tokens.shape[1] // STEPS
    for step in range(STEPS):
        span = slice(step * cols, (step + 1) * cols)
        merged[:, span] = nn(hidden_t[...], tokens[:, span]) + feedback[:, span].astype(F32)


def merged_sum(hidden_t, feedback, tokens):
    return pl.pallas_call(
        merged_kernel,
        in_specs=[pl.BlockSpec(memory_space=pltpu.VMEM)] * 3,
        out_specs=pl.BlockSpec(memory_space=pltpu.VMEM),
        out_shape=jax.ShapeDtypeStruct(feedback.shape, F32),
        compiler_params=params(),
        cost_estimate=cost(SMALL),
        name="merged",
    )(hidden_t, feedback, tokens)


def put_message(message, value, gram):
    rank = gram.shape[0]
    blocks = value.shape[1] // rank
    rows = rank // blocks
    message[:rank, :] = value
    for block in range(blocks):
        message[rank:, block * rank : (block + 1) * rank] = gram[block * rows : (block + 1) * rows, :]


def begin_kernel(keep, got, gram, *messages):
    core = lax.axis_index("dp")
    for pair, message in enumerate(messages):
        index = 2 * pair + core
        put_message(message, keep[index] + got[index], gram)


def begin_messages(keep, got, gram):
    rank, cols = keep.shape[1:]
    pairs = keep.shape[0] // 2
    rows = rank + rank // (cols // rank)
    return pl.pallas_call(
        begin_kernel,
        in_specs=[pl.BlockSpec(memory_space=pltpu.VMEM)] * 3,
        out_specs=[pl.BlockSpec(memory_space=pltpu.VMEM)] * pairs,
        out_shape=[jax.ShapeDtypeStruct((rows, cols), F32)] * pairs,
        compiler_params=params(),
        cost_estimate=cost(SMALL),
        name="begin_messages",
    )(keep, got, gram)


def rest_kernel(keep_far, got_far, keep, got, gram, own, beside, *messages):
    first = lax.axis_index("dp") == 0
    put_message(own, keep[0] + got[0], gram)
    put_message(beside, keep[1] + got[1], gram)
    for pair in range(len(messages) // 2):
        direct = keep_far[2 * pair + 1] + got_far[2 * pair + 1]
        crossing = keep_far[2 * pair] + got_far[2 * pair]
        if pair == 0:
            direct = jnp.where(first, direct, keep[0] + got[0])
            crossing = jnp.where(first, keep[1] + got[1], crossing)
        put_message(messages[2 * pair], direct, gram)
        put_message(messages[2 * pair + 1], crossing, gram)


def rest_messages(keep_far, got_far, keep, got, gram):
    rank, cols = keep.shape[1:]
    count = 2 + keep_far.shape[0]
    rows = rank + rank // (cols // rank)
    own, beside, *messages = pl.pallas_call(
        rest_kernel,
        in_specs=[pl.BlockSpec(memory_space=pltpu.VMEM)] * 5,
        out_specs=[pl.BlockSpec(memory_space=pltpu.VMEM)] * count,
        out_shape=[jax.ShapeDtypeStruct((rows, cols), F32)] * count,
        compiler_params=params(),
        cost_estimate=cost(SMALL),
        name="rest_messages",
    )(keep_far, got_far, keep, got, gram)
    return own, beside, messages[::2], messages[1::2]


def cross_kernel(message, passed, total):
    total[...] = message[...] + jnp.where(lax.axis_index("dp") == 0, 0.0, passed[...])


def crossing(message, passed):
    return pl.pallas_call(
        cross_kernel,
        in_specs=[pl.BlockSpec(memory_space=pltpu.VMEM)] * 2,
        out_specs=pl.BlockSpec(memory_space=pltpu.VMEM),
        out_shape=jax.ShapeDtypeStruct(message.shape, F32),
        compiler_params=params(),
        cost_estimate=cost(SMALL),
        name="crossing",
    )(message, passed)


def core_sum_kernel(own, third, *refs):
    messages, total = refs[:-1], refs[-1]
    pairs = len(messages) // 3
    begun, direct, crossed = messages[:pairs], messages[pairs : 2 * pairs], messages[2 * pairs :]
    first = lax.axis_index("dp") == 0
    parts = [jnp.where(first, own[...] + crossed[0][...], direct[0][...] + third[...])]
    for pair in range(pairs):
        parts.append(jnp.where(first, begun[pair][...] + direct[pair][...], crossed[pair][...]))
    while len(parts) > 1:
        parts = [a + b for a, b in zip(parts[::2], parts[1::2])]
    total[...] = parts[0]


def core_sum(own, third, begun, direct, crossed):
    operands = [own, third, *begun, *direct, *crossed]
    return pl.pallas_call(
        core_sum_kernel,
        in_specs=[pl.BlockSpec(memory_space=pltpu.VMEM)] * len(operands),
        out_specs=pl.BlockSpec(memory_space=pltpu.VMEM),
        out_shape=jax.ShapeDtypeStruct(own.shape, F32),
        compiler_params=params(),
        cost_estimate=cost(SMALL),
        name="core_sum",
    )(*operands)


def choose_kernel(here, there, chosen):
    chosen[...] = jnp.where(lax.axis_index("dp") == 0, here[...], there[...])


def by_core(here, there):
    return pl.pallas_call(
        choose_kernel,
        in_specs=[pl.BlockSpec(memory_space=pltpu.VMEM)] * 2,
        out_specs=pl.BlockSpec(memory_space=pltpu.VMEM),
        out_shape=jax.ShapeDtypeStruct(here.shape, F32),
        compiler_params=params(),
        cost_estimate=cost(SMALL),
        name="by_core",
    )(here, there)


def join_kernel(share, third, *refs):
    shares, mine = refs[:-1], refs[-1]
    pairs = len(shares) // 2
    begun, direct = shares[:pairs], shares[pairs:]
    first = lax.axis_index("dp") == 0
    mine[0] = jnp.where(first, share[...], direct[0][...])
    mine[1] = jnp.where(first, begun[0][...], third[...])
    for pair in range(pairs):
        mine[pair + 2] = jnp.where(first, direct[pair][...], begun[pair][...])


def joined(share, third, begun, direct):
    operands = [share, third, *begun, *direct]
    return pl.pallas_call(
        join_kernel,
        in_specs=[pl.BlockSpec(memory_space=pltpu.VMEM)] * len(operands),
        out_specs=pl.BlockSpec(memory_space=pltpu.VMEM),
        out_shape=jax.ShapeDtypeStruct((len(begun) + 2, *share.shape), F32),
        compiler_params=params(),
        cost_estimate=cost(SMALL),
        name="joined",
    )(*operands)


def chip_sum_kernel(here, other, share, gram):
    total = here[...] + other[...]
    rank, cols = share.shape
    blocks = cols // rank
    rows = rank // blocks
    share[...] = total[:rank]
    for block in range(blocks):
        gram[block * rows : (block + 1) * rows, :] = total[rank:, block * rank : (block + 1) * rank]


def chip_sum(here, other, rank):
    return pl.pallas_call(
        chip_sum_kernel,
        in_specs=[pl.BlockSpec(memory_space=pltpu.VMEM)] * 2,
        out_specs=[pl.BlockSpec(memory_space=pltpu.VMEM)] * 2,
        out_shape=[
            jax.ShapeDtypeStruct((rank, here.shape[1]), F32),
            jax.ShapeDtypeStruct((rank, rank), F32),
        ],
        compiler_params=params(),
        cost_estimate=cost(SMALL),
        name="chip_sum",
    )(here, other)


def inverse_kernel(gram, inverse):
    rank = gram.shape[0]
    row = lax.broadcasted_iota(jnp.int32, (rank, 2 * rank), 0)
    lane = lax.broadcasted_iota(jnp.int32, (rank, 2 * rank), 1)
    eye = (lane[:, rank:] == row[:, rank:] + rank).astype(F32)
    table = jnp.concatenate([gram[...], eye], axis=1)
    done = []
    for start in range(0, rank, PIVOTS):
        below = row[start:]
        each = range(PIVOTS)
        lines = [table[k : k + 1, :] for k in each]
        columns = [jnp.broadcast_to(table[:, start + k : start + k + 1], table.shape) for k in each]
        change = None
        for k in each:
            top = columns[k][k : k + 1, :]
            reciprocal = 1.0 / top
            factor = jnp.where(below > start + k, columns[k] * reciprocal, 0.0)
            for m in range(k + 1, PIVOTS):
                entry = columns[m][k : k + 1, :]
                lines[m] = lines[m] - (entry * reciprocal) * lines[k]
                columns[m] = columns[m] - factor * entry
            done.append(lines[k] * lax.rsqrt(top))
            part = factor * lines[k]
            change = part if change is None else change + part
        table = (table - change)[PIVOTS:]
    inverse[...] = jnp.concatenate(done, axis=0)[:, rank:]


def cholesky_inverse(gram):
    return pl.pallas_call(
        inverse_kernel,
        in_specs=[pl.BlockSpec(memory_space=pltpu.VMEM)],
        out_specs=pl.BlockSpec(memory_space=pltpu.VMEM),
        out_shape=jax.ShapeDtypeStruct(gram.shape, F32),
        compiler_params=params(),
        cost_estimate=cost(5.0),
        name="cholesky_inverse",
    )(gram)


def spread(target, rows, value):
    rank = value.shape[1]
    high, low = split2(value)
    for place, term in enumerate((high, high, low, low)):
        target[rows, place * rank : (place + 1) * rank] = term


def operand_kernel(replicas, inverse, left_sum, lhs):
    rank, rows = left_sum.shape
    orth_t = jnp.dot(inverse[...], left_sum[...], precision=HIGHEST, preferred_element_type=F32)
    share = inverse[...] * (1.0 / replicas)
    weight_t = lax.dot_general(
        share, orth_t, (((0,), (0,)), ((), ())), precision=HIGHEST, preferred_element_type=F32
    )
    spread(lhs, slice(0, rows), -weight_t.T)
    spread(lhs, slice(rows, rows + rank), share)


def last_operand(inverse, left_sum, replicas):
    rank, rows = left_sum.shape
    return pl.pallas_call(
        functools.partial(operand_kernel, replicas),
        in_specs=[pl.BlockSpec(memory_space=pltpu.VMEM)] * 2,
        out_specs=pl.BlockSpec(memory_space=pltpu.VMEM),
        out_shape=jax.ShapeDtypeStruct((rows + rank, 4 * rank), BF16),
        compiler_params=params(),
        cost_estimate=cost(SMALL),
        name="last_operand",
    )(inverse, left_sum)


def final_kernel(indices, side, shares, lhs, merged, *refs):
    out, factor, rhs, out_here, factor_here, sems = refs[-6:]
    owner = lax.axis_index("dp") ^ side
    rows = merged.shape[0]
    rank, cols = shares.shape[1:]
    copies = []
    for block, index in enumerate(indices):
        span = columns_of(place_of(owner, index), cols)
        high, low = split2(shares[block])
        for place, term in enumerate((high, low, high, low)):
            rhs[block % 2, place * rank : (place + 1) * rank, :] = term
        product = nn(lhs[...], rhs[block % 2])
        factor_here[block] = product[rows:]
        out_here[block] = (merged[:, span] + product[:rows]).astype(BF16)
        for number, (source, target) in enumerate(((out_here, out), (factor_here, factor))):
            copies.append(
                pltpu.make_async_copy(source.at[block], target.at[:, span], sems.at[block, number])
            )
            copies[-1].start()
    for copy in copies:
        copy.wait()


def finish(indices, shares, side, lhs, merged, begun=()):
    rank, cols = shares.shape[1:]
    rows, width = merged.shape
    blocks = len(indices)
    return pl.pallas_call(
        functools.partial(final_kernel, indices, side),
        in_specs=[pl.BlockSpec(memory_space=pltpu.VMEM)] * 3
        + [pl.BlockSpec(memory_space=pl.ANY)] * len(begun),
        out_specs=[pl.BlockSpec(memory_space=pl.ANY)] * 2,
        out_shape=[
            jax.ShapeDtypeStruct((rows, width), BF16),
            jax.ShapeDtypeStruct((rank, width), F32),
        ],
        input_output_aliases={3 + index: index for index in range(len(begun))},
        scratch_shapes=[
            pltpu.VMEM((2, lhs.shape[1], cols), BF16),
            pltpu.VMEM((blocks, rows, cols), BF16),
            pltpu.VMEM((blocks, rank, cols), F32),
            pltpu.SemaphoreType.DMA((blocks, 2)),
        ],
        compiler_params=params(),
        cost_estimate=cost(SMALL),
        name="finish",
    )(shares, lhs, merged, *begun)


def ring_order(chips):
    if chips == 8:
        return [0, 1, 3, 5, 7, 6, 4, 2]
    return list(range(chips))


def ring_gather(shard, chips, beside):
    order = ring_order(chips)
    position = {chip: place for place, chip in enumerate(order)}

    def pairs(way):
        steps = ((0, way), (1, -way))
        return [
            (2 * order[i] + core, 2 * order[(i + step) % chips] + core)
            for i in range(chips)
            for core, step in steps
        ]

    halves = halves_of(shard)
    pieces = list(halves)
    origin = [(0, 0), (0, 1)]
    far = chips // 2
    *later, beside = lax.optimization_barrier((*halves, beside))
    going = {(1, 0): halves[0], (-1, 1): halves[1], (1, 1): later[1], (-1, 0): later[0]}
    for hop in range(1, far + 1):
        for way, half in ((1, 0), (-1, 1), (1, 1), (-1, 0)):
            if hop == far and (half == 0) != (way == 1):
                continue
            going[way, half] = lax.ppermute(going[way, half], ("tp", "dp"), pairs(way))
            pieces.append(going[way, half])
            origin.append((-way * hop, half))
    places = np.zeros((2 * chips, len(pieces)), np.int32)
    for chip in range(chips):
        for core, sign in ((0, 1), (1, -1)):
            for index, (shift, half) in enumerate(origin):
                source = order[(position[chip] + sign * shift) % chips]
                places[2 * chip + core, index] = 2 * source + half
    return pieces, places, beside


def swap(value):
    return lax.ppermute(value, "dp", [(0, 1), (1, 0)])


def local(grad_out, hidden, feedback, right_factor):
    shard, residue = grad_out[0], feedback[0]
    hidden_t = hidden[0].T
    chips, replicas = lax.axis_size("tp"), lax.axis_size("dp")
    rank = right_factor.shape[0]

    def send(value, first, second):
        pairs = []
        for chip in range(chips):
            for core, place in enumerate((first, second)):
                if place:
                    pairs.append((2 * chip + core, 2 * (chip ^ place) + core))
        return lax.ppermute(value, ("tp", "dp"), pairs)

    pieces, places, (terms, residue_t) = ring_gather(shard, chips, residue_left(right_factor, residue))
    places = jnp.asarray(places)
    tokens, hidden_rows, left_t = early_left(places, pieces[:-2], terms, residue_t, hidden_t)
    tokens, left_t = late_left(places, pieces[-2:], terms, hidden_rows, left_t, tokens)
    give, left_sum, lhs, rhs = given_far(left_t, swap(left_t), hidden_t, residue, tokens, chips)
    got = swap(give)
    keep, gram = kept_far(left_sum, lhs, rhs, residue, tokens, chips)
    begin = begin_messages(keep, got, gram)
    give, keep_near = near_terms(lhs, rhs, residue, tokens, chips)
    own, beside, direct, cross = rest_messages(keep, got, keep_near, swap(give), gram)

    evens = range(4, chips, 4)
    begun = [send(value, place, 1) for value, place in zip(begin, evens)]
    direct = [send(value, place + 1, 2 * (place == 4)) for value, place in zip(direct, evens)]
    third = send(beside, 0, 3)
    cross = [crossing(value, passed) for value, passed in zip(cross, begun)]
    crossed = [send(value, int(place == 4), place + 2) for value, place in zip(cross, evens)]
    tokens, _ = lax.optimization_barrier((tokens, beside))
    merged = merged_sum(hidden_t, residue, tokens)
    third, merged = lax.optimization_barrier((third, merged))
    partial = core_sum(own, third, begun, direct, crossed)
    share, gram_matrix = chip_sum(partial, swap(partial), rank)

    begun = [send(share, int(place == 4), place + 2) for place in evens]
    direct = [send(share, place, 2 * (place == 4)) for place in evens]
    third = send(share, 0, 3)
    passed = [send(by_core(share, value), place + 1, 1) for value, place in zip(begun, evens)]
    inverse = cholesky_inverse(gram_matrix)
    inverse, third, begun, direct = lax.optimization_barrier((inverse, third, begun, direct))
    lhs = last_operand(inverse, left_sum, replicas)
    mine = joined(share, third, begun, direct)
    half = chips // 2
    begun = finish([0, 1, *range(2, half, 2)], mine, 0, lhs, merged)
    passed, begun = lax.optimization_barrier((passed, begun))
    rest = passed[0][None] if len(passed) == 1 else jnp.stack(passed)
    theirs = swap(jnp.concatenate([mine, rest]))
    begun = finish([*range(3, half, 2)], rest, 0, lhs, merged, begun)
    order = [0, 1, *range(2, half, 2), *range(3, half, 2)]
    new_feedback, new_factor = finish(order, theirs, 1, lhs, merged, begun)
    return new_feedback[None], new_factor


def solution(mesh):
    return jax.shard_map(
        local,
        mesh=mesh,
        in_specs=(
            P(("runs", "dp"), "tp", None),
            P(("runs", "dp"), None, "tp"),
            P(("runs", "dp"), "tp", None),
            P(),
        ),
        out_specs=(P(("runs", "dp"), "tp", None), P("runs", None)),
        check_vma=False,
    )
```

```python
import functools

import jax
import jax.numpy as jnp
import numpy as np
from jax import lax
from jax.experimental import pallas as pl
from jax.experimental.pallas import tpu as pltpu
from jax.sharding import PartitionSpec as P

F32 = jnp.float32
BF16 = jnp.bfloat16
HIGHEST = lax.Precision.HIGHEST
VMEM_LIMIT = 24 * 1024 * 1024
STEPS = 4
SMALL = 0.05
PIVOTS = 8


def split2(value):
    high = value.astype(BF16)
    return high, (value - high.astype(F32)).astype(BF16)


def fold2(stacked):
    rank = stacked.shape[0] // 2
    return stacked[:rank] + stacked[rank:]


def nn(a, b):
    return lax.dot_general(a, b, (((1,), (0,)), ((), ())), preferred_element_type=F32)


def nt(a, b):
    return lax.dot_general(a, b, (((1,), (1,)), ((), ())), preferred_element_type=F32)


def params(semantics=None, limit=VMEM_LIMIT):
    return pltpu.CompilerParams(vmem_limit_bytes=limit, dimension_semantics=semantics)


def cost(microseconds):
    return pl.CostEstimate(flops=int(microseconds * 1.15e9), bytes_accessed=0, transcendentals=0)


def whole(shape):
    return pl.BlockSpec(shape, lambda *_: (0,) * len(shape))


def halves_kernel(shard, first, second):
    size = first.shape[0]
    first[...] = shard[:size, :]
    second[...] = shard[size:, :]


def halves_of(shard):
    half = jax.ShapeDtypeStruct((shard.shape[0] // 2, shard.shape[1]), BF16)
    return pl.pallas_call(
        halves_kernel,
        in_specs=[pl.BlockSpec(memory_space=pltpu.VMEM)],
        out_specs=[pl.BlockSpec(memory_space=pltpu.VMEM)] * 2,
        out_shape=[half, half],
        compiler_params=params(),
        cost_estimate=cost(4.0),
        name="halves",
    )(shard)


def residue_kernel(right, feedback, terms, left_t):
    cols = right.shape[1] // STEPS
    total = None
    for step in range(STEPS):
        span = slice(step * cols, (step + 1) * cols)
        stacked = jnp.concatenate(split2(right[:, span]), axis=0)
        terms[:, span] = stacked
        part = nt(stacked, feedback[:, span])
        total = part if total is None else total + part
    left_t[...] = fold2(total)


def residue_left(right, feedback):
    rank, width = right.shape
    rows = feedback.shape[0]
    return pl.pallas_call(
        residue_kernel,
        in_specs=[pl.BlockSpec(memory_space=pltpu.VMEM)] * 2,
        out_specs=[pl.BlockSpec(memory_space=pltpu.VMEM)] * 2,
        out_shape=[
            jax.ShapeDtypeStruct((2 * rank, width), BF16),
            jax.ShapeDtypeStruct((rank, rows), F32),
        ],
        compiler_params=params(),
        cost_estimate=cost(2.2),
        name="residue_left",
    )(right, feedback)


def early_kernel(places, *refs):
    pieces, (terms, residue_t, hidden_t, tokens, hidden, left_t) = refs[:-6], refs[-6:]
    here = 2 * lax.axis_index("tp") + lax.axis_index("dp")
    size = pieces[0].shape[0]
    for index in range(len(pieces) + 2):
        rows = pl.ds(pl.multiple_of(places[here, index] * size, size), size)
        if index < len(pieces):
            tokens[rows, :] = pieces[index][...]
        else:
            tokens[rows, :] = jnp.zeros((size, tokens.shape[1]), BF16)
    projected = fold2(nt(terms[...], tokens[...]))
    stacked = jnp.concatenate(split2(projected), axis=0)
    left_t[...] = residue_t[...] + fold2(nt(stacked, hidden_t[...]))
    hidden[...] = hidden_t[...].T


def early_left(places, pieces, terms, residue_t, hidden_t):
    rows, count = hidden_t.shape
    width = terms.shape[1]
    operands = [*pieces, terms, residue_t, hidden_t]
    return pl.pallas_call(
        early_kernel,
        in_specs=[pl.BlockSpec(memory_space=pltpu.SMEM)]
        + [pl.BlockSpec(memory_space=pltpu.VMEM)] * len(operands),
        out_specs=[pl.BlockSpec(memory_space=pltpu.VMEM)] * 3,
        out_shape=[
            jax.ShapeDtypeStruct((count, width), BF16),
            jax.ShapeDtypeStruct((count, rows), BF16),
            jax.ShapeDtypeStruct(residue_t.shape, F32),
        ],
        compiler_params=params(),
        cost_estimate=cost(2.0),
        name="early_left",
    )(places, *operands)


def late_kernel(places, first, second, terms, hidden, early_t, _, tokens, left_t):
    here = 2 * lax.axis_index("tp") + lax.axis_index("dp")
    size = first.shape[0]
    count = places.shape[1]
    seen = []
    for index, piece in enumerate((first, second)):
        rows = pl.ds(pl.multiple_of(places[here, count - 2 + index] * size, size), size)
        tokens[rows, :] = piece[...]
        seen.append(hidden[rows, :])
    projected = fold2(nt(terms[...], jnp.concatenate([first[...], second[...]], axis=0)))
    stacked = jnp.concatenate(split2(projected), axis=0)
    left_t[...] = early_t[...] + fold2(nn(stacked, jnp.concatenate(seen, axis=0)))


def late_left(places, pieces, terms, hidden, early_t, tokens):
    operands = [*pieces, terms, hidden, early_t, tokens]
    return pl.pallas_call(
        late_kernel,
        in_specs=[pl.BlockSpec(memory_space=pltpu.SMEM)]
        + [pl.BlockSpec(memory_space=pltpu.VMEM)] * len(operands),
        out_specs=[pl.BlockSpec(memory_space=pltpu.VMEM)] * 2,
        out_shape=[
            jax.ShapeDtypeStruct(tokens.shape, BF16),
            jax.ShapeDtypeStruct(early_t.shape, F32),
        ],
        input_output_aliases={len(operands): 0},
        compiler_params=params(),
        cost_estimate=cost(1.0),
        name="late_left",
    )(places, *operands)


def core_of(place):
    return (place >> 1) & 1


def index_of(place):
    return (place >> 2) * 2 + (place & 1)


def place_of(core, index):
    return (index >> 1) * 4 + core * 2 + (index & 1)


def columns_of(place, cols):
    shard = lax.axis_index("tp") ^ place
    return pl.ds(pl.multiple_of(shard * cols, cols), cols)


def block_sum(lhs, rhs, feedback, tokens, core, index, cols):
    span = columns_of(place_of(core, index), cols)
    return fold2(nn(lhs[...], feedback[:, span]) + nn(rhs[...], tokens[:, span]))


def give_far_kernel(here_l, other_l, hidden_t, feedback, tokens, give, left_sum, lhs, rhs):
    left_t = here_l[...] + other_l[...]
    left_sum[...] = left_t
    lhs[...] = jnp.concatenate(split2(left_t), axis=0)
    seen_t = fold2(nn(lhs[...], hidden_t[...]))
    rhs[...] = jnp.concatenate(split2(seen_t), axis=0)
    other = 1 - lax.axis_index("dp")
    for index in range(give.shape[0]):
        give[index] = block_sum(lhs, rhs, feedback, tokens, other, index + 2, give.shape[2])


def given_far(here_l, other_l, hidden_t, feedback, tokens, chips):
    rank, rows = here_l.shape
    count, width = tokens.shape
    return pl.pallas_call(
        give_far_kernel,
        in_specs=[pl.BlockSpec(memory_space=pltpu.VMEM)] * 5,
        out_specs=[pl.BlockSpec(memory_space=pltpu.VMEM)] * 4,
        out_shape=[
            jax.ShapeDtypeStruct((chips // 2 - 2, rank, width // chips), F32),
            jax.ShapeDtypeStruct((rank, rows), F32),
            jax.ShapeDtypeStruct((2 * rank, rows), BF16),
            jax.ShapeDtypeStruct((2 * rank, count), BF16),
        ],
        compiler_params=params(),
        cost_estimate=cost(SMALL),
        name="given_far",
    )(here_l, other_l, hidden_t, feedback, tokens)


def keep_far_kernel(left_sum, lhs, rhs, feedback, tokens, keep, gram):
    core = lax.axis_index("dp")
    for index in range(keep.shape[0]):
        keep[index] = block_sum(lhs, rhs, feedback, tokens, core, index + 2, keep.shape[2])
    left_t = left_sum[...]
    gram[...] = lax.dot_general(
        left_t, left_t, (((1,), (1,)), ((), ())), precision=HIGHEST, preferred_element_type=F32
    )


def kept_far(left_sum, lhs, rhs, feedback, tokens, chips):
    rank = left_sum.shape[0]
    return pl.pallas_call(
        keep_far_kernel,
        in_specs=[pl.BlockSpec(memory_space=pltpu.VMEM)] * 5,
        out_specs=[pl.BlockSpec(memory_space=pltpu.VMEM)] * 2,
        out_shape=[
            jax.ShapeDtypeStruct((chips // 2 - 2, rank, tokens.shape[1] // chips), F32),
            jax.ShapeDtypeStruct((rank, rank), F32),
        ],
        compiler_params=params(),
        cost_estimate=cost(SMALL),
        name="kept_far",
    )(left_sum, lhs, rhs, feedback, tokens)


def near_kernel(lhs, rhs, feedback, tokens, give, keep):
    core = lax.axis_index("dp")
    for target, owner in ((give, 1 - core), (keep, core)):
        for index in range(2):
            target[index] = block_sum(lhs, rhs, feedback, tokens, owner, index, target.shape[2])


def near_terms(lhs, rhs, feedback, tokens, chips):
    block = jax.ShapeDtypeStruct((2, lhs.shape[0] // 2, tokens.shape[1] // chips), F32)
    return pl.pallas_call(
        near_kernel,
        in_specs=[pl.BlockSpec(memory_space=pltpu.VMEM)] * 4,
        out_specs=[pl.BlockSpec(memory_space=pltpu.VMEM)] * 2,
        out_shape=[block, block],
        compiler_params=params(),
        cost_estimate=cost(SMALL),
        name="near_terms",
    )(lhs, rhs, feedback, tokens)


def merged_kernel(hidden_t, feedback, tokens, merged):
    cols = tokens.shape[1] // STEPS
    for step in range(STEPS):
        span = slice(step * cols, (step + 1) * cols)
        merged[:, span] = nn(hidden_t[...], tokens[:, span]) + feedback[:, span].astype(F32)


def merged_sum(hidden_t, feedback, tokens):
    return pl.pallas_call(
        merged_kernel,
        in_specs=[pl.BlockSpec(memory_space=pltpu.VMEM)] * 3,
        out_specs=pl.BlockSpec(memory_space=pltpu.VMEM),
        out_shape=jax.ShapeDtypeStruct(feedback.shape, F32),
        compiler_params=params(),
        cost_estimate=cost(SMALL),
        name="merged",
    )(hidden_t, feedback, tokens)


def put_message(message, value, gram):
    rank = gram.shape[0]
    blocks = value.shape[1] // rank
    rows = rank // blocks
    message[:rank, :] = value
    for block in range(blocks):
        message[rank:, block * rank : (block + 1) * rank] = gram[block * rows : (block + 1) * rows, :]


def begin_kernel(keep, got, gram, *messages):
    core = lax.axis_index("dp")
    for pair, message in enumerate(messages):
        index = 2 * pair + core
        put_message(message, keep[index] + got[index], gram)


def begin_messages(keep, got, gram):
    rank, cols = keep.shape[1:]
    pairs = keep.shape[0] // 2
    rows = rank + rank // (cols // rank)
    return pl.pallas_call(
        begin_kernel,
        in_specs=[pl.BlockSpec(memory_space=pltpu.VMEM)] * 3,
        out_specs=[pl.BlockSpec(memory_space=pltpu.VMEM)] * pairs,
        out_shape=[jax.ShapeDtypeStruct((rows, cols), F32)] * pairs,
        compiler_params=params(),
        cost_estimate=cost(SMALL),
        name="begin_messages",
    )(keep, got, gram)


def rest_kernel(keep_far, got_far, keep, got, gram, own, beside, *messages):
    first = lax.axis_index("dp") == 0
    put_message(own, keep[0] + got[0], gram)
    put_message(beside, keep[1] + got[1], gram)
    for pair in range(len(messages) // 2):
        direct = keep_far[2 * pair + 1] + got_far[2 * pair + 1]
        crossing = keep_far[2 * pair] + got_far[2 * pair]
        if pair == 0:
            direct = jnp.where(first, direct, keep[0] + got[0])
            crossing = jnp.where(first, keep[1] + got[1], crossing)
        put_message(messages[2 * pair], direct, gram)
        put_message(messages[2 * pair + 1], crossing, gram)


def rest_messages(keep_far, got_far, keep, got, gram):
    rank, cols = keep.shape[1:]
    count = 2 + keep_far.shape[0]
    rows = rank + rank // (cols // rank)
    own, beside, *messages = pl.pallas_call(
        rest_kernel,
        in_specs=[pl.BlockSpec(memory_space=pltpu.VMEM)] * 5,
        out_specs=[pl.BlockSpec(memory_space=pltpu.VMEM)] * count,
        out_shape=[jax.ShapeDtypeStruct((rows, cols), F32)] * count,
        compiler_params=params(),
        cost_estimate=cost(SMALL),
        name="rest_messages",
    )(keep_far, got_far, keep, got, gram)
    return own, beside, messages[::2], messages[1::2]


def cross_kernel(message, passed, total):
    total[...] = message[...] + jnp.where(lax.axis_index("dp") == 0, 0.0, passed[...])


def crossing(message, passed):
    return pl.pallas_call(
        cross_kernel,
        in_specs=[pl.BlockSpec(memory_space=pltpu.VMEM)] * 2,
        out_specs=pl.BlockSpec(memory_space=pltpu.VMEM),
        out_shape=jax.ShapeDtypeStruct(message.shape, F32),
        compiler_params=params(),
        cost_estimate=cost(SMALL),
        name="crossing",
    )(message, passed)


def core_sum_kernel(own, third, *refs):
    messages, total = refs[:-1], refs[-1]
    pairs = len(messages) // 3
    begun, direct, crossed = messages[:pairs], messages[pairs : 2 * pairs], messages[2 * pairs :]
    first = lax.axis_index("dp") == 0
    parts = [jnp.where(first, own[...] + crossed[0][...], direct[0][...] + third[...])]
    for pair in range(pairs):
        parts.append(jnp.where(first, begun[pair][...] + direct[pair][...], crossed[pair][...]))
    while len(parts) > 1:
        parts = [a + b for a, b in zip(parts[::2], parts[1::2])]
    total[...] = parts[0]


def core_sum(own, third, begun, direct, crossed):
    operands = [own, third, *begun, *direct, *crossed]
    return pl.pallas_call(
        core_sum_kernel,
        in_specs=[pl.BlockSpec(memory_space=pltpu.VMEM)] * len(operands),
        out_specs=pl.BlockSpec(memory_space=pltpu.VMEM),
        out_shape=jax.ShapeDtypeStruct(own.shape, F32),
        compiler_params=params(),
        cost_estimate=cost(SMALL),
        name="core_sum",
    )(*operands)


def choose_kernel(here, there, chosen):
    chosen[...] = jnp.where(lax.axis_index("dp") == 0, here[...], there[...])


def by_core(here, there):
    return pl.pallas_call(
        choose_kernel,
        in_specs=[pl.BlockSpec(memory_space=pltpu.VMEM)] * 2,
        out_specs=pl.BlockSpec(memory_space=pltpu.VMEM),
        out_shape=jax.ShapeDtypeStruct(here.shape, F32),
        compiler_params=params(),
        cost_estimate=cost(SMALL),
        name="by_core",
    )(here, there)


def join_kernel(share, third, *refs):
    shares, mine = refs[:-1], refs[-1]
    pairs = len(shares) // 2
    begun, direct = shares[:pairs], shares[pairs:]
    first = lax.axis_index("dp") == 0
    mine[0] = jnp.where(first, share[...], direct[0][...])
    mine[1] = jnp.where(first, begun[0][...], third[...])
    for pair in range(pairs):
        mine[pair + 2] = jnp.where(first, direct[pair][...], begun[pair][...])


def joined(share, third, begun, direct):
    operands = [share, third, *begun, *direct]
    return pl.pallas_call(
        join_kernel,
        in_specs=[pl.BlockSpec(memory_space=pltpu.VMEM)] * len(operands),
        out_specs=pl.BlockSpec(memory_space=pltpu.VMEM),
        out_shape=jax.ShapeDtypeStruct((len(begun) + 2, *share.shape), F32),
        compiler_params=params(),
        cost_estimate=cost(SMALL),
        name="joined",
    )(*operands)


def chip_sum_kernel(here, other, share, gram):
    total = here[...] + other[...]
    rank, cols = share.shape
    blocks = cols // rank
    rows = rank // blocks
    share[...] = total[:rank]
    for block in range(blocks):
        gram[block * rows : (block + 1) * rows, :] = total[rank:, block * rank : (block + 1) * rank]


def chip_sum(here, other, rank):
    return pl.pallas_call(
        chip_sum_kernel,
        in_specs=[pl.BlockSpec(memory_space=pltpu.VMEM)] * 2,
        out_specs=[pl.BlockSpec(memory_space=pltpu.VMEM)] * 2,
        out_shape=[
            jax.ShapeDtypeStruct((rank, here.shape[1]), F32),
            jax.ShapeDtypeStruct((rank, rank), F32),
        ],
        compiler_params=params(),
        cost_estimate=cost(SMALL),
        name="chip_sum",
    )(here, other)


def inverse_kernel(gram, inverse):
    rank = gram.shape[0]
    row = lax.broadcasted_iota(jnp.int32, (rank, 2 * rank), 0)
    lane = lax.broadcasted_iota(jnp.int32, (rank, 2 * rank), 1)
    eye = (lane[:, rank:] == row[:, rank:] + rank).astype(F32)
    table = jnp.concatenate([gram[...], eye], axis=1)
    done = []
    for start in range(0, rank, PIVOTS):
        below = row[start:]
        each = range(PIVOTS)
        lines = [table[k : k + 1, :] for k in each]
        columns = [jnp.broadcast_to(table[:, start + k : start + k + 1], table.shape) for k in each]
        change = None
        for k in each:
            top = columns[k][k : k + 1, :]
            reciprocal = 1.0 / top
            factor = jnp.where(below > start + k, columns[k] * reciprocal, 0.0)
            for m in range(k + 1, PIVOTS):
                entry = columns[m][k : k + 1, :]
                lines[m] = lines[m] - (entry * reciprocal) * lines[k]
                columns[m] = columns[m] - factor * entry
            done.append(lines[k] * lax.rsqrt(top))
            part = factor * lines[k]
            change = part if change is None else change + part
        table = (table - change)[PIVOTS:]
    inverse[...] = jnp.concatenate(done, axis=0)[:, rank:]


def cholesky_inverse(gram):
    return pl.pallas_call(
        inverse_kernel,
        in_specs=[pl.BlockSpec(memory_space=pltpu.VMEM)],
        out_specs=pl.BlockSpec(memory_space=pltpu.VMEM),
        out_shape=jax.ShapeDtypeStruct(gram.shape, F32),
        compiler_params=params(),
        cost_estimate=cost(5.0),
        name="cholesky_inverse",
    )(gram)


def spread(target, rows, value):
    rank = value.shape[1]
    high, low = split2(value)
    for place, term in enumerate((high, high, low, low)):
        target[rows, place * rank : (place + 1) * rank] = term


def operand_kernel(replicas, inverse, left_sum, lhs):
    rank, rows = left_sum.shape
    orth_t = jnp.dot(inverse[...], left_sum[...], precision=HIGHEST, preferred_element_type=F32)
    share = inverse[...] * (1.0 / replicas)
    weight_t = lax.dot_general(
        share, orth_t, (((0,), (0,)), ((), ())), precision=HIGHEST, preferred_element_type=F32
    )
    spread(lhs, slice(0, rows), -weight_t.T)
    spread(lhs, slice(rows, rows + rank), share)


def last_operand(inverse, left_sum, replicas):
    rank, rows = left_sum.shape
    return pl.pallas_call(
        functools.partial(operand_kernel, replicas),
        in_specs=[pl.BlockSpec(memory_space=pltpu.VMEM)] * 2,
        out_specs=pl.BlockSpec(memory_space=pltpu.VMEM),
        out_shape=jax.ShapeDtypeStruct((rows + rank, 4 * rank), BF16),
        compiler_params=params(),
        cost_estimate=cost(SMALL),
        name="last_operand",
    )(inverse, left_sum)


def final_kernel(indices, side, shares, lhs, merged, *refs):
    out, factor, rhs, out_here, factor_here, sems = refs[-6:]
    owner = lax.axis_index("dp") ^ side
    rows = merged.shape[0]
    rank, cols = shares.shape[1:]
    copies = []
    for block, index in enumerate(indices):
        span = columns_of(place_of(owner, index), cols)
        high, low = split2(shares[block])
        for place, term in enumerate((high, low, high, low)):
            rhs[block % 2, place * rank : (place + 1) * rank, :] = term
        product = nn(lhs[...], rhs[block % 2])
        factor_here[block] = product[rows:]
        out_here[block] = (merged[:, span] + product[:rows]).astype(BF16)
        for number, (source, target) in enumerate(((out_here, out), (factor_here, factor))):
            copies.append(
                pltpu.make_async_copy(source.at[block], target.at[:, span], sems.at[block, number])
            )
            copies[-1].start()
    for copy in copies:
        copy.wait()


def finish(indices, shares, side, lhs, merged, begun=()):
    rank, cols = shares.shape[1:]
    rows, width = merged.shape
    blocks = len(indices)
    return pl.pallas_call(
        functools.partial(final_kernel, indices, side),
        in_specs=[pl.BlockSpec(memory_space=pltpu.VMEM)] * 3
        + [pl.BlockSpec(memory_space=pl.ANY)] * len(begun),
        out_specs=[pl.BlockSpec(memory_space=pl.ANY)] * 2,
        out_shape=[
            jax.ShapeDtypeStruct((rows, width), BF16),
            jax.ShapeDtypeStruct((rank, width), F32),
        ],
        input_output_aliases={3 + index: index for index in range(len(begun))},
        scratch_shapes=[
            pltpu.VMEM((2, lhs.shape[1], cols), BF16),
            pltpu.VMEM((blocks, rows, cols), BF16),
            pltpu.VMEM((blocks, rank, cols), F32),
            pltpu.SemaphoreType.DMA((blocks, 2)),
        ],
        compiler_params=params(),
        cost_estimate=cost(SMALL),
        name="finish",
    )(shares, lhs, merged, *begun)


def ring_order(chips):
    if chips == 8:
        return [0, 1, 3, 5, 7, 6, 4, 2]
    return list(range(chips))


def ring_gather(shard, chips, beside):
    order = ring_order(chips)
    position = {chip: place for place, chip in enumerate(order)}

    def pairs(way):
        steps = ((0, way), (1, -way))
        return [
            (2 * order[i] + core, 2 * order[(i + step) % chips] + core)
            for i in range(chips)
            for core, step in steps
        ]

    halves = halves_of(shard)
    pieces = list(halves)
    origin = [(0, 0), (0, 1)]
    far = chips // 2
    *later, beside = lax.optimization_barrier((*halves, beside))
    going = {(1, 0): halves[0], (-1, 1): halves[1], (1, 1): later[1], (-1, 0): later[0]}
    for hop in range(1, far + 1):
        for way, half in ((1, 0), (-1, 1), (1, 1), (-1, 0)):
            if hop == far and (half == 0) != (way == 1):
                continue
            going[way, half] = lax.ppermute(going[way, half], ("tp", "dp"), pairs(way))
            pieces.append(going[way, half])
            origin.append((-way * hop, half))
    places = np.zeros((2 * chips, len(pieces)), np.int32)
    for chip in range(chips):
        for core, sign in ((0, 1), (1, -1)):
            for index, (shift, half) in enumerate(origin):
                source = order[(position[chip] + sign * shift) % chips]
                places[2 * chip + core, index] = 2 * source + half
    return pieces, places, beside


def swap(value):
    return lax.ppermute(value, "dp", [(0, 1), (1, 0)])


def local(grad_out, hidden, feedback, right_factor):
    shard, residue = grad_out[0], feedback[0]
    hidden_t = hidden[0].T
    chips, replicas = lax.axis_size("tp"), lax.axis_size("dp")
    rank = right_factor.shape[0]

    def send(value, first, second):
        pairs = []
        for chip in range(chips):
            for core, place in enumerate((first, second)):
                if place:
                    pairs.append((2 * chip + core, 2 * (chip ^ place) + core))
        return lax.ppermute(value, ("tp", "dp"), pairs)

    pieces, places, (terms, residue_t) = ring_gather(shard, chips, residue_left(right_factor, residue))
    places = jnp.asarray(places)
    tokens, hidden_rows, left_t = early_left(places, pieces[:-2], terms, residue_t, hidden_t)
    tokens, left_t = late_left(places, pieces[-2:], terms, hidden_rows, left_t, tokens)
    give, left_sum, lhs, rhs = given_far(left_t, swap(left_t), hidden_t, residue, tokens, chips)
    got = swap(give)
    keep, gram = kept_far(left_sum, lhs, rhs, residue, tokens, chips)
    begin = begin_messages(keep, got, gram)
    give, keep_near = near_terms(lhs, rhs, residue, tokens, chips)
    own, beside, direct, cross = rest_messages(keep, got, keep_near, swap(give), gram)

    evens = range(4, chips, 4)
    begun = [send(value, place, 1) for value, place in zip(begin, evens)]
    direct = [send(value, place + 1, 2 * (place == 4)) for value, place in zip(direct, evens)]
    third = send(beside, 0, 3)
    cross = [crossing(value, passed) for value, passed in zip(cross, begun)]
    crossed = [send(value, int(place == 4), place + 2) for value, place in zip(cross, evens)]
    tokens, _ = lax.optimization_barrier((tokens, beside))
    merged = merged_sum(hidden_t, residue, tokens)
    third, merged = lax.optimization_barrier((third, merged))
    partial = core_sum(own, third, begun, direct, crossed)
    share, gram_matrix = chip_sum(partial, swap(partial), rank)

    begun = [send(share, int(place == 4), place + 2) for place in evens]
    direct = [send(share, place, 2 * (place == 4)) for place in evens]
    third = send(share, 0, 3)
    passed = [send(by_core(share, value), place + 1, 1) for value, place in zip(begun, evens)]
    inverse = cholesky_inverse(gram_matrix)
    inverse, begun, direct = lax.optimization_barrier((inverse, begun, direct))
    lhs = last_operand(inverse, left_sum, replicas)
    mine = joined(share, third, begun, direct)
    half = chips // 2
    begun = finish([0, 1, *range(2, half, 2)], mine, 0, lhs, merged)
    passed, begun = lax.optimization_barrier((passed, begun))
    rest = passed[0][None] if len(passed) == 1 else jnp.stack(passed)
    theirs = swap(jnp.concatenate([mine, rest]))
    begun = finish([*range(3, half, 2)], rest, 0, lhs, merged, begun)
    order = [0, 1, *range(2, half, 2), *range(3, half, 2)]
    new_feedback, new_factor = finish(order, theirs, 1, lhs, merged, begun)
    return new_feedback[None], new_factor


def solution(mesh):
    return jax.shard_map(
        local,
        mesh=mesh,
        in_specs=(
            P(("runs", "dp"), "tp", None),
            P(("runs", "dp"), None, "tp"),
            P(("runs", "dp"), "tp", None),
            P(),
        ),
        out_specs=(P(("runs", "dp"), "tp", None), P("runs", None)),
        check_vma=False,
    )
```

```python
import functools

import jax
import jax.numpy as jnp
from jax import lax
from jax.experimental import pallas as pl
from jax.experimental.pallas import tpu as pltpu
from jax.sharding import PartitionSpec as P

F32 = jnp.float32
BF16 = jnp.bfloat16
HIGHEST = lax.Precision.HIGHEST
VMEM_LIMIT = 24 * 1024 * 1024
STEPS = 4
SMALL = 0.05
PIVOTS = 8


def split2(value):
    high = value.astype(BF16)
    return high, (value - high.astype(F32)).astype(BF16)


def fold2(stacked):
    rank = stacked.shape[0] // 2
    return stacked[:rank] + stacked[rank:]


def nn(a, b):
    return lax.dot_general(a, b, (((1,), (0,)), ((), ())), preferred_element_type=F32)


def nt(a, b):
    return lax.dot_general(a, b, (((1,), (1,)), ((), ())), preferred_element_type=F32)


def params(semantics=None, limit=VMEM_LIMIT):
    return pltpu.CompilerParams(vmem_limit_bytes=limit, dimension_semantics=semantics)


def cost(microseconds):
    return pl.CostEstimate(flops=int(microseconds * 1.15e9), bytes_accessed=0, transcendentals=0)


def whole(shape):
    return pl.BlockSpec(shape, lambda *_: (0,) * len(shape))


def halves_kernel(shard, first, second):
    size = first.shape[0]
    first[...] = shard[:size, :]
    second[...] = shard[size:, :]


def halves_of(shard):
    half = jax.ShapeDtypeStruct((shard.shape[0] // 2, shard.shape[1]), BF16)
    return pl.pallas_call(
        halves_kernel,
        in_specs=[pl.BlockSpec(memory_space=pltpu.VMEM)],
        out_specs=[pl.BlockSpec(memory_space=pltpu.VMEM)] * 2,
        out_shape=[half, half],
        compiler_params=params(),
        cost_estimate=cost(4.0),
        name="halves",
    )(shard)


def relay_kernel(first, second, first_copy, second_copy):
    first_copy[...] = first[...]
    second_copy[...] = second[...]


def relayed(halves):
    return pl.pallas_call(
        relay_kernel,
        in_specs=[pl.BlockSpec(memory_space=pltpu.VMEM)] * 2,
        out_specs=[pl.BlockSpec(memory_space=pltpu.VMEM)] * 2,
        out_shape=[jax.ShapeDtypeStruct(half.shape, BF16) for half in halves],
        compiler_params=params(),
        cost_estimate=cost(2.2),
        name="relayed",
    )(*halves)


def residue_kernel(right, feedback, terms, left_t):
    cols = right.shape[1] // STEPS
    total = None
    for step in range(STEPS):
        span = slice(step * cols, (step + 1) * cols)
        stacked = jnp.concatenate(split2(right[:, span]), axis=0)
        terms[:, span] = stacked
        part = nt(stacked, feedback[:, span])
        total = part if total is None else total + part
    left_t[...] = fold2(total)


def residue_left(right, feedback):
    rank, width = right.shape
    rows = feedback.shape[0]
    return pl.pallas_call(
        residue_kernel,
        in_specs=[pl.BlockSpec(memory_space=pltpu.VMEM)] * 2,
        out_specs=[pl.BlockSpec(memory_space=pltpu.VMEM)] * 2,
        out_shape=[
            jax.ShapeDtypeStruct((2 * rank, width), BF16),
            jax.ShapeDtypeStruct((rank, rows), F32),
        ],
        compiler_params=params(),
        cost_estimate=cost(2.2),
        name="residue_left",
    )(right, feedback)


def ring_chip(position, chips):
    if chips != 8:
        return position
    up = jnp.where(position == 0, 0, 2 * position - 1)
    return jnp.where(position < 4, up, jnp.where(position == 4, 7, 2 * (8 - position)))


def ring_position(chip, chips):
    if chips != 8:
        return chip
    return jnp.where(chip % 2 == 1, (chip + 1) // 2, jnp.where(chip == 0, 0, 8 - chip // 2))


def piece_rows(origin, size):
    shift, half = origin
    chips = lax.axis_size("tp")
    sign = 1 - 2 * lax.axis_index("dp")
    position = ring_position(lax.axis_index("tp"), chips) + sign * shift + chips
    source = ring_chip(position % chips, chips)
    return pl.ds(pl.multiple_of((2 * source + half) * size, size), size)


def early_kernel(origins, *refs):
    pieces, (terms, residue_t, hidden_t, tokens, hidden, left_t) = refs[:-6], refs[-6:]
    size = pieces[0].shape[0]
    for index, origin in enumerate(origins):
        rows = piece_rows(origin, size)
        if index < len(pieces):
            tokens[rows, :] = pieces[index][...]
        else:
            tokens[rows, :] = jnp.zeros((size, tokens.shape[1]), BF16)
    projected = fold2(nt(terms[...], tokens[...]))
    stacked = jnp.concatenate(split2(projected), axis=0)
    left_t[...] = residue_t[...] + fold2(nt(stacked, hidden_t[...]))
    hidden[...] = hidden_t[...].T


def early_left(origins, pieces, terms, residue_t, hidden_t):
    rows, count = hidden_t.shape
    width = terms.shape[1]
    operands = [*pieces, terms, residue_t, hidden_t]
    return pl.pallas_call(
        functools.partial(early_kernel, origins),
        in_specs=[pl.BlockSpec(memory_space=pltpu.VMEM)] * len(operands),
        out_specs=[pl.BlockSpec(memory_space=pltpu.VMEM)] * 3,
        out_shape=[
            jax.ShapeDtypeStruct((count, width), BF16),
            jax.ShapeDtypeStruct((count, rows), BF16),
            jax.ShapeDtypeStruct(residue_t.shape, F32),
        ],
        compiler_params=params(),
        cost_estimate=cost(2.0),
        name="early_left",
    )(*operands)


def late_kernel(origins, first, second, terms, hidden, early_t, _, tokens, left_t):
    size = first.shape[0]
    seen = []
    for origin, piece in zip(origins, (first, second)):
        rows = piece_rows(origin, size)
        tokens[rows, :] = piece[...]
        seen.append(hidden[rows, :])
    projected = fold2(nt(terms[...], jnp.concatenate([first[...], second[...]], axis=0)))
    stacked = jnp.concatenate(split2(projected), axis=0)
    left_t[...] = early_t[...] + fold2(nn(stacked, jnp.concatenate(seen, axis=0)))


def late_left(origins, pieces, terms, hidden, early_t, tokens):
    operands = [*pieces, terms, hidden, early_t, tokens]
    return pl.pallas_call(
        functools.partial(late_kernel, origins),
        in_specs=[pl.BlockSpec(memory_space=pltpu.VMEM)] * len(operands),
        out_specs=[pl.BlockSpec(memory_space=pltpu.VMEM)] * 2,
        out_shape=[
            jax.ShapeDtypeStruct(tokens.shape, BF16),
            jax.ShapeDtypeStruct(early_t.shape, F32),
        ],
        input_output_aliases={len(operands) - 1: 0},
        compiler_params=params(),
        cost_estimate=cost(1.0),
        name="late_left",
    )(*operands)


def core_of(place):
    return (place >> 1) & 1


def index_of(place):
    return (place >> 2) * 2 + (place & 1)


def place_of(core, index):
    return (index >> 1) * 4 + core * 2 + (index & 1)


def columns_of(place, cols):
    shard = lax.axis_index("tp") ^ place
    return pl.ds(pl.multiple_of(shard * cols, cols), cols)


def block_sum(lhs, rhs, feedback, tokens, core, index, cols):
    span = columns_of(place_of(core, index), cols)
    return fold2(nn(lhs[...], feedback[:, span]) + nn(rhs[...], tokens[:, span]))


def give_far_kernel(here_l, other_l, hidden_t, feedback, tokens, give, left_sum, lhs, rhs):
    left_t = here_l[...] + other_l[...]
    left_sum[...] = left_t
    lhs[...] = jnp.concatenate(split2(left_t), axis=0)
    seen_t = fold2(nn(lhs[...], hidden_t[...]))
    rhs[...] = jnp.concatenate(split2(seen_t), axis=0)
    other = 1 - lax.axis_index("dp")
    for index in range(give.shape[0]):
        give[index] = block_sum(lhs, rhs, feedback, tokens, other, index + 2, give.shape[2])


def given_far(here_l, other_l, hidden_t, feedback, tokens, chips):
    rank, rows = here_l.shape
    count, width = tokens.shape
    return pl.pallas_call(
        give_far_kernel,
        in_specs=[pl.BlockSpec(memory_space=pltpu.VMEM)] * 5,
        out_specs=[pl.BlockSpec(memory_space=pltpu.VMEM)] * 4,
        out_shape=[
            jax.ShapeDtypeStruct((chips // 2 - 2, rank, width // chips), F32),
            jax.ShapeDtypeStruct((rank, rows), F32),
            jax.ShapeDtypeStruct((2 * rank, rows), BF16),
            jax.ShapeDtypeStruct((2 * rank, count), BF16),
        ],
        compiler_params=params(),
        cost_estimate=cost(SMALL),
        name="given_far",
    )(here_l, other_l, hidden_t, feedback, tokens)


def keep_far_kernel(left_sum, lhs, rhs, feedback, tokens, keep, gram):
    core = lax.axis_index("dp")
    for index in range(keep.shape[0]):
        keep[index] = block_sum(lhs, rhs, feedback, tokens, core, index + 2, keep.shape[2])
    left_t = left_sum[...]
    gram[...] = lax.dot_general(
        left_t, left_t, (((1,), (1,)), ((), ())), precision=HIGHEST, preferred_element_type=F32
    )


def kept_far(left_sum, lhs, rhs, feedback, tokens, chips):
    rank = left_sum.shape[0]
    return pl.pallas_call(
        keep_far_kernel,
        in_specs=[pl.BlockSpec(memory_space=pltpu.VMEM)] * 5,
        out_specs=[pl.BlockSpec(memory_space=pltpu.VMEM)] * 2,
        out_shape=[
            jax.ShapeDtypeStruct((chips // 2 - 2, rank, tokens.shape[1] // chips), F32),
            jax.ShapeDtypeStruct((rank, rank), F32),
        ],
        compiler_params=params(),
        cost_estimate=cost(SMALL),
        name="kept_far",
    )(left_sum, lhs, rhs, feedback, tokens)


def near_kernel(lhs, rhs, feedback, tokens, give, keep):
    core = lax.axis_index("dp")
    for target, owner in ((give, 1 - core), (keep, core)):
        for index in range(2):
            target[index] = block_sum(lhs, rhs, feedback, tokens, owner, index, target.shape[2])


def near_terms(lhs, rhs, feedback, tokens, chips):
    block = jax.ShapeDtypeStruct((2, lhs.shape[0] // 2, tokens.shape[1] // chips), F32)
    return pl.pallas_call(
        near_kernel,
        in_specs=[pl.BlockSpec(memory_space=pltpu.VMEM)] * 4,
        out_specs=[pl.BlockSpec(memory_space=pltpu.VMEM)] * 2,
        out_shape=[block, block],
        compiler_params=params(),
        cost_estimate=cost(SMALL),
        name="near_terms",
    )(lhs, rhs, feedback, tokens)


def merged_kernel(hidden_t, feedback, tokens, merged):
    cols = tokens.shape[1] // STEPS
    for step in range(STEPS):
        span = slice(step * cols, (step + 1) * cols)
        merged[:, span] = nn(hidden_t[...], tokens[:, span]) + feedback[:, span].astype(F32)


def merged_sum(hidden_t, feedback, tokens):
    return pl.pallas_call(
        merged_kernel,
        in_specs=[pl.BlockSpec(memory_space=pltpu.VMEM)] * 3,
        out_specs=pl.BlockSpec(memory_space=pltpu.VMEM),
        out_shape=jax.ShapeDtypeStruct(feedback.shape, F32),
        compiler_params=params(),
        cost_estimate=cost(SMALL),
        name="merged",
    )(hidden_t, feedback, tokens)


def put_message(message, value, gram):
    rank = gram.shape[0]
    blocks = value.shape[1] // rank
    rows = rank // blocks
    message[:rank, :] = value
    for block in range(blocks):
        message[rank:, block * rank : (block + 1) * rank] = gram[block * rows : (block + 1) * rows, :]


def begin_kernel(keep, got, gram, *messages):
    core = lax.axis_index("dp")
    for pair, message in enumerate(messages):
        index = 2 * pair + core
        put_message(message, keep[index] + got[index], gram)


def begin_messages(keep, got, gram):
    rank, cols = keep.shape[1:]
    pairs = keep.shape[0] // 2
    rows = rank + rank // (cols // rank)
    return pl.pallas_call(
        begin_kernel,
        in_specs=[pl.BlockSpec(memory_space=pltpu.VMEM)] * 3,
        out_specs=[pl.BlockSpec(memory_space=pltpu.VMEM)] * pairs,
        out_shape=[jax.ShapeDtypeStruct((rows, cols), F32)] * pairs,
        compiler_params=params(),
        cost_estimate=cost(SMALL),
        name="begin_messages",
    )(keep, got, gram)


def rest_kernel(keep_far, got_far, keep, got, gram, own, beside, *messages):
    first = lax.axis_index("dp") == 0
    put_message(own, keep[0] + got[0], gram)
    put_message(beside, keep[1] + got[1], gram)
    for pair in range(len(messages) // 2):
        direct = keep_far[2 * pair + 1] + got_far[2 * pair + 1]
        crossing = keep_far[2 * pair] + got_far[2 * pair]
        if pair == 0:
            direct = jnp.where(first, direct, keep[0] + got[0])
            crossing = jnp.where(first, keep[1] + got[1], crossing)
        put_message(messages[2 * pair], direct, gram)
        put_message(messages[2 * pair + 1], crossing, gram)


def rest_messages(keep_far, got_far, keep, got, gram):
    rank, cols = keep.shape[1:]
    count = 2 + keep_far.shape[0]
    rows = rank + rank // (cols // rank)
    own, beside, *messages = pl.pallas_call(
        rest_kernel,
        in_specs=[pl.BlockSpec(memory_space=pltpu.VMEM)] * 5,
        out_specs=[pl.BlockSpec(memory_space=pltpu.VMEM)] * count,
        out_shape=[jax.ShapeDtypeStruct((rows, cols), F32)] * count,
        compiler_params=params(),
        cost_estimate=cost(SMALL),
        name="rest_messages",
    )(keep_far, got_far, keep, got, gram)
    return own, beside, messages[::2], messages[1::2]


def cross_kernel(message, passed, total):
    total[...] = message[...] + jnp.where(lax.axis_index("dp") == 0, 0.0, passed[...])


def crossing(message, passed):
    return pl.pallas_call(
        cross_kernel,
        in_specs=[pl.BlockSpec(memory_space=pltpu.VMEM)] * 2,
        out_specs=pl.BlockSpec(memory_space=pltpu.VMEM),
        out_shape=jax.ShapeDtypeStruct(message.shape, F32),
        compiler_params=params(),
        cost_estimate=cost(SMALL),
        name="crossing",
    )(message, passed)


def core_sum_kernel(own, third, *refs):
    messages, total = refs[:-1], refs[-1]
    pairs = len(messages) // 3
    begun, direct, crossed = messages[:pairs], messages[pairs : 2 * pairs], messages[2 * pairs :]
    first = lax.axis_index("dp") == 0
    parts = [jnp.where(first, own[...] + crossed[0][...], direct[0][...] + third[...])]
    for pair in range(pairs):
        parts.append(jnp.where(first, begun[pair][...] + direct[pair][...], crossed[pair][...]))
    while len(parts) > 1:
        parts = [a + b for a, b in zip(parts[::2], parts[1::2])]
    total[...] = parts[0]


def core_sum(own, third, begun, direct, crossed):
    operands = [own, third, *begun, *direct, *crossed]
    return pl.pallas_call(
        core_sum_kernel,
        in_specs=[pl.BlockSpec(memory_space=pltpu.VMEM)] * len(operands),
        out_specs=pl.BlockSpec(memory_space=pltpu.VMEM),
        out_shape=jax.ShapeDtypeStruct(own.shape, F32),
        compiler_params=params(),
        cost_estimate=cost(SMALL),
        name="core_sum",
    )(*operands)


def choose_kernel(here, there, chosen):
    chosen[...] = jnp.where(lax.axis_index("dp") == 0, here[...], there[...])


def by_core(here, there):
    return pl.pallas_call(
        choose_kernel,
        in_specs=[pl.BlockSpec(memory_space=pltpu.VMEM)] * 2,
        out_specs=pl.BlockSpec(memory_space=pltpu.VMEM),
        out_shape=jax.ShapeDtypeStruct(here.shape, F32),
        compiler_params=params(),
        cost_estimate=cost(SMALL),
        name="by_core",
    )(here, there)


def join_kernel(share, third, *refs):
    shares, mine = refs[:-1], refs[-1]
    pairs = len(shares) // 2
    begun, direct = shares[:pairs], shares[pairs:]
    first = lax.axis_index("dp") == 0
    mine[0] = jnp.where(first, share[...], direct[0][...])
    mine[1] = jnp.where(first, begun[0][...], third[...])
    for pair in range(pairs):
        mine[pair + 2] = jnp.where(first, direct[pair][...], begun[pair][...])


def joined(share, third, begun, direct):
    operands = [share, third, *begun, *direct]
    return pl.pallas_call(
        join_kernel,
        in_specs=[pl.BlockSpec(memory_space=pltpu.VMEM)] * len(operands),
        out_specs=pl.BlockSpec(memory_space=pltpu.VMEM),
        out_shape=jax.ShapeDtypeStruct((len(begun) + 2, *share.shape), F32),
        compiler_params=params(),
        cost_estimate=cost(SMALL),
        name="joined",
    )(*operands)


def chip_sum_kernel(here, other, share, gram):
    total = here[...] + other[...]
    rank, cols = share.shape
    blocks = cols // rank
    rows = rank // blocks
    share[...] = total[:rank]
    for block in range(blocks):
        gram[block * rows : (block + 1) * rows, :] = total[rank:, block * rank : (block + 1) * rank]


def chip_sum(here, other, rank):
    return pl.pallas_call(
        chip_sum_kernel,
        in_specs=[pl.BlockSpec(memory_space=pltpu.VMEM)] * 2,
        out_specs=[pl.BlockSpec(memory_space=pltpu.VMEM)] * 2,
        out_shape=[
            jax.ShapeDtypeStruct((rank, here.shape[1]), F32),
            jax.ShapeDtypeStruct((rank, rank), F32),
        ],
        compiler_params=params(),
        cost_estimate=cost(SMALL),
        name="chip_sum",
    )(here, other)


def inverse_kernel(gram, inverse):
    rank = gram.shape[0]
    row = lax.broadcasted_iota(jnp.int32, (rank, 2 * rank), 0)
    lane = lax.broadcasted_iota(jnp.int32, (rank, 2 * rank), 1)
    eye = (lane[:, rank:] == row[:, rank:] + rank).astype(F32)
    table = jnp.concatenate([gram[...], eye], axis=1)
    done = []
    for start in range(0, rank, PIVOTS):
        below = row[start:]
        each = range(PIVOTS)
        lines = [table[k : k + 1, :] for k in each]
        columns = [jnp.broadcast_to(table[:, start + k : start + k + 1], table.shape) for k in each]
        change = None
        for k in each:
            top = columns[k][k : k + 1, :]
            reciprocal = 1.0 / top
            factor = jnp.where(below > start + k, columns[k] * reciprocal, 0.0)
            for m in range(k + 1, PIVOTS):
                entry = columns[m][k : k + 1, :]
                lines[m] = lines[m] - (entry * reciprocal) * lines[k]
                columns[m] = columns[m] - factor * entry
            done.append(lines[k] * lax.rsqrt(top))
            part = factor * lines[k]
            change = part if change is None else change + part
        table = (table - change)[PIVOTS:]
    inverse[...] = jnp.concatenate(done, axis=0)[:, rank:]


def cholesky_inverse(gram):
    return pl.pallas_call(
        inverse_kernel,
        in_specs=[pl.BlockSpec(memory_space=pltpu.VMEM)],
        out_specs=pl.BlockSpec(memory_space=pltpu.VMEM),
        out_shape=jax.ShapeDtypeStruct(gram.shape, F32),
        compiler_params=params(),
        cost_estimate=cost(5.0),
        name="cholesky_inverse",
    )(gram)


def spread(target, rows, value):
    rank = value.shape[1]
    high, low = split2(value)
    for place, term in enumerate((high, high, low, low)):
        target[rows, place * rank : (place + 1) * rank] = term


def operand_kernel(replicas, inverse, left_sum, lhs):
    rank, rows = left_sum.shape
    orth_t = jnp.dot(inverse[...], left_sum[...], precision=HIGHEST, preferred_element_type=F32)
    share = inverse[...] * (1.0 / replicas)
    weight_t = lax.dot_general(
        share, orth_t, (((0,), (0,)), ((), ())), precision=HIGHEST, preferred_element_type=F32
    )
    spread(lhs, slice(0, rows), -weight_t.T)
    spread(lhs, slice(rows, rows + rank), share)


def last_operand(inverse, left_sum, replicas):
    rank, rows = left_sum.shape
    return pl.pallas_call(
        functools.partial(operand_kernel, replicas),
        in_specs=[pl.BlockSpec(memory_space=pltpu.VMEM)] * 2,
        out_specs=pl.BlockSpec(memory_space=pltpu.VMEM),
        out_shape=jax.ShapeDtypeStruct((rows + rank, 4 * rank), BF16),
        compiler_params=params(),
        cost_estimate=cost(SMALL),
        name="last_operand",
    )(inverse, left_sum)


def final_kernel(indices, side, shares, lhs, merged, *refs):
    out, factor, rhs, out_here, factor_here, sems = refs[-6:]
    owner = lax.axis_index("dp") ^ side
    rows = merged.shape[0]
    rank, cols = shares.shape[1:]
    copies = []
    for block, index in enumerate(indices):
        span = columns_of(place_of(owner, index), cols)
        high, low = split2(shares[block])
        for place, term in enumerate((high, low, high, low)):
            rhs[block % 2, place * rank : (place + 1) * rank, :] = term
        product = nn(lhs[...], rhs[block % 2])
        factor_here[block] = product[rows:]
        out_here[block] = (merged[:, span] + product[:rows]).astype(BF16)
        for number, (source, target) in enumerate(((out_here, out), (factor_here, factor))):
            copies.append(
                pltpu.make_async_copy(source.at[block], target.at[:, span], sems.at[block, number])
            )
            copies[-1].start()
    for copy in copies:
        copy.wait()


def finish(indices, shares, side, lhs, merged, begun=()):
    rank, cols = shares.shape[1:]
    rows, width = merged.shape
    blocks = len(indices)
    return pl.pallas_call(
        functools.partial(final_kernel, indices, side),
        in_specs=[pl.BlockSpec(memory_space=pltpu.VMEM)] * 3
        + [pl.BlockSpec(memory_space=pl.ANY)] * len(begun),
        out_specs=[pl.BlockSpec(memory_space=pl.ANY)] * 2,
        out_shape=[
            jax.ShapeDtypeStruct((rows, width), BF16),
            jax.ShapeDtypeStruct((rank, width), F32),
        ],
        input_output_aliases={3 + index: index for index in range(len(begun))},
        scratch_shapes=[
            pltpu.VMEM((2, lhs.shape[1], cols), BF16),
            pltpu.VMEM((blocks, rows, cols), BF16),
            pltpu.VMEM((blocks, rank, cols), F32),
            pltpu.SemaphoreType.DMA((blocks, 2)),
        ],
        compiler_params=params(),
        cost_estimate=cost(SMALL),
        name="finish",
    )(shares, lhs, merged, *begun)


def ring_order(chips):
    if chips == 8:
        return [0, 1, 3, 5, 7, 6, 4, 2]
    return list(range(chips))


def ring_gather(shard, chips, right_factor):
    order = ring_order(chips)

    def pairs(way):
        steps = ((0, way), (1, -way))
        return [
            (2 * order[i] + core, 2 * order[(i + step) % chips] + core)
            for i in range(chips)
            for core, step in steps
        ]

    halves = halves_of(shard)
    pieces = list(halves)
    origin = [(0, 0), (0, 1)]
    far = chips // 2
    later = relayed(halves)
    going = {(1, 0): halves[0], (-1, 1): halves[1], (1, 1): later[1], (-1, 0): later[0]}
    for hop in range(1, far + 1):
        for way, half in ((1, 0), (-1, 1), (1, 1), (-1, 0)):
            if hop == far and (half == 0) != (way == 1):
                continue
            going[way, half] = lax.ppermute(going[way, half], ("tp", "dp"), pairs(way))
            pieces.append(going[way, half])
            origin.append((-way * hop, half))
        if hop == far - 1:
            going[1, 0], right_factor = lax.optimization_barrier((going[1, 0], right_factor))
    return pieces, origin, right_factor


def swap(value):
    return lax.ppermute(value, "dp", [(0, 1), (1, 0)])


def local(grad_out, hidden, feedback, right_factor):
    shard, residue = grad_out[0], feedback[0]
    hidden_t = hidden[0].T
    chips, replicas = lax.axis_size("tp"), lax.axis_size("dp")
    rank = right_factor.shape[0]

    def send(value, first, second):
        pairs = []
        for chip in range(chips):
            for core, place in enumerate((first, second)):
                if place:
                    pairs.append((2 * chip + core, 2 * (chip ^ place) + core))
        return lax.ppermute(value, ("tp", "dp"), pairs)

    pieces, origins, right_factor = ring_gather(shard, chips, right_factor)
    terms, residue_t = residue_left(right_factor, residue)
    tokens, hidden_rows, left_t = early_left(origins, pieces[:-2], terms, residue_t, hidden_t)
    tokens, left_t = late_left(origins[-2:], pieces[-2:], terms, hidden_rows, left_t, tokens)
    give, left_sum, lhs, rhs = given_far(left_t, swap(left_t), hidden_t, residue, tokens, chips)
    got = swap(give)
    keep, gram = kept_far(left_sum, lhs, rhs, residue, tokens, chips)
    begin = begin_messages(keep, got, gram)
    give, keep_near = near_terms(lhs, rhs, residue, tokens, chips)
    own, beside, direct, cross = rest_messages(keep, got, keep_near, swap(give), gram)

    evens = range(4, chips, 4)
    begun = [send(value, place, 1) for value, place in zip(begin, evens)]
    direct = [send(value, place + 1, 2 * (place == 4)) for value, place in zip(direct, evens)]
    third = send(beside, 0, 3)
    cross = [crossing(value, passed) for value, passed in zip(cross, begun)]
    crossed = [send(value, int(place == 4), place + 2) for value, place in zip(cross, evens)]
    tokens, _ = lax.optimization_barrier((tokens, beside))
    merged = merged_sum(hidden_t, residue, tokens)
    third, merged = lax.optimization_barrier((third, merged))
    partial = core_sum(own, third, begun, direct, crossed)
    share, gram_matrix = chip_sum(partial, swap(partial), rank)

    begun = [send(share, int(place == 4), place + 2) for place in evens]
    direct = [send(share, place, 2 * (place == 4)) for place in evens]
    third = send(share, 0, 3)
    passed = [send(by_core(share, value), place + 1, 1) for value, place in zip(begun, evens)]
    inverse = cholesky_inverse(gram_matrix)
    inverse, begun, direct = lax.optimization_barrier((inverse, begun, direct))
    lhs = last_operand(inverse, left_sum, replicas)
    mine = joined(share, third, begun, direct)
    half = chips // 2
    begun = finish([0, 1, *range(2, half, 2)], mine, 0, lhs, merged)
    passed, begun = lax.optimization_barrier((passed, begun))
    rest = passed[0][None] if len(passed) == 1 else jnp.stack(passed)
    theirs = swap(jnp.concatenate([mine, rest]))
    begun = finish([*range(3, half, 2)], rest, 0, lhs, merged, begun)
    order = [0, 1, *range(2, half, 2), *range(3, half, 2)]
    new_feedback, new_factor = finish(order, theirs, 1, lhs, merged, begun)
    return new_feedback[None], new_factor


def solution(mesh):
    return jax.shard_map(
        local,
        mesh=mesh,
        in_specs=(
            P(("runs", "dp"), "tp", None),
            P(("runs", "dp"), None, "tp"),
            P(("runs", "dp"), "tp", None),
            P(),
        ),
        out_specs=(P(("runs", "dp"), "tp", None), P("runs", None)),
        check_vma=False,
    )
```

```python
import functools

import jax
import jax.numpy as jnp
from jax import lax
from jax.experimental import pallas as pl
from jax.experimental.pallas import tpu as pltpu
from jax.sharding import PartitionSpec as P

F32 = jnp.float32
BF16 = jnp.bfloat16
HIGHEST = lax.Precision.HIGHEST
VMEM_LIMIT = 24 * 1024 * 1024
STEPS = 4
SMALL = 0.05
PIVOTS = 8


def split2(value):
    high = value.astype(BF16)
    return high, (value - high.astype(F32)).astype(BF16)


def fold2(stacked):
    rank = stacked.shape[0] // 2
    return stacked[:rank] + stacked[rank:]


def nn(a, b):
    return lax.dot_general(a, b, (((1,), (0,)), ((), ())), preferred_element_type=F32)


def nt(a, b):
    return lax.dot_general(a, b, (((1,), (1,)), ((), ())), preferred_element_type=F32)


def params(semantics=None, limit=VMEM_LIMIT):
    return pltpu.CompilerParams(vmem_limit_bytes=limit, dimension_semantics=semantics)


def cost(microseconds):
    return pl.CostEstimate(flops=int(microseconds * 1.15e9), bytes_accessed=0, transcendentals=0)


def whole(shape):
    return pl.BlockSpec(shape, lambda *_: (0,) * len(shape))


def halves_kernel(shard, first, second):
    size = first.shape[0]
    first[...] = shard[:size, :]
    second[...] = shard[size:, :]


def halves_of(shard):
    half = jax.ShapeDtypeStruct((shard.shape[0] // 2, shard.shape[1]), BF16)
    return pl.pallas_call(
        halves_kernel,
        in_specs=[pl.BlockSpec(memory_space=pltpu.VMEM)],
        out_specs=[pl.BlockSpec(memory_space=pltpu.VMEM)] * 2,
        out_shape=[half, half],
        compiler_params=params(),
        cost_estimate=cost(4.0),
        name="halves",
    )(shard)


def relay_kernel(first, second, first_copy, second_copy):
    first_copy[...] = first[...]
    second_copy[...] = second[...]


def relayed(halves):
    return pl.pallas_call(
        relay_kernel,
        in_specs=[pl.BlockSpec(memory_space=pltpu.VMEM)] * 2,
        out_specs=[pl.BlockSpec(memory_space=pltpu.VMEM)] * 2,
        out_shape=[jax.ShapeDtypeStruct(half.shape, BF16) for half in halves],
        compiler_params=params(),
        cost_estimate=cost(2.2),
        name="relayed",
    )(*halves)


def residue_kernel(right, feedback, terms, left_t):
    cols = right.shape[1] // STEPS
    total = None
    for step in range(STEPS):
        span = slice(step * cols, (step + 1) * cols)
        stacked = jnp.concatenate(split2(right[:, span]), axis=0)
        terms[:, span] = stacked
        part = nt(stacked, feedback[:, span])
        total = part if total is None else total + part
    left_t[...] = fold2(total)


def residue_left(right, feedback):
    rank, width = right.shape
    rows = feedback.shape[0]
    return pl.pallas_call(
        residue_kernel,
        in_specs=[pl.BlockSpec(memory_space=pltpu.VMEM)] * 2,
        out_specs=[pl.BlockSpec(memory_space=pltpu.VMEM)] * 2,
        out_shape=[
            jax.ShapeDtypeStruct((2 * rank, width), BF16),
            jax.ShapeDtypeStruct((rank, rows), F32),
        ],
        compiler_params=params(),
        cost_estimate=cost(2.2),
        name="residue_left",
    )(right, feedback)


def ring_chip(position, chips):
    if chips != 8:
        return position
    up = jnp.where(position == 0, 0, 2 * position - 1)
    return jnp.where(position < 4, up, jnp.where(position == 4, 7, 2 * (8 - position)))


def ring_position(chip, chips):
    if chips != 8:
        return chip
    return jnp.where(chip % 2 == 1, (chip + 1) // 2, jnp.where(chip == 0, 0, 8 - chip // 2))


def piece_rows(origin, size):
    shift, half = origin
    chips = lax.axis_size("tp")
    sign = 1 - 2 * lax.axis_index("dp")
    position = ring_position(lax.axis_index("tp"), chips) + sign * shift + chips
    source = ring_chip(position % chips, chips)
    return pl.ds(pl.multiple_of((2 * source + half) * size, size), size)


def early_kernel(origins, *refs):
    pieces, (terms, residue_t, hidden_t, tokens, hidden, left_t) = refs[:-6], refs[-6:]
    size = pieces[0].shape[0]
    for index, origin in enumerate(origins):
        rows = piece_rows(origin, size)
        if index < len(pieces):
            tokens[rows, :] = pieces[index][...]
        else:
            tokens[rows, :] = jnp.zeros((size, tokens.shape[1]), BF16)
    projected = fold2(nt(terms[...], tokens[...]))
    stacked = jnp.concatenate(split2(projected), axis=0)
    left_t[...] = residue_t[...] + fold2(nt(stacked, hidden_t[...]))
    hidden[...] = hidden_t[...].T


def early_left(origins, pieces, terms, residue_t, hidden_t):
    rows, count = hidden_t.shape
    width = terms.shape[1]
    operands = [*pieces, terms, residue_t, hidden_t]
    return pl.pallas_call(
        functools.partial(early_kernel, origins),
        in_specs=[pl.BlockSpec(memory_space=pltpu.VMEM)] * len(operands),
        out_specs=[pl.BlockSpec(memory_space=pltpu.VMEM)] * 3,
        out_shape=[
            jax.ShapeDtypeStruct((count, width), BF16),
            jax.ShapeDtypeStruct((count, rows), BF16),
            jax.ShapeDtypeStruct(residue_t.shape, F32),
        ],
        compiler_params=params(),
        cost_estimate=cost(2.0),
        name="early_left",
    )(*operands)


def late_kernel(origins, first, second, terms, hidden, early_t, _, tokens, left_t):
    size = first.shape[0]
    seen = []
    for origin, piece in zip(origins, (first, second)):
        rows = piece_rows(origin, size)
        tokens[rows, :] = piece[...]
        seen.append(hidden[rows, :])
    projected = fold2(nt(terms[...], jnp.concatenate([first[...], second[...]], axis=0)))
    stacked = jnp.concatenate(split2(projected), axis=0)
    left_t[...] = early_t[...] + fold2(nn(stacked, jnp.concatenate(seen, axis=0)))


def late_left(origins, pieces, terms, hidden, early_t, tokens):
    operands = [*pieces, terms, hidden, early_t, tokens]
    return pl.pallas_call(
        functools.partial(late_kernel, origins),
        in_specs=[pl.BlockSpec(memory_space=pltpu.VMEM)] * len(operands),
        out_specs=[pl.BlockSpec(memory_space=pltpu.VMEM)] * 2,
        out_shape=[
            jax.ShapeDtypeStruct(tokens.shape, BF16),
            jax.ShapeDtypeStruct(early_t.shape, F32),
        ],
        input_output_aliases={len(operands) - 1: 0},
        compiler_params=params(),
        cost_estimate=cost(1.0),
        name="late_left",
    )(*operands)


def core_of(place):
    return (place >> 1) & 1


def index_of(place):
    return (place >> 2) * 2 + (place & 1)


def place_of(core, index):
    return (index >> 1) * 4 + core * 2 + (index & 1)


def columns_of(place, cols):
    shard = lax.axis_index("tp") ^ place
    return pl.ds(pl.multiple_of(shard * cols, cols), cols)


def block_sum(lhs, rhs, feedback, tokens, core, index, cols):
    span = columns_of(place_of(core, index), cols)
    return fold2(nn(lhs[...], feedback[:, span]) + nn(rhs[...], tokens[:, span]))


def give_far_kernel(here_l, other_l, hidden_t, feedback, tokens, give, left_sum, lhs, rhs):
    left_t = here_l[...] + other_l[...]
    left_sum[...] = left_t
    lhs[...] = jnp.concatenate(split2(left_t), axis=0)
    seen_t = fold2(nn(lhs[...], hidden_t[...]))
    rhs[...] = jnp.concatenate(split2(seen_t), axis=0)
    other = 1 - lax.axis_index("dp")
    for index in range(give.shape[0]):
        give[index] = block_sum(lhs, rhs, feedback, tokens, other, index + 2, give.shape[2])


def given_far(here_l, other_l, hidden_t, feedback, tokens, chips):
    rank, rows = here_l.shape
    count, width = tokens.shape
    return pl.pallas_call(
        give_far_kernel,
        in_specs=[pl.BlockSpec(memory_space=pltpu.VMEM)] * 5,
        out_specs=[pl.BlockSpec(memory_space=pltpu.VMEM)] * 4,
        out_shape=[
            jax.ShapeDtypeStruct((chips // 2 - 2, rank, width // chips), F32),
            jax.ShapeDtypeStruct((rank, rows), F32),
            jax.ShapeDtypeStruct((2 * rank, rows), BF16),
            jax.ShapeDtypeStruct((2 * rank, count), BF16),
        ],
        compiler_params=params(),
        cost_estimate=cost(SMALL),
        name="given_far",
    )(here_l, other_l, hidden_t, feedback, tokens)


def keep_far_kernel(left_sum, lhs, rhs, feedback, tokens, keep, gram):
    core = lax.axis_index("dp")
    for index in range(keep.shape[0]):
        keep[index] = block_sum(lhs, rhs, feedback, tokens, core, index + 2, keep.shape[2])
    left_t = left_sum[...]
    gram[...] = lax.dot_general(
        left_t, left_t, (((1,), (1,)), ((), ())), precision=HIGHEST, preferred_element_type=F32
    )


def kept_far(left_sum, lhs, rhs, feedback, tokens, chips):
    rank = left_sum.shape[0]
    return pl.pallas_call(
        keep_far_kernel,
        in_specs=[pl.BlockSpec(memory_space=pltpu.VMEM)] * 5,
        out_specs=[pl.BlockSpec(memory_space=pltpu.VMEM)] * 2,
        out_shape=[
            jax.ShapeDtypeStruct((chips // 2 - 2, rank, tokens.shape[1] // chips), F32),
            jax.ShapeDtypeStruct((rank, rank), F32),
        ],
        compiler_params=params(),
        cost_estimate=cost(SMALL),
        name="kept_far",
    )(left_sum, lhs, rhs, feedback, tokens)


def near_kernel(lhs, rhs, feedback, tokens, give, keep):
    core = lax.axis_index("dp")
    for target, owner in ((give, 1 - core), (keep, core)):
        for index in range(2):
            target[index] = block_sum(lhs, rhs, feedback, tokens, owner, index, target.shape[2])


def near_terms(lhs, rhs, feedback, tokens, chips):
    block = jax.ShapeDtypeStruct((2, lhs.shape[0] // 2, tokens.shape[1] // chips), F32)
    return pl.pallas_call(
        near_kernel,
        in_specs=[pl.BlockSpec(memory_space=pltpu.VMEM)] * 4,
        out_specs=[pl.BlockSpec(memory_space=pltpu.VMEM)] * 2,
        out_shape=[block, block],
        compiler_params=params(),
        cost_estimate=cost(SMALL),
        name="near_terms",
    )(lhs, rhs, feedback, tokens)


def merged_kernel(hidden_t, feedback, tokens, merged):
    cols = tokens.shape[1] // STEPS
    for step in range(STEPS):
        span = slice(step * cols, (step + 1) * cols)
        merged[:, span] = nn(hidden_t[...], tokens[:, span]) + feedback[:, span].astype(F32)


def merged_sum(hidden_t, feedback, tokens):
    return pl.pallas_call(
        merged_kernel,
        in_specs=[pl.BlockSpec(memory_space=pltpu.VMEM)] * 3,
        out_specs=pl.BlockSpec(memory_space=pltpu.VMEM),
        out_shape=jax.ShapeDtypeStruct(feedback.shape, F32),
        compiler_params=params(),
        cost_estimate=cost(SMALL),
        name="merged",
    )(hidden_t, feedback, tokens)


def put_message(message, value, gram):
    rank = gram.shape[0]
    blocks = value.shape[1] // rank
    rows = rank // blocks
    message[:rank, :] = value
    for block in range(blocks):
        message[rank:, block * rank : (block + 1) * rank] = gram[block * rows : (block + 1) * rows, :]


def begin_kernel(keep, got, gram, *messages):
    core = lax.axis_index("dp")
    for pair, message in enumerate(messages):
        index = 2 * pair + core
        put_message(message, keep[index] + got[index], gram)


def begin_messages(keep, got, gram):
    rank, cols = keep.shape[1:]
    pairs = keep.shape[0] // 2
    rows = rank + rank // (cols // rank)
    return pl.pallas_call(
        begin_kernel,
        in_specs=[pl.BlockSpec(memory_space=pltpu.VMEM)] * 3,
        out_specs=[pl.BlockSpec(memory_space=pltpu.VMEM)] * pairs,
        out_shape=[jax.ShapeDtypeStruct((rows, cols), F32)] * pairs,
        compiler_params=params(),
        cost_estimate=cost(SMALL),
        name="begin_messages",
    )(keep, got, gram)


def rest_kernel(keep_far, got_far, keep, got, gram, own, beside, *messages):
    first = lax.axis_index("dp") == 0
    put_message(own, keep[0] + got[0], gram)
    put_message(beside, keep[1] + got[1], gram)
    for pair in range(len(messages) // 2):
        direct = keep_far[2 * pair + 1] + got_far[2 * pair + 1]
        crossing = keep_far[2 * pair] + got_far[2 * pair]
        if pair == 0:
            direct = jnp.where(first, direct, keep[0] + got[0])
            crossing = jnp.where(first, keep[1] + got[1], crossing)
        put_message(messages[2 * pair], direct, gram)
        put_message(messages[2 * pair + 1], crossing, gram)


def rest_messages(keep_far, got_far, keep, got, gram):
    rank, cols = keep.shape[1:]
    count = 2 + keep_far.shape[0]
    rows = rank + rank // (cols // rank)
    own, beside, *messages = pl.pallas_call(
        rest_kernel,
        in_specs=[pl.BlockSpec(memory_space=pltpu.VMEM)] * 5,
        out_specs=[pl.BlockSpec(memory_space=pltpu.VMEM)] * count,
        out_shape=[jax.ShapeDtypeStruct((rows, cols), F32)] * count,
        compiler_params=params(),
        cost_estimate=cost(SMALL),
        name="rest_messages",
    )(keep_far, got_far, keep, got, gram)
    return own, beside, messages[::2], messages[1::2]


def cross_kernel(message, passed, total):
    total[...] = message[...] + jnp.where(lax.axis_index("dp") == 0, 0.0, passed[...])


def crossing(message, passed):
    return pl.pallas_call(
        cross_kernel,
        in_specs=[pl.BlockSpec(memory_space=pltpu.VMEM)] * 2,
        out_specs=pl.BlockSpec(memory_space=pltpu.VMEM),
        out_shape=jax.ShapeDtypeStruct(message.shape, F32),
        compiler_params=params(),
        cost_estimate=cost(SMALL),
        name="crossing",
    )(message, passed)


def core_sum_kernel(own, third, *refs):
    messages, total = refs[:-1], refs[-1]
    pairs = len(messages) // 3
    begun, direct, crossed = messages[:pairs], messages[pairs : 2 * pairs], messages[2 * pairs :]
    first = lax.axis_index("dp") == 0
    parts = [jnp.where(first, own[...] + crossed[0][...], direct[0][...] + third[...])]
    for pair in range(pairs):
        parts.append(jnp.where(first, begun[pair][...] + direct[pair][...], crossed[pair][...]))
    while len(parts) > 1:
        parts = [a + b for a, b in zip(parts[::2], parts[1::2])]
    total[...] = parts[0]


def core_sum(own, third, begun, direct, crossed):
    operands = [own, third, *begun, *direct, *crossed]
    return pl.pallas_call(
        core_sum_kernel,
        in_specs=[pl.BlockSpec(memory_space=pltpu.VMEM)] * len(operands),
        out_specs=pl.BlockSpec(memory_space=pltpu.VMEM),
        out_shape=jax.ShapeDtypeStruct(own.shape, F32),
        compiler_params=params(),
        cost_estimate=cost(SMALL),
        name="core_sum",
    )(*operands)


def choose_kernel(here, there, chosen):
    chosen[...] = jnp.where(lax.axis_index("dp") == 0, here[...], there[...])


def by_core(here, there):
    return pl.pallas_call(
        choose_kernel,
        in_specs=[pl.BlockSpec(memory_space=pltpu.VMEM)] * 2,
        out_specs=pl.BlockSpec(memory_space=pltpu.VMEM),
        out_shape=jax.ShapeDtypeStruct(here.shape, F32),
        compiler_params=params(),
        cost_estimate=cost(SMALL),
        name="by_core",
    )(here, there)


def join_kernel(share, third, *refs):
    shares, mine = refs[:-1], refs[-1]
    pairs = len(shares) // 2
    begun, direct = shares[:pairs], shares[pairs:]
    first = lax.axis_index("dp") == 0
    mine[0] = jnp.where(first, share[...], direct[0][...])
    mine[1] = jnp.where(first, begun[0][...], third[...])
    for pair in range(pairs):
        mine[pair + 2] = jnp.where(first, direct[pair][...], begun[pair][...])


def joined(share, third, begun, direct):
    operands = [share, third, *begun, *direct]
    return pl.pallas_call(
        join_kernel,
        in_specs=[pl.BlockSpec(memory_space=pltpu.VMEM)] * len(operands),
        out_specs=pl.BlockSpec(memory_space=pltpu.VMEM),
        out_shape=jax.ShapeDtypeStruct((len(begun) + 2, *share.shape), F32),
        compiler_params=params(),
        cost_estimate=cost(SMALL),
        name="joined",
    )(*operands)


def chip_sum_kernel(here, other, share, gram):
    total = here[...] + other[...]
    rank, cols = share.shape
    blocks = cols // rank
    rows = rank // blocks
    share[...] = total[:rank]
    for block in range(blocks):
        gram[block * rows : (block + 1) * rows, :] = total[rank:, block * rank : (block + 1) * rank]


def chip_sum(here, other, rank):
    return pl.pallas_call(
        chip_sum_kernel,
        in_specs=[pl.BlockSpec(memory_space=pltpu.VMEM)] * 2,
        out_specs=[pl.BlockSpec(memory_space=pltpu.VMEM)] * 2,
        out_shape=[
            jax.ShapeDtypeStruct((rank, here.shape[1]), F32),
            jax.ShapeDtypeStruct((rank, rank), F32),
        ],
        compiler_params=params(),
        cost_estimate=cost(SMALL),
        name="chip_sum",
    )(here, other)


def inverse_kernel(gram, inverse):
    rank = gram.shape[0]
    row = lax.broadcasted_iota(jnp.int32, (rank, 2 * rank), 0)
    lane = lax.broadcasted_iota(jnp.int32, (rank, 2 * rank), 1)
    eye = (lane[:, rank:] == row[:, rank:] + rank).astype(F32)
    table = jnp.concatenate([gram[...], eye], axis=1)
    done = []
    for start in range(0, rank, PIVOTS):
        below = row[start:]
        each = range(PIVOTS)
        lines = [table[k : k + 1, :] for k in each]
        columns = [jnp.broadcast_to(table[:, start + k : start + k + 1], table.shape) for k in each]
        change = None
        for k in each:
            top = columns[k][k : k + 1, :]
            reciprocal = 1.0 / top
            factor = jnp.where(below > start + k, columns[k] * reciprocal, 0.0)
            for m in range(k + 1, PIVOTS):
                entry = columns[m][k : k + 1, :]
                lines[m] = lines[m] - (entry * reciprocal) * lines[k]
                columns[m] = columns[m] - factor * entry
            done.append(lines[k] * lax.rsqrt(top))
            part = factor * lines[k]
            change = part if change is None else change + part
        table = (table - change)[PIVOTS:]
    inverse[...] = jnp.concatenate(done, axis=0)[:, rank:]


def cholesky_inverse(gram):
    return pl.pallas_call(
        inverse_kernel,
        in_specs=[pl.BlockSpec(memory_space=pltpu.VMEM)],
        out_specs=pl.BlockSpec(memory_space=pltpu.VMEM),
        out_shape=jax.ShapeDtypeStruct(gram.shape, F32),
        compiler_params=params(),
        cost_estimate=cost(5.0),
        name="cholesky_inverse",
    )(gram)


def spread(target, rows, value):
    rank = value.shape[1]
    high, low = split2(value)
    for place, term in enumerate((high, high, low, low)):
        target[rows, place * rank : (place + 1) * rank] = term


def operand_kernel(replicas, inverse, left_sum, lhs):
    rank, rows = left_sum.shape
    orth_t = jnp.dot(inverse[...], left_sum[...], precision=HIGHEST, preferred_element_type=F32)
    share = inverse[...] * (1.0 / replicas)
    weight_t = lax.dot_general(
        share, orth_t, (((0,), (0,)), ((), ())), precision=HIGHEST, preferred_element_type=F32
    )
    spread(lhs, slice(0, rows), -weight_t.T)
    spread(lhs, slice(rows, rows + rank), share)


def last_operand(inverse, left_sum, replicas):
    rank, rows = left_sum.shape
    return pl.pallas_call(
        functools.partial(operand_kernel, replicas),
        in_specs=[pl.BlockSpec(memory_space=pltpu.VMEM)] * 2,
        out_specs=pl.BlockSpec(memory_space=pltpu.VMEM),
        out_shape=jax.ShapeDtypeStruct((rows + rank, 4 * rank), BF16),
        compiler_params=params(),
        cost_estimate=cost(SMALL),
        name="last_operand",
    )(inverse, left_sum)


def final_kernel(indices, side, shares, lhs, merged, *refs):
    out, factor, rhs, out_here, factor_here, sems = refs[-6:]
    owner = lax.axis_index("dp") ^ side
    rows = merged.shape[0]
    rank, cols = shares.shape[1:]
    copies = []
    for block, (index, other) in enumerate(indices):
        place = jnp.where(owner == 0, place_of(0, index), place_of(1, other))
        span = columns_of(place, cols)
        high, low = split2(shares[block])
        for place, term in enumerate((high, low, high, low)):
            rhs[block % 2, place * rank : (place + 1) * rank, :] = term
        product = nn(lhs[...], rhs[block % 2])
        factor_here[block] = product[rows:]
        out_here[block] = (merged[:, span] + product[:rows]).astype(BF16)
        for number, (source, target) in enumerate(((out_here, out), (factor_here, factor))):
            copies.append(
                pltpu.make_async_copy(source.at[block], target.at[:, span], sems.at[block, number])
            )
            copies[-1].start()
    for copy in copies:
        copy.wait()


def finish(indices, shares, side, lhs, merged, begun=()):
    rank, cols = shares.shape[1:]
    rows, width = merged.shape
    blocks = len(indices)
    return pl.pallas_call(
        functools.partial(final_kernel, indices, side),
        in_specs=[pl.BlockSpec(memory_space=pltpu.VMEM)] * 3
        + [pl.BlockSpec(memory_space=pl.ANY)] * len(begun),
        out_specs=[pl.BlockSpec(memory_space=pl.ANY)] * 2,
        out_shape=[
            jax.ShapeDtypeStruct((rows, width), BF16),
            jax.ShapeDtypeStruct((rank, width), F32),
        ],
        input_output_aliases={3 + index: index for index in range(len(begun))},
        scratch_shapes=[
            pltpu.VMEM((2, lhs.shape[1], cols), BF16),
            pltpu.VMEM((blocks, rows, cols), BF16),
            pltpu.VMEM((blocks, rank, cols), F32),
            pltpu.SemaphoreType.DMA((blocks, 2)),
        ],
        compiler_params=params(),
        cost_estimate=cost(SMALL),
        name="finish",
    )(shares, lhs, merged, *begun)


def ring_order(chips):
    if chips == 8:
        return [0, 1, 3, 5, 7, 6, 4, 2]
    return list(range(chips))


def ring_gather(shard, chips, right_factor):
    order = ring_order(chips)

    def pairs(way):
        steps = ((0, way), (1, -way))
        return [
            (2 * order[i] + core, 2 * order[(i + step) % chips] + core)
            for i in range(chips)
            for core, step in steps
        ]

    halves = halves_of(shard)
    pieces = list(halves)
    origin = [(0, 0), (0, 1)]
    far = chips // 2
    later = relayed(halves)
    going = {(1, 0): halves[0], (-1, 1): halves[1], (1, 1): later[1], (-1, 0): later[0]}
    for hop in range(1, far + 1):
        for way, half in ((1, 0), (-1, 1), (1, 1), (-1, 0)):
            if hop == far and (half == 0) != (way == 1):
                continue
            going[way, half] = lax.ppermute(going[way, half], ("tp", "dp"), pairs(way))
            pieces.append(going[way, half])
            origin.append((-way * hop, half))
        if hop == far - 1:
            going[1, 0], right_factor = lax.optimization_barrier((going[1, 0], right_factor))
    return pieces, origin, right_factor


def swap(value):
    return lax.ppermute(value, "dp", [(0, 1), (1, 0)])


def local(grad_out, hidden, feedback, right_factor):
    shard, residue = grad_out[0], feedback[0]
    hidden_t = hidden[0].T
    chips, replicas = lax.axis_size("tp"), lax.axis_size("dp")
    rank = right_factor.shape[0]

    def send(value, first, second):
        pairs = []
        for chip in range(chips):
            for core, place in enumerate((first, second)):
                if place:
                    pairs.append((2 * chip + core, 2 * (chip ^ place) + core))
        return lax.ppermute(value, ("tp", "dp"), pairs)

    pieces, origins, right_factor = ring_gather(shard, chips, right_factor)
    terms, residue_t = residue_left(right_factor, residue)
    tokens, hidden_rows, left_t = early_left(origins, pieces[:-2], terms, residue_t, hidden_t)
    tokens, left_t = late_left(origins[-2:], pieces[-2:], terms, hidden_rows, left_t, tokens)
    give, left_sum, lhs, rhs = given_far(left_t, swap(left_t), hidden_t, residue, tokens, chips)
    got = swap(give)
    keep, gram = kept_far(left_sum, lhs, rhs, residue, tokens, chips)
    begin = begin_messages(keep, got, gram)
    give, keep_near = near_terms(lhs, rhs, residue, tokens, chips)
    own, beside, direct, cross = rest_messages(keep, got, keep_near, swap(give), gram)

    evens = range(4, chips, 4)
    begun = [send(value, place, 1) for value, place in zip(begin, evens)]
    direct = [send(value, place + 1, 2 * (place == 4)) for value, place in zip(direct, evens)]
    third = send(beside, 0, 3)
    cross = [crossing(value, passed) for value, passed in zip(cross, begun)]
    crossed = [send(value, int(place == 4), place + 2) for value, place in zip(cross, evens)]
    tokens, _ = lax.optimization_barrier((tokens, beside))
    merged = merged_sum(hidden_t, residue, tokens)
    third, merged = lax.optimization_barrier((third, merged))
    partial = core_sum(own, third, begun, direct, crossed)
    share, gram_matrix = chip_sum(partial, swap(partial), rank)

    begun = [send(share, int(place == 4), place + 2) for place in evens]
    direct = [send(share, place + 1, 2 * (place == 4)) for place in evens]
    third = send(share, 0, 3)
    passed = [send(by_core(share, value), place, 1) for value, place in zip(begun, evens)]
    inverse = cholesky_inverse(gram_matrix)
    inverse, begun, direct = lax.optimization_barrier((inverse, begun, direct))
    lhs = last_operand(inverse, left_sum, replicas)
    mine = joined(share, third, begun, direct)
    early = [(0, 0), (1, 1)] + [(index + 1, index) for index in range(2, chips // 2, 2)]
    late = [(index, index + 1) for index in range(2, chips // 2, 2)]
    done = finish(early, mine, 0, lhs, merged)
    passed, done = lax.optimization_barrier((passed, done))
    rest = passed[0][None] if len(passed) == 1 else jnp.stack(passed)
    theirs = swap(jnp.concatenate([mine, rest]))
    done = finish(late, rest, 0, lhs, merged, done)
    new_feedback, new_factor = finish(early + late, theirs, 1, lhs, merged, done)
    return new_feedback[None], new_factor


def solution(mesh):
    return jax.shard_map(
        local,
        mesh=mesh,
        in_specs=(
            P(("runs", "dp"), "tp", None),
            P(("runs", "dp"), None, "tp"),
            P(("runs", "dp"), "tp", None),
            P(),
        ),
        out_specs=(P(("runs", "dp"), "tp", None), P("runs", None)),
        check_vma=False,
    )
```

```python
import functools

import jax
import jax.numpy as jnp
from jax import lax
from jax.experimental import pallas as pl
from jax.experimental.pallas import tpu as pltpu
from jax.sharding import PartitionSpec as P

F32 = jnp.float32
BF16 = jnp.bfloat16
HIGHEST = lax.Precision.HIGHEST
VMEM_LIMIT = 24 * 1024 * 1024
STEPS = 4
SMALL = 0.05
PIVOTS = 8


def split2(value):
    high = value.astype(BF16)
    return high, (value - high.astype(F32)).astype(BF16)


def fold2(stacked):
    rank = stacked.shape[0] // 2
    return stacked[:rank] + stacked[rank:]


def nn(a, b):
    return lax.dot_general(a, b, (((1,), (0,)), ((), ())), preferred_element_type=F32)


def nt(a, b):
    return lax.dot_general(a, b, (((1,), (1,)), ((), ())), preferred_element_type=F32)


def params(semantics=None, limit=VMEM_LIMIT):
    return pltpu.CompilerParams(vmem_limit_bytes=limit, dimension_semantics=semantics)


def cost(microseconds):
    return pl.CostEstimate(flops=int(microseconds * 1.15e9), bytes_accessed=0, transcendentals=0)


def whole(shape):
    return pl.BlockSpec(shape, lambda *_: (0,) * len(shape))


def halves_kernel(shard, first, second):
    size = first.shape[0]
    first[...] = shard[:size, :]
    second[...] = shard[size:, :]


def halves_of(shard):
    half = jax.ShapeDtypeStruct((shard.shape[0] // 2, shard.shape[1]), BF16)
    return pl.pallas_call(
        halves_kernel,
        in_specs=[pl.BlockSpec(memory_space=pltpu.VMEM)],
        out_specs=[pl.BlockSpec(memory_space=pltpu.VMEM)] * 2,
        out_shape=[half, half],
        compiler_params=params(),
        cost_estimate=cost(4.0),
        name="halves",
    )(shard)


def relay_kernel(first, second, first_copy, second_copy):
    first_copy[...] = first[...]
    second_copy[...] = second[...]


def relayed(halves):
    return pl.pallas_call(
        relay_kernel,
        in_specs=[pl.BlockSpec(memory_space=pltpu.VMEM)] * 2,
        out_specs=[pl.BlockSpec(memory_space=pltpu.VMEM)] * 2,
        out_shape=[jax.ShapeDtypeStruct(half.shape, BF16) for half in halves],
        compiler_params=params(),
        cost_estimate=cost(2.2),
        name="relayed",
    )(*halves)


def residue_kernel(right, feedback, terms, left_t):
    cols = right.shape[1] // STEPS
    total = None
    for step in range(STEPS):
        span = slice(step * cols, (step + 1) * cols)
        stacked = jnp.concatenate(split2(right[:, span]), axis=0)
        terms[:, span] = stacked
        part = nt(stacked, feedback[:, span])
        total = part if total is None else total + part
    left_t[...] = fold2(total)


def residue_left(right, feedback):
    rank, width = right.shape
    rows = feedback.shape[0]
    return pl.pallas_call(
        residue_kernel,
        in_specs=[pl.BlockSpec(memory_space=pltpu.VMEM)] * 2,
        out_specs=[pl.BlockSpec(memory_space=pltpu.VMEM)] * 2,
        out_shape=[
            jax.ShapeDtypeStruct((2 * rank, width), BF16),
            jax.ShapeDtypeStruct((rank, rows), F32),
        ],
        compiler_params=params(),
        cost_estimate=cost(2.2),
        name="residue_left",
    )(right, feedback)


def ring_chip(position, chips):
    if chips != 8:
        return position
    up = jnp.where(position == 0, 0, 2 * position - 1)
    return jnp.where(position < 4, up, jnp.where(position == 4, 7, 2 * (8 - position)))


def ring_position(chip, chips):
    if chips != 8:
        return chip
    return jnp.where(chip % 2 == 1, (chip + 1) // 2, jnp.where(chip == 0, 0, 8 - chip // 2))


def piece_rows(origin, size):
    shift, half = origin
    chips = lax.axis_size("tp")
    sign = 1 - 2 * lax.axis_index("dp")
    position = ring_position(lax.axis_index("tp"), chips) + sign * shift + chips
    source = ring_chip(position % chips, chips)
    return pl.ds(pl.multiple_of((2 * source + half) * size, size), size)


def early_kernel(origins, *refs):
    pieces, (terms, residue_t, hidden_t, tokens, hidden, left_t) = refs[:-6], refs[-6:]
    size = pieces[0].shape[0]
    for index, origin in enumerate(origins):
        rows = piece_rows(origin, size)
        if index < len(pieces):
            tokens[rows, :] = pieces[index][...]
        else:
            tokens[rows, :] = jnp.zeros((size, tokens.shape[1]), BF16)
    projected = fold2(nt(terms[...], tokens[...]))
    stacked = jnp.concatenate(split2(projected), axis=0)
    left_t[...] = residue_t[...] + fold2(nt(stacked, hidden_t[...]))
    hidden[...] = hidden_t[...].T


def early_left(origins, pieces, terms, residue_t, hidden_t):
    rows, count = hidden_t.shape
    width = terms.shape[1]
    operands = [*pieces, terms, residue_t, hidden_t]
    return pl.pallas_call(
        functools.partial(early_kernel, origins),
        in_specs=[pl.BlockSpec(memory_space=pltpu.VMEM)] * len(operands),
        out_specs=[pl.BlockSpec(memory_space=pltpu.VMEM)] * 3,
        out_shape=[
            jax.ShapeDtypeStruct((count, width), BF16),
            jax.ShapeDtypeStruct((count, rows), BF16),
            jax.ShapeDtypeStruct(residue_t.shape, F32),
        ],
        compiler_params=params(),
        cost_estimate=cost(2.0),
        name="early_left",
    )(*operands)


def late_kernel(origins, first, second, terms, hidden, early_t, _, tokens, left_t):
    size = first.shape[0]
    seen = []
    for origin, piece in zip(origins, (first, second)):
        rows = piece_rows(origin, size)
        tokens[rows, :] = piece[...]
        seen.append(hidden[rows, :])
    projected = fold2(nt(terms[...], jnp.concatenate([first[...], second[...]], axis=0)))
    stacked = jnp.concatenate(split2(projected), axis=0)
    left_t[...] = early_t[...] + fold2(nn(stacked, jnp.concatenate(seen, axis=0)))


def late_left(origins, pieces, terms, hidden, early_t, tokens):
    operands = [*pieces, terms, hidden, early_t, tokens]
    return pl.pallas_call(
        functools.partial(late_kernel, origins),
        in_specs=[pl.BlockSpec(memory_space=pltpu.VMEM)] * len(operands),
        out_specs=[pl.BlockSpec(memory_space=pltpu.VMEM)] * 2,
        out_shape=[
            jax.ShapeDtypeStruct(tokens.shape, BF16),
            jax.ShapeDtypeStruct(early_t.shape, F32),
        ],
        input_output_aliases={len(operands) - 1: 0},
        compiler_params=params(),
        cost_estimate=cost(1.0),
        name="late_left",
    )(*operands)


def core_of(place):
    return (place >> 1) & 1


def index_of(place):
    return (place >> 2) * 2 + (place & 1)


def place_of(core, index):
    return (index >> 1) * 4 + core * 2 + (index & 1)


def columns_of(place, cols):
    shard = lax.axis_index("tp") ^ place
    return pl.ds(pl.multiple_of(shard * cols, cols), cols)


def block_sum(lhs, rhs, feedback, tokens, core, index, cols):
    span = columns_of(place_of(core, index), cols)
    return fold2(nn(lhs[...], feedback[:, span]) + nn(rhs[...], tokens[:, span]))


def give_far_kernel(here_l, other_l, hidden_t, feedback, tokens, give, left_sum, lhs, rhs):
    left_t = here_l[...] + other_l[...]
    left_sum[...] = left_t
    lhs[...] = jnp.concatenate(split2(left_t), axis=0)
    seen_t = fold2(nn(lhs[...], hidden_t[...]))
    rhs[...] = jnp.concatenate(split2(seen_t), axis=0)
    other = 1 - lax.axis_index("dp")
    for index in range(give.shape[0]):
        give[index] = block_sum(lhs, rhs, feedback, tokens, other, index + 2, give.shape[2])


def given_far(here_l, other_l, hidden_t, feedback, tokens, chips):
    rank, rows = here_l.shape
    count, width = tokens.shape
    return pl.pallas_call(
        give_far_kernel,
        in_specs=[pl.BlockSpec(memory_space=pltpu.VMEM)] * 5,
        out_specs=[pl.BlockSpec(memory_space=pltpu.VMEM)] * 4,
        out_shape=[
            jax.ShapeDtypeStruct((chips // 2 - 2, rank, width // chips), F32),
            jax.ShapeDtypeStruct((rank, rows), F32),
            jax.ShapeDtypeStruct((2 * rank, rows), BF16),
            jax.ShapeDtypeStruct((2 * rank, count), BF16),
        ],
        compiler_params=params(),
        cost_estimate=cost(SMALL),
        name="given_far",
    )(here_l, other_l, hidden_t, feedback, tokens)


def keep_far_kernel(left_sum, lhs, rhs, feedback, tokens, keep, gram):
    core = lax.axis_index("dp")
    for index in range(keep.shape[0]):
        keep[index] = block_sum(lhs, rhs, feedback, tokens, core, index + 2, keep.shape[2])
    left_t = left_sum[...]
    gram[...] = lax.dot_general(
        left_t, left_t, (((1,), (1,)), ((), ())), precision=HIGHEST, preferred_element_type=F32
    )


def kept_far(left_sum, lhs, rhs, feedback, tokens, chips):
    rank = left_sum.shape[0]
    return pl.pallas_call(
        keep_far_kernel,
        in_specs=[pl.BlockSpec(memory_space=pltpu.VMEM)] * 5,
        out_specs=[pl.BlockSpec(memory_space=pltpu.VMEM)] * 2,
        out_shape=[
            jax.ShapeDtypeStruct((chips // 2 - 2, rank, tokens.shape[1] // chips), F32),
            jax.ShapeDtypeStruct((rank, rank), F32),
        ],
        compiler_params=params(),
        cost_estimate=cost(SMALL),
        name="kept_far",
    )(left_sum, lhs, rhs, feedback, tokens)


def near_kernel(lhs, rhs, feedback, tokens, give, keep):
    core = lax.axis_index("dp")
    for target, owner in ((give, 1 - core), (keep, core)):
        for index in range(2):
            target[index] = block_sum(lhs, rhs, feedback, tokens, owner, index, target.shape[2])


def near_terms(lhs, rhs, feedback, tokens, chips):
    block = jax.ShapeDtypeStruct((2, lhs.shape[0] // 2, tokens.shape[1] // chips), F32)
    return pl.pallas_call(
        near_kernel,
        in_specs=[pl.BlockSpec(memory_space=pltpu.VMEM)] * 4,
        out_specs=[pl.BlockSpec(memory_space=pltpu.VMEM)] * 2,
        out_shape=[block, block],
        compiler_params=params(),
        cost_estimate=cost(SMALL),
        name="near_terms",
    )(lhs, rhs, feedback, tokens)


def merged_kernel(hidden_t, feedback, tokens, merged):
    cols = tokens.shape[1] // STEPS
    for step in range(STEPS):
        span = slice(step * cols, (step + 1) * cols)
        merged[:, span] = nn(hidden_t[...], tokens[:, span]) + feedback[:, span].astype(F32)


def merged_sum(hidden_t, feedback, tokens):
    return pl.pallas_call(
        merged_kernel,
        in_specs=[pl.BlockSpec(memory_space=pltpu.VMEM)] * 3,
        out_specs=pl.BlockSpec(memory_space=pltpu.VMEM),
        out_shape=jax.ShapeDtypeStruct(feedback.shape, F32),
        compiler_params=params(),
        cost_estimate=cost(SMALL),
        name="merged",
    )(hidden_t, feedback, tokens)


def put_message(message, value, gram):
    rank = gram.shape[0]
    blocks = value.shape[1] // rank
    rows = rank // blocks
    message[:rank, :] = value
    for block in range(blocks):
        message[rank:, block * rank : (block + 1) * rank] = gram[block * rows : (block + 1) * rows, :]


def begin_kernel(keep, got, gram, *messages):
    core = lax.axis_index("dp")
    for pair, message in enumerate(messages):
        index = 2 * pair + core
        put_message(message, keep[index] + got[index], gram)


def begin_messages(keep, got, gram):
    rank, cols = keep.shape[1:]
    pairs = keep.shape[0] // 2
    rows = rank + rank // (cols // rank)
    return pl.pallas_call(
        begin_kernel,
        in_specs=[pl.BlockSpec(memory_space=pltpu.VMEM)] * 3,
        out_specs=[pl.BlockSpec(memory_space=pltpu.VMEM)] * pairs,
        out_shape=[jax.ShapeDtypeStruct((rows, cols), F32)] * pairs,
        compiler_params=params(),
        cost_estimate=cost(SMALL),
        name="begin_messages",
    )(keep, got, gram)


def rest_kernel(keep_far, got_far, keep, got, gram, own, beside, *messages):
    first = lax.axis_index("dp") == 0
    put_message(own, keep[0] + got[0], gram)
    put_message(beside, keep[1] + got[1], gram)
    for pair in range(len(messages) // 2):
        direct = keep_far[2 * pair + 1] + got_far[2 * pair + 1]
        crossing = keep_far[2 * pair] + got_far[2 * pair]
        if pair == 0:
            direct = jnp.where(first, direct, keep[0] + got[0])
            crossing = jnp.where(first, keep[1] + got[1], crossing)
        put_message(messages[2 * pair], direct, gram)
        put_message(messages[2 * pair + 1], crossing, gram)


def rest_messages(keep_far, got_far, keep, got, gram):
    rank, cols = keep.shape[1:]
    count = 2 + keep_far.shape[0]
    rows = rank + rank // (cols // rank)
    own, beside, *messages = pl.pallas_call(
        rest_kernel,
        in_specs=[pl.BlockSpec(memory_space=pltpu.VMEM)] * 5,
        out_specs=[pl.BlockSpec(memory_space=pltpu.VMEM)] * count,
        out_shape=[jax.ShapeDtypeStruct((rows, cols), F32)] * count,
        compiler_params=params(),
        cost_estimate=cost(SMALL),
        name="rest_messages",
    )(keep_far, got_far, keep, got, gram)
    return own, beside, messages[::2], messages[1::2]


def cross_kernel(message, passed, total):
    total[...] = message[...] + jnp.where(lax.axis_index("dp") == 0, 0.0, passed[...])


def crossing(message, passed):
    return pl.pallas_call(
        cross_kernel,
        in_specs=[pl.BlockSpec(memory_space=pltpu.VMEM)] * 2,
        out_specs=pl.BlockSpec(memory_space=pltpu.VMEM),
        out_shape=jax.ShapeDtypeStruct(message.shape, F32),
        compiler_params=params(),
        cost_estimate=cost(SMALL),
        name="crossing",
    )(message, passed)


def core_sum_kernel(own, third, *refs):
    messages, total = refs[:-1], refs[-1]
    pairs = len(messages) // 3
    begun, direct, crossed = messages[:pairs], messages[pairs : 2 * pairs], messages[2 * pairs :]
    first = lax.axis_index("dp") == 0
    parts = [jnp.where(first, own[...] + crossed[0][...], direct[0][...] + third[...])]
    for pair in range(pairs):
        parts.append(jnp.where(first, begun[pair][...] + direct[pair][...], crossed[pair][...]))
    while len(parts) > 1:
        parts = [a + b for a, b in zip(parts[::2], parts[1::2])]
    total[...] = parts[0]


def core_sum(own, third, begun, direct, crossed):
    operands = [own, third, *begun, *direct, *crossed]
    return pl.pallas_call(
        core_sum_kernel,
        in_specs=[pl.BlockSpec(memory_space=pltpu.VMEM)] * len(operands),
        out_specs=pl.BlockSpec(memory_space=pltpu.VMEM),
        out_shape=jax.ShapeDtypeStruct(own.shape, F32),
        compiler_params=params(),
        cost_estimate=cost(SMALL),
        name="core_sum",
    )(*operands)


def choose_kernel(here, there, chosen):
    chosen[...] = jnp.where(lax.axis_index("dp") == 0, here[...], there[...])


def by_core(here, there):
    return pl.pallas_call(
        choose_kernel,
        in_specs=[pl.BlockSpec(memory_space=pltpu.VMEM)] * 2,
        out_specs=pl.BlockSpec(memory_space=pltpu.VMEM),
        out_shape=jax.ShapeDtypeStruct(here.shape, F32),
        compiler_params=params(),
        cost_estimate=cost(SMALL),
        name="by_core",
    )(here, there)


def join_kernel(share, third, *refs):
    shares, mine = refs[:-1], refs[-1]
    pairs = len(shares) // 2
    begun, direct = shares[:pairs], shares[pairs:]
    first = lax.axis_index("dp") == 0
    mine[0] = jnp.where(first, share[...], direct[0][...])
    mine[1] = jnp.where(first, begun[0][...], third[...])
    for pair in range(pairs):
        mine[pair + 2] = jnp.where(first, direct[pair][...], begun[pair][...])


def joined(share, third, begun, direct):
    operands = [share, third, *begun, *direct]
    return pl.pallas_call(
        join_kernel,
        in_specs=[pl.BlockSpec(memory_space=pltpu.VMEM)] * len(operands),
        out_specs=pl.BlockSpec(memory_space=pltpu.VMEM),
        out_shape=jax.ShapeDtypeStruct((len(begun) + 2, *share.shape), F32),
        compiler_params=params(),
        cost_estimate=cost(SMALL),
        name="joined",
    )(*operands)


def chip_sum_kernel(here, other, share, gram):
    total = here[...] + other[...]
    rank, cols = share.shape
    blocks = cols // rank
    rows = rank // blocks
    share[...] = total[:rank]
    for block in range(blocks):
        gram[block * rows : (block + 1) * rows, :] = total[rank:, block * rank : (block + 1) * rank]


def chip_sum(here, other, rank):
    return pl.pallas_call(
        chip_sum_kernel,
        in_specs=[pl.BlockSpec(memory_space=pltpu.VMEM)] * 2,
        out_specs=[pl.BlockSpec(memory_space=pltpu.VMEM)] * 2,
        out_shape=[
            jax.ShapeDtypeStruct((rank, here.shape[1]), F32),
            jax.ShapeDtypeStruct((rank, rank), F32),
        ],
        compiler_params=params(),
        cost_estimate=cost(SMALL),
        name="chip_sum",
    )(here, other)


def inverse_kernel(gram, inverse):
    rank = gram.shape[0]
    row = lax.broadcasted_iota(jnp.int32, (rank, 2 * rank), 0)
    lane = lax.broadcasted_iota(jnp.int32, (rank, 2 * rank), 1)
    eye = (lane[:, rank:] == row[:, rank:] + rank).astype(F32)
    table = jnp.concatenate([gram[...], eye], axis=1)
    done = []
    for start in range(0, rank, PIVOTS):
        below = row[start:]
        each = range(PIVOTS)
        lines = [table[k : k + 1, :] for k in each]
        columns = [jnp.broadcast_to(table[:, start + k : start + k + 1], table.shape) for k in each]
        change = None
        for k in each:
            top = columns[k][k : k + 1, :]
            reciprocal = 1.0 / top
            factor = jnp.where(below > start + k, columns[k] * reciprocal, 0.0)
            for m in range(k + 1, PIVOTS):
                entry = columns[m][k : k + 1, :]
                lines[m] = lines[m] - (entry * reciprocal) * lines[k]
                columns[m] = columns[m] - factor * entry
            done.append(lines[k] * lax.rsqrt(top))
            part = factor * lines[k]
            change = part if change is None else change + part
        table = (table - change)[PIVOTS:]
    inverse[...] = jnp.concatenate(done, axis=0)[:, rank:]


def cholesky_inverse(gram):
    return pl.pallas_call(
        inverse_kernel,
        in_specs=[pl.BlockSpec(memory_space=pltpu.VMEM)],
        out_specs=pl.BlockSpec(memory_space=pltpu.VMEM),
        out_shape=jax.ShapeDtypeStruct(gram.shape, F32),
        compiler_params=params(),
        cost_estimate=cost(5.0),
        name="cholesky_inverse",
    )(gram)


def spread(target, rows, value):
    rank = value.shape[1]
    high, low = split2(value)
    for place, term in enumerate((high, high, low, low)):
        target[rows, place * rank : (place + 1) * rank] = term


def operand_kernel(replicas, inverse, left_sum, lhs):
    rank, rows = left_sum.shape
    orth_t = jnp.dot(inverse[...], left_sum[...], precision=HIGHEST, preferred_element_type=F32)
    share = inverse[...] * (1.0 / replicas)
    weight_t = lax.dot_general(
        share, orth_t, (((0,), (0,)), ((), ())), precision=HIGHEST, preferred_element_type=F32
    )
    spread(lhs, slice(0, rows), -weight_t.T)
    spread(lhs, slice(rows, rows + rank), share)


def last_operand(inverse, left_sum, replicas):
    rank, rows = left_sum.shape
    return pl.pallas_call(
        functools.partial(operand_kernel, replicas),
        in_specs=[pl.BlockSpec(memory_space=pltpu.VMEM)] * 2,
        out_specs=pl.BlockSpec(memory_space=pltpu.VMEM),
        out_shape=jax.ShapeDtypeStruct((rows + rank, 4 * rank), BF16),
        compiler_params=params(),
        cost_estimate=cost(SMALL),
        name="last_operand",
    )(inverse, left_sum)


def final_kernel(indices, side, shares, lhs, merged, *refs):
    out, factor, rhs, out_here, factor_here, sems = refs[-6:]
    owner = lax.axis_index("dp") ^ side
    rows = merged.shape[0]
    rank, cols = shares.shape[1:]
    copies = []
    for block, (index, other) in enumerate(indices):
        place = jnp.where(owner == 0, place_of(0, index), place_of(1, other))
        span = columns_of(place, cols)
        high, low = split2(shares[block])
        for place, term in enumerate((high, low, high, low)):
            rhs[block % 2, place * rank : (place + 1) * rank, :] = term
        product = nn(lhs[...], rhs[block % 2])
        factor_here[block] = product[rows:]
        out_here[block] = (merged[:, span] + product[:rows]).astype(BF16)
        for number, (source, target) in enumerate(((out_here, out), (factor_here, factor))):
            copies.append(
                pltpu.make_async_copy(source.at[block], target.at[:, span], sems.at[block, number])
            )
            copies[-1].start()
    for copy in copies:
        copy.wait()


def finish(indices, shares, side, lhs, merged, begun=()):
    rank, cols = shares.shape[1:]
    rows, width = merged.shape
    blocks = len(indices)
    return pl.pallas_call(
        functools.partial(final_kernel, indices, side),
        in_specs=[pl.BlockSpec(memory_space=pltpu.VMEM)] * 3
        + [pl.BlockSpec(memory_space=pl.ANY)] * len(begun),
        out_specs=[pl.BlockSpec(memory_space=pl.ANY)] * 2,
        out_shape=[
            jax.ShapeDtypeStruct((rows, width), BF16),
            jax.ShapeDtypeStruct((rank, width), F32),
        ],
        input_output_aliases={3 + index: index for index in range(len(begun))},
        scratch_shapes=[
            pltpu.VMEM((2, lhs.shape[1], cols), BF16),
            pltpu.VMEM((blocks, rows, cols), BF16),
            pltpu.VMEM((blocks, rank, cols), F32),
            pltpu.SemaphoreType.DMA((blocks, 2)),
        ],
        compiler_params=params(),
        cost_estimate=cost(SMALL),
        name="finish",
    )(shares, lhs, merged, *begun)


def ring_order(chips):
    if chips == 8:
        return [0, 1, 3, 5, 7, 6, 4, 2]
    return list(range(chips))


def ring_gather(shard, chips, right_factor):
    order = ring_order(chips)

    def pairs(way):
        steps = ((0, way), (1, -way))
        return [
            (2 * order[i] + core, 2 * order[(i + step) % chips] + core)
            for i in range(chips)
            for core, step in steps
        ]

    halves = halves_of(shard)
    pieces = list(halves)
    origin = [(0, 0), (0, 1)]
    far = chips // 2
    later = relayed(halves)
    going = {(1, 0): halves[0], (-1, 1): halves[1], (1, 1): later[1], (-1, 0): later[0]}
    for hop in range(1, far + 1):
        for way, half in ((1, 0), (-1, 1), (1, 1), (-1, 0)):
            if hop == far and (half == 0) != (way == 1):
                continue
            going[way, half] = lax.ppermute(going[way, half], ("tp", "dp"), pairs(way))
            pieces.append(going[way, half])
            origin.append((-way * hop, half))
        if hop == far - 1:
            going[1, 0], right_factor = lax.optimization_barrier((going[1, 0], right_factor))
    return pieces, origin, right_factor


def swap(value):
    return lax.ppermute(value, "dp", [(0, 1), (1, 0)])


def local(grad_out, hidden, feedback, right_factor):
    shard, residue = grad_out[0], feedback[0]
    hidden_t = hidden[0].T
    chips, replicas = lax.axis_size("tp"), lax.axis_size("dp")
    rank = right_factor.shape[0]

    def send(value, first, second):
        pairs = []
        for chip in range(chips):
            for core, place in enumerate((first, second)):
                if place:
                    pairs.append((2 * chip + core, 2 * (chip ^ place) + core))
        return lax.ppermute(value, ("tp", "dp"), pairs)

    pieces, origins, right_factor = ring_gather(shard, chips, right_factor)
    terms, residue_t = residue_left(right_factor, residue)
    tokens, hidden_rows, left_t = early_left(origins, pieces[:-2], terms, residue_t, hidden_t)
    tokens, left_t = late_left(origins[-2:], pieces[-2:], terms, hidden_rows, left_t, tokens)
    give, left_sum, lhs, rhs = given_far(left_t, swap(left_t), hidden_t, residue, tokens, chips)
    got = swap(give)
    keep, gram = kept_far(left_sum, lhs, rhs, residue, tokens, chips)
    begin = begin_messages(keep, got, gram)
    give, keep_near = near_terms(lhs, rhs, residue, tokens, chips)
    own, beside, direct, cross = rest_messages(keep, got, keep_near, swap(give), gram)

    evens = range(4, chips, 4)
    begun = [send(value, place, 1) for value, place in zip(begin, evens)]
    direct = [send(value, place + 1, 2 * (place == 4)) for value, place in zip(direct, evens)]
    third = send(beside, 0, 3)
    cross = [crossing(value, passed) for value, passed in zip(cross, begun)]
    crossed = [send(value, int(place == 4), place + 2) for value, place in zip(cross, evens)]
    tokens, _ = lax.optimization_barrier((tokens, beside))
    merged = merged_sum(hidden_t, residue, tokens)
    third, merged = lax.optimization_barrier((third, merged))
    partial = core_sum(own, third, begun, direct, crossed)
    share, gram_matrix = chip_sum(partial, swap(partial), rank)

    begun = [send(share, int(place == 4), place + 2) for place in evens]
    direct = [send(share, place + 1, 2 * (place == 4)) for place in evens]
    third = send(share, 0, 3)
    passed = [send(by_core(share, value), place, 1) for value, place in zip(begun, evens)]
    inverse = cholesky_inverse(gram_matrix)
    inverse, begun = lax.optimization_barrier((inverse, begun))
    lhs = last_operand(inverse, left_sum, replicas)
    mine = joined(share, third, begun, direct)
    early = [(0, 0), (1, 1)] + [(index + 1, index) for index in range(2, chips // 2, 2)]
    late = [(index, index + 1) for index in range(2, chips // 2, 2)]
    done = finish(early, mine, 0, lhs, merged)
    passed, done = lax.optimization_barrier((passed, done))
    rest = passed[0][None] if len(passed) == 1 else jnp.stack(passed)
    theirs = swap(jnp.concatenate([mine, rest]))
    done = finish(late, rest, 0, lhs, merged, done)
    new_feedback, new_factor = finish(early + late, theirs, 1, lhs, merged, done)
    return new_feedback[None], new_factor


def solution(mesh):
    return jax.shard_map(
        local,
        mesh=mesh,
        in_specs=(
            P(("runs", "dp"), "tp", None),
            P(("runs", "dp"), None, "tp"),
            P(("runs", "dp"), "tp", None),
            P(),
        ),
        out_specs=(P(("runs", "dp"), "tp", None), P("runs", None)),
        check_vma=False,
    )
```

```python
import functools

import jax
import jax.numpy as jnp
from jax import lax
from jax.experimental import pallas as pl
from jax.experimental.pallas import tpu as pltpu
from jax.sharding import PartitionSpec as P

F32 = jnp.float32
BF16 = jnp.bfloat16
HIGHEST = lax.Precision.HIGHEST
VMEM_LIMIT = 24 * 1024 * 1024
STEPS = 4
SMALL = 0.05
PIVOTS = 8


def split2(value):
    high = value.astype(BF16)
    return high, (value - high.astype(F32)).astype(BF16)


def fold2(stacked):
    rank = stacked.shape[0] // 2
    return stacked[:rank] + stacked[rank:]


def nn(a, b):
    return lax.dot_general(a, b, (((1,), (0,)), ((), ())), preferred_element_type=F32)


def nt(a, b):
    return lax.dot_general(a, b, (((1,), (1,)), ((), ())), preferred_element_type=F32)


def params(semantics=None, limit=VMEM_LIMIT):
    return pltpu.CompilerParams(vmem_limit_bytes=limit, dimension_semantics=semantics)


def cost(microseconds):
    return pl.CostEstimate(flops=int(microseconds * 1.15e9), bytes_accessed=0, transcendentals=0)


def whole(shape):
    return pl.BlockSpec(shape, lambda *_: (0,) * len(shape))


def halves_kernel(shard, first, second):
    size = first.shape[0]
    first[...] = shard[:size, :]
    second[...] = shard[size:, :]


def halves_of(shard):
    half = jax.ShapeDtypeStruct((shard.shape[0] // 2, shard.shape[1]), BF16)
    return pl.pallas_call(
        halves_kernel,
        in_specs=[pl.BlockSpec(memory_space=pltpu.VMEM)],
        out_specs=[pl.BlockSpec(memory_space=pltpu.VMEM)] * 2,
        out_shape=[half, half],
        compiler_params=params(),
        cost_estimate=cost(4.0),
        name="halves",
    )(shard)


def relay_kernel(first, second, first_copy, second_copy):
    first_copy[...] = first[...]
    second_copy[...] = second[...]


def relayed(halves):
    return pl.pallas_call(
        relay_kernel,
        in_specs=[pl.BlockSpec(memory_space=pltpu.VMEM)] * 2,
        out_specs=[pl.BlockSpec(memory_space=pltpu.VMEM)] * 2,
        out_shape=[jax.ShapeDtypeStruct(half.shape, BF16) for half in halves],
        compiler_params=params(),
        cost_estimate=cost(2.2),
        name="relayed",
    )(*halves)


def residue_kernel(right, feedback, terms, left_t):
    cols = right.shape[1] // STEPS
    total = None
    for step in range(STEPS):
        span = slice(step * cols, (step + 1) * cols)
        stacked = jnp.concatenate(split2(right[:, span]), axis=0)
        terms[:, span] = stacked
        part = nt(stacked, feedback[:, span])
        total = part if total is None else total + part
    left_t[...] = fold2(total)


def residue_left(right, feedback):
    rank, width = right.shape
    rows = feedback.shape[0]
    return pl.pallas_call(
        residue_kernel,
        in_specs=[pl.BlockSpec(memory_space=pltpu.VMEM)] * 2,
        out_specs=[pl.BlockSpec(memory_space=pltpu.VMEM)] * 2,
        out_shape=[
            jax.ShapeDtypeStruct((2 * rank, width), BF16),
            jax.ShapeDtypeStruct((rank, rows), F32),
        ],
        compiler_params=params(),
        cost_estimate=cost(2.2),
        name="residue_left",
    )(right, feedback)


def ring_chip(position, chips):
    if chips != 8:
        return position
    up = jnp.where(position == 0, 0, 2 * position - 1)
    return jnp.where(position < 4, up, jnp.where(position == 4, 7, 2 * (8 - position)))


def ring_position(chip, chips):
    if chips != 8:
        return chip
    return jnp.where(chip % 2 == 1, (chip + 1) // 2, jnp.where(chip == 0, 0, 8 - chip // 2))


def piece_rows(origin, size):
    shift, half = origin
    chips = lax.axis_size("tp")
    sign = 1 - 2 * lax.axis_index("dp")
    position = ring_position(lax.axis_index("tp"), chips) + sign * shift + chips
    source = ring_chip(position % chips, chips)
    return pl.ds(pl.multiple_of((2 * source + half) * size, size), size)


def early_kernel(origins, *refs):
    pieces, (terms, residue_t, hidden_t, tokens, hidden, left_t) = refs[:-6], refs[-6:]
    size = pieces[0].shape[0]
    for index, origin in enumerate(origins):
        rows = piece_rows(origin, size)
        if index < len(pieces):
            tokens[rows, :] = pieces[index][...]
        else:
            tokens[rows, :] = jnp.zeros((size, tokens.shape[1]), BF16)
    projected = fold2(nt(terms[...], tokens[...]))
    stacked = jnp.concatenate(split2(projected), axis=0)
    left_t[...] = residue_t[...] + fold2(nt(stacked, hidden_t[...]))
    hidden[...] = hidden_t[...].T


def early_left(origins, pieces, terms, residue_t, hidden_t):
    rows, count = hidden_t.shape
    width = terms.shape[1]
    operands = [*pieces, terms, residue_t, hidden_t]
    return pl.pallas_call(
        functools.partial(early_kernel, origins),
        in_specs=[pl.BlockSpec(memory_space=pltpu.VMEM)] * len(operands),
        out_specs=[pl.BlockSpec(memory_space=pltpu.VMEM)] * 3,
        out_shape=[
            jax.ShapeDtypeStruct((count, width), BF16),
            jax.ShapeDtypeStruct((count, rows), BF16),
            jax.ShapeDtypeStruct(residue_t.shape, F32),
        ],
        compiler_params=params(),
        cost_estimate=cost(2.0),
        name="early_left",
    )(*operands)


def late_kernel(origins, first, second, terms, hidden, early_t, _, tokens, left_t, sems):
    size = first.shape[0]
    seen, copies = [], []
    for index, (origin, piece) in enumerate(zip(origins, (first, second))):
        rows = piece_rows(origin, size)
        copies.append(pltpu.make_async_copy(piece, tokens.at[rows, :], sems.at[index]))
        copies[-1].start()
        seen.append(hidden[rows, :])
    projected = fold2(nt(terms[...], jnp.concatenate([first[...], second[...]], axis=0)))
    stacked = jnp.concatenate(split2(projected), axis=0)
    left_t[...] = early_t[...] + fold2(nn(stacked, jnp.concatenate(seen, axis=0)))
    for copy in copies:
        copy.wait()


def late_left(origins, pieces, terms, hidden, early_t, tokens):
    operands = [*pieces, terms, hidden, early_t, tokens]
    return pl.pallas_call(
        functools.partial(late_kernel, origins),
        in_specs=[pl.BlockSpec(memory_space=pltpu.VMEM)] * (len(operands) - 1)
        + [pl.BlockSpec(memory_space=pl.ANY)],
        out_specs=[pl.BlockSpec(memory_space=pl.ANY), pl.BlockSpec(memory_space=pltpu.VMEM)],
        out_shape=[
            jax.ShapeDtypeStruct(tokens.shape, BF16),
            jax.ShapeDtypeStruct(early_t.shape, F32),
        ],
        input_output_aliases={len(operands) - 1: 0},
        scratch_shapes=[pltpu.SemaphoreType.DMA((2,))],
        compiler_params=params(),
        cost_estimate=cost(1.0),
        name="late_left",
    )(*operands)


def core_of(place):
    return (place >> 1) & 1


def index_of(place):
    return (place >> 2) * 2 + (place & 1)


def place_of(core, index):
    return (index >> 1) * 4 + core * 2 + (index & 1)


def columns_of(place, cols):
    shard = lax.axis_index("tp") ^ place
    return pl.ds(pl.multiple_of(shard * cols, cols), cols)


def block_sum(lhs, rhs, feedback, tokens, core, index, cols):
    span = columns_of(place_of(core, index), cols)
    return fold2(nn(lhs[...], feedback[:, span]) + nn(rhs[...], tokens[:, span]))


def give_far_kernel(here_l, other_l, hidden_t, feedback, tokens, give, left_sum, lhs, rhs):
    left_t = here_l[...] + other_l[...]
    left_sum[...] = left_t
    lhs[...] = jnp.concatenate(split2(left_t), axis=0)
    seen_t = fold2(nn(lhs[...], hidden_t[...]))
    rhs[...] = jnp.concatenate(split2(seen_t), axis=0)
    other = 1 - lax.axis_index("dp")
    for index in range(give.shape[0]):
        give[index] = block_sum(lhs, rhs, feedback, tokens, other, index + 2, give.shape[2])


def given_far(here_l, other_l, hidden_t, feedback, tokens, chips):
    rank, rows = here_l.shape
    count, width = tokens.shape
    return pl.pallas_call(
        give_far_kernel,
        in_specs=[pl.BlockSpec(memory_space=pltpu.VMEM)] * 5,
        out_specs=[pl.BlockSpec(memory_space=pltpu.VMEM)] * 4,
        out_shape=[
            jax.ShapeDtypeStruct((chips // 2 - 2, rank, width // chips), F32),
            jax.ShapeDtypeStruct((rank, rows), F32),
            jax.ShapeDtypeStruct((2 * rank, rows), BF16),
            jax.ShapeDtypeStruct((2 * rank, count), BF16),
        ],
        compiler_params=params(),
        cost_estimate=cost(SMALL),
        name="given_far",
    )(here_l, other_l, hidden_t, feedback, tokens)


def keep_far_kernel(left_sum, lhs, rhs, feedback, tokens, keep, gram):
    core = lax.axis_index("dp")
    for index in range(keep.shape[0]):
        keep[index] = block_sum(lhs, rhs, feedback, tokens, core, index + 2, keep.shape[2])
    left_t = left_sum[...]
    gram[...] = lax.dot_general(
        left_t, left_t, (((1,), (1,)), ((), ())), precision=HIGHEST, preferred_element_type=F32
    )


def kept_far(left_sum, lhs, rhs, feedback, tokens, chips):
    rank = left_sum.shape[0]
    return pl.pallas_call(
        keep_far_kernel,
        in_specs=[pl.BlockSpec(memory_space=pltpu.VMEM)] * 5,
        out_specs=[pl.BlockSpec(memory_space=pltpu.VMEM)] * 2,
        out_shape=[
            jax.ShapeDtypeStruct((chips // 2 - 2, rank, tokens.shape[1] // chips), F32),
            jax.ShapeDtypeStruct((rank, rank), F32),
        ],
        compiler_params=params(),
        cost_estimate=cost(SMALL),
        name="kept_far",
    )(left_sum, lhs, rhs, feedback, tokens)


def near_kernel(lhs, rhs, feedback, tokens, give, keep):
    core = lax.axis_index("dp")
    for target, owner in ((give, 1 - core), (keep, core)):
        for index in range(2):
            target[index] = block_sum(lhs, rhs, feedback, tokens, owner, index, target.shape[2])


def near_terms(lhs, rhs, feedback, tokens, chips):
    block = jax.ShapeDtypeStruct((2, lhs.shape[0] // 2, tokens.shape[1] // chips), F32)
    return pl.pallas_call(
        near_kernel,
        in_specs=[pl.BlockSpec(memory_space=pltpu.VMEM)] * 4,
        out_specs=[pl.BlockSpec(memory_space=pltpu.VMEM)] * 2,
        out_shape=[block, block],
        compiler_params=params(),
        cost_estimate=cost(SMALL),
        name="near_terms",
    )(lhs, rhs, feedback, tokens)


def merged_kernel(hidden_t, feedback, tokens, merged):
    cols = tokens.shape[1] // STEPS
    for step in range(STEPS):
        span = slice(step * cols, (step + 1) * cols)
        merged[:, span] = nn(hidden_t[...], tokens[:, span]) + feedback[:, span].astype(F32)


def merged_sum(hidden_t, feedback, tokens):
    return pl.pallas_call(
        merged_kernel,
        in_specs=[pl.BlockSpec(memory_space=pltpu.VMEM)] * 3,
        out_specs=pl.BlockSpec(memory_space=pltpu.VMEM),
        out_shape=jax.ShapeDtypeStruct(feedback.shape, F32),
        compiler_params=params(),
        cost_estimate=cost(SMALL),
        name="merged",
    )(hidden_t, feedback, tokens)


def put_message(message, value, gram):
    rank = gram.shape[0]
    blocks = value.shape[1] // rank
    rows = rank // blocks
    message[:rank, :] = value
    for block in range(blocks):
        message[rank:, block * rank : (block + 1) * rank] = gram[block * rows : (block + 1) * rows, :]


def begin_kernel(keep, got, gram, *messages):
    core = lax.axis_index("dp")
    for pair, message in enumerate(messages):
        index = 2 * pair + core
        put_message(message, keep[index] + got[index], gram)


def begin_messages(keep, got, gram):
    rank, cols = keep.shape[1:]
    pairs = keep.shape[0] // 2
    rows = rank + rank // (cols // rank)
    return pl.pallas_call(
        begin_kernel,
        in_specs=[pl.BlockSpec(memory_space=pltpu.VMEM)] * 3,
        out_specs=[pl.BlockSpec(memory_space=pltpu.VMEM)] * pairs,
        out_shape=[jax.ShapeDtypeStruct((rows, cols), F32)] * pairs,
        compiler_params=params(),
        cost_estimate=cost(SMALL),
        name="begin_messages",
    )(keep, got, gram)


def rest_kernel(keep_far, got_far, keep, got, gram, own, beside, *messages):
    first = lax.axis_index("dp") == 0
    put_message(own, keep[0] + got[0], gram)
    put_message(beside, keep[1] + got[1], gram)
    for pair in range(len(messages) // 2):
        direct = keep_far[2 * pair + 1] + got_far[2 * pair + 1]
        crossing = keep_far[2 * pair] + got_far[2 * pair]
        if pair == 0:
            direct = jnp.where(first, direct, keep[0] + got[0])
            crossing = jnp.where(first, keep[1] + got[1], crossing)
        put_message(messages[2 * pair], direct, gram)
        put_message(messages[2 * pair + 1], crossing, gram)


def rest_messages(keep_far, got_far, keep, got, gram):
    rank, cols = keep.shape[1:]
    count = 2 + keep_far.shape[0]
    rows = rank + rank // (cols // rank)
    own, beside, *messages = pl.pallas_call(
        rest_kernel,
        in_specs=[pl.BlockSpec(memory_space=pltpu.VMEM)] * 5,
        out_specs=[pl.BlockSpec(memory_space=pltpu.VMEM)] * count,
        out_shape=[jax.ShapeDtypeStruct((rows, cols), F32)] * count,
        compiler_params=params(),
        cost_estimate=cost(SMALL),
        name="rest_messages",
    )(keep_far, got_far, keep, got, gram)
    return own, beside, messages[::2], messages[1::2]


def cross_kernel(message, passed, total):
    total[...] = message[...] + jnp.where(lax.axis_index("dp") == 0, 0.0, passed[...])


def crossing(message, passed):
    return pl.pallas_call(
        cross_kernel,
        in_specs=[pl.BlockSpec(memory_space=pltpu.VMEM)] * 2,
        out_specs=pl.BlockSpec(memory_space=pltpu.VMEM),
        out_shape=jax.ShapeDtypeStruct(message.shape, F32),
        compiler_params=params(),
        cost_estimate=cost(SMALL),
        name="crossing",
    )(message, passed)


def core_sum_kernel(own, third, *refs):
    messages, total = refs[:-1], refs[-1]
    pairs = len(messages) // 3
    begun, direct, crossed = messages[:pairs], messages[pairs : 2 * pairs], messages[2 * pairs :]
    first = lax.axis_index("dp") == 0
    parts = [jnp.where(first, own[...] + crossed[0][...], direct[0][...] + third[...])]
    for pair in range(pairs):
        parts.append(jnp.where(first, begun[pair][...] + direct[pair][...], crossed[pair][...]))
    while len(parts) > 1:
        parts = [a + b for a, b in zip(parts[::2], parts[1::2])]
    total[...] = parts[0]


def core_sum(own, third, begun, direct, crossed):
    operands = [own, third, *begun, *direct, *crossed]
    return pl.pallas_call(
        core_sum_kernel,
        in_specs=[pl.BlockSpec(memory_space=pltpu.VMEM)] * len(operands),
        out_specs=pl.BlockSpec(memory_space=pltpu.VMEM),
        out_shape=jax.ShapeDtypeStruct(own.shape, F32),
        compiler_params=params(),
        cost_estimate=cost(SMALL),
        name="core_sum",
    )(*operands)


def choose_kernel(here, there, chosen):
    chosen[...] = jnp.where(lax.axis_index("dp") == 0, here[...], there[...])


def by_core(here, there):
    return pl.pallas_call(
        choose_kernel,
        in_specs=[pl.BlockSpec(memory_space=pltpu.VMEM)] * 2,
        out_specs=pl.BlockSpec(memory_space=pltpu.VMEM),
        out_shape=jax.ShapeDtypeStruct(here.shape, F32),
        compiler_params=params(),
        cost_estimate=cost(SMALL),
        name="by_core",
    )(here, there)


def join_kernel(share, third, *refs):
    shares, mine = refs[:-1], refs[-1]
    pairs = len(shares) // 2
    begun, direct = shares[:pairs], shares[pairs:]
    first = lax.axis_index("dp") == 0
    mine[0] = jnp.where(first, share[...], direct[0][...])
    mine[1] = jnp.where(first, begun[0][...], third[...])
    for pair in range(pairs):
        mine[pair + 2] = jnp.where(first, direct[pair][...], begun[pair][...])


def joined(share, third, begun, direct):
    operands = [share, third, *begun, *direct]
    return pl.pallas_call(
        join_kernel,
        in_specs=[pl.BlockSpec(memory_space=pltpu.VMEM)] * len(operands),
        out_specs=pl.BlockSpec(memory_space=pltpu.VMEM),
        out_shape=jax.ShapeDtypeStruct((len(begun) + 2, *share.shape), F32),
        compiler_params=params(),
        cost_estimate=cost(SMALL),
        name="joined",
    )(*operands)


def chip_sum_kernel(here, other, share, gram):
    total = here[...] + other[...]
    rank, cols = share.shape
    blocks = cols // rank
    rows = rank // blocks
    share[...] = total[:rank]
    for block in range(blocks):
        gram[block * rows : (block + 1) * rows, :] = total[rank:, block * rank : (block + 1) * rank]


def chip_sum(here, other, rank):
    return pl.pallas_call(
        chip_sum_kernel,
        in_specs=[pl.BlockSpec(memory_space=pltpu.VMEM)] * 2,
        out_specs=[pl.BlockSpec(memory_space=pltpu.VMEM)] * 2,
        out_shape=[
            jax.ShapeDtypeStruct((rank, here.shape[1]), F32),
            jax.ShapeDtypeStruct((rank, rank), F32),
        ],
        compiler_params=params(),
        cost_estimate=cost(SMALL),
        name="chip_sum",
    )(here, other)


def inverse_kernel(gram, inverse):
    rank = gram.shape[0]
    row = lax.broadcasted_iota(jnp.int32, (rank, 2 * rank), 0)
    lane = lax.broadcasted_iota(jnp.int32, (rank, 2 * rank), 1)
    eye = (lane[:, rank:] == row[:, rank:] + rank).astype(F32)
    table = jnp.concatenate([gram[...], eye], axis=1)
    done = []
    for start in range(0, rank, PIVOTS):
        below = row[start:]
        each = range(PIVOTS)
        lines = [table[k : k + 1, :] for k in each]
        columns = [jnp.broadcast_to(table[:, start + k : start + k + 1], table.shape) for k in each]
        change = None
        for k in each:
            top = columns[k][k : k + 1, :]
            reciprocal = 1.0 / top
            factor = jnp.where(below > start + k, columns[k] * reciprocal, 0.0)
            for m in range(k + 1, PIVOTS):
                entry = columns[m][k : k + 1, :]
                lines[m] = lines[m] - (entry * reciprocal) * lines[k]
                columns[m] = columns[m] - factor * entry
            done.append(lines[k] * lax.rsqrt(top))
            part = factor * lines[k]
            change = part if change is None else change + part
        table = (table - change)[PIVOTS:]
    inverse[...] = jnp.concatenate(done, axis=0)[:, rank:]


def cholesky_inverse(gram):
    return pl.pallas_call(
        inverse_kernel,
        in_specs=[pl.BlockSpec(memory_space=pltpu.VMEM)],
        out_specs=pl.BlockSpec(memory_space=pltpu.VMEM),
        out_shape=jax.ShapeDtypeStruct(gram.shape, F32),
        compiler_params=params(),
        cost_estimate=cost(5.0),
        name="cholesky_inverse",
    )(gram)


def spread(target, rows, value):
    rank = value.shape[1]
    high, low = split2(value)
    for place, term in enumerate((high, high, low, low)):
        target[rows, place * rank : (place + 1) * rank] = term


def operand_kernel(replicas, inverse, left_sum, lhs):
    rank, rows = left_sum.shape
    orth_t = jnp.dot(inverse[...], left_sum[...], precision=HIGHEST, preferred_element_type=F32)
    share = inverse[...] * (1.0 / replicas)
    weight_t = lax.dot_general(
        share, orth_t, (((0,), (0,)), ((), ())), precision=HIGHEST, preferred_element_type=F32
    )
    spread(lhs, slice(0, rows), -weight_t.T)
    spread(lhs, slice(rows, rows + rank), share)


def last_operand(inverse, left_sum, replicas):
    rank, rows = left_sum.shape
    return pl.pallas_call(
        functools.partial(operand_kernel, replicas),
        in_specs=[pl.BlockSpec(memory_space=pltpu.VMEM)] * 2,
        out_specs=pl.BlockSpec(memory_space=pltpu.VMEM),
        out_shape=jax.ShapeDtypeStruct((rows + rank, 4 * rank), BF16),
        compiler_params=params(),
        cost_estimate=cost(SMALL),
        name="last_operand",
    )(inverse, left_sum)


def final_kernel(indices, side, shares, lhs, merged, *refs):
    out, factor, rhs, out_here, factor_here, sems = refs[-6:]
    owner = lax.axis_index("dp") ^ side
    rows = merged.shape[0]
    rank, cols = shares.shape[1:]
    copies = []
    for block, (index, other) in enumerate(indices):
        place = jnp.where(owner == 0, place_of(0, index), place_of(1, other))
        span = columns_of(place, cols)
        high, low = split2(shares[block])
        for place, term in enumerate((high, low, high, low)):
            rhs[block % 2, place * rank : (place + 1) * rank, :] = term
        product = nn(lhs[...], rhs[block % 2])
        factor_here[block] = product[rows:]
        out_here[block] = (merged[:, span] + product[:rows]).astype(BF16)
        for number, (source, target) in enumerate(((out_here, out), (factor_here, factor))):
            copies.append(
                pltpu.make_async_copy(source.at[block], target.at[:, span], sems.at[block, number])
            )
            copies[-1].start()
    for copy in copies:
        copy.wait()


def finish(indices, shares, side, lhs, merged, begun=()):
    rank, cols = shares.shape[1:]
    rows, width = merged.shape
    blocks = len(indices)
    return pl.pallas_call(
        functools.partial(final_kernel, indices, side),
        in_specs=[pl.BlockSpec(memory_space=pltpu.VMEM)] * 3
        + [pl.BlockSpec(memory_space=pl.ANY)] * len(begun),
        out_specs=[pl.BlockSpec(memory_space=pl.ANY)] * 2,
        out_shape=[
            jax.ShapeDtypeStruct((rows, width), BF16),
            jax.ShapeDtypeStruct((rank, width), F32),
        ],
        input_output_aliases={3 + index: index for index in range(len(begun))},
        scratch_shapes=[
            pltpu.VMEM((2, lhs.shape[1], cols), BF16),
            pltpu.VMEM((blocks, rows, cols), BF16),
            pltpu.VMEM((blocks, rank, cols), F32),
            pltpu.SemaphoreType.DMA((blocks, 2)),
        ],
        compiler_params=params(),
        cost_estimate=cost(SMALL),
        name="finish",
    )(shares, lhs, merged, *begun)


def ring_order(chips):
    if chips == 8:
        return [0, 1, 3, 5, 7, 6, 4, 2]
    return list(range(chips))


def ring_gather(shard, chips, right_factor):
    order = ring_order(chips)

    def pairs(way):
        steps = ((0, way), (1, -way))
        return [
            (2 * order[i] + core, 2 * order[(i + step) % chips] + core)
            for i in range(chips)
            for core, step in steps
        ]

    halves = halves_of(shard)
    pieces = list(halves)
    origin = [(0, 0), (0, 1)]
    far = chips // 2
    later = relayed(halves)
    going = {(1, 0): halves[0], (-1, 1): halves[1], (1, 1): later[1], (-1, 0): later[0]}
    for hop in range(1, far + 1):
        for way, half in ((1, 0), (-1, 1), (1, 1), (-1, 0)):
            if hop == far and (half == 0) != (way == 1):
                continue
            going[way, half] = lax.ppermute(going[way, half], ("tp", "dp"), pairs(way))
            pieces.append(going[way, half])
            origin.append((-way * hop, half))
        if hop == far - 1:
            going[1, 0], right_factor = lax.optimization_barrier((going[1, 0], right_factor))
    return pieces, origin, right_factor


def swap(value):
    return lax.ppermute(value, "dp", [(0, 1), (1, 0)])


def local(grad_out, hidden, feedback, right_factor):
    shard, residue = grad_out[0], feedback[0]
    hidden_t = hidden[0].T
    chips, replicas = lax.axis_size("tp"), lax.axis_size("dp")
    rank = right_factor.shape[0]

    def send(value, first, second):
        pairs = []
        for chip in range(chips):
            for core, place in enumerate((first, second)):
                if place:
                    pairs.append((2 * chip + core, 2 * (chip ^ place) + core))
        return lax.ppermute(value, ("tp", "dp"), pairs)

    pieces, origins, right_factor = ring_gather(shard, chips, right_factor)
    terms, residue_t = residue_left(right_factor, residue)
    tokens, hidden_rows, left_t = early_left(origins, pieces[:-2], terms, residue_t, hidden_t)
    tokens, left_t = late_left(origins[-2:], pieces[-2:], terms, hidden_rows, left_t, tokens)
    give, left_sum, lhs, rhs = given_far(left_t, swap(left_t), hidden_t, residue, tokens, chips)
    got = swap(give)
    keep, gram = kept_far(left_sum, lhs, rhs, residue, tokens, chips)
    begin = begin_messages(keep, got, gram)
    give, keep_near = near_terms(lhs, rhs, residue, tokens, chips)
    own, beside, direct, cross = rest_messages(keep, got, keep_near, swap(give), gram)

    evens = range(4, chips, 4)
    begun = [send(value, place, 1) for value, place in zip(begin, evens)]
    direct = [send(value, place + 1, 2 * (place == 4)) for value, place in zip(direct, evens)]
    third = send(beside, 0, 3)
    cross = [crossing(value, passed) for value, passed in zip(cross, begun)]
    crossed = [send(value, int(place == 4), place + 2) for value, place in zip(cross, evens)]
    tokens, _ = lax.optimization_barrier((tokens, beside))
    merged = merged_sum(hidden_t, residue, tokens)
    third, merged = lax.optimization_barrier((third, merged))
    partial = core_sum(own, third, begun, direct, crossed)
    share, gram_matrix = chip_sum(partial, swap(partial), rank)

    begun = [send(share, int(place == 4), place + 2) for place in evens]
    direct = [send(share, place + 1, 2 * (place == 4)) for place in evens]
    third = send(share, 0, 3)
    passed = [send(by_core(share, value), place, 1) for value, place in zip(begun, evens)]
    inverse = cholesky_inverse(gram_matrix)
    inverse, begun = lax.optimization_barrier((inverse, begun))
    lhs = last_operand(inverse, left_sum, replicas)
    mine = joined(share, third, begun, direct)
    early = [(0, 0), (1, 1)] + [(index + 1, index) for index in range(2, chips // 2, 2)]
    late = [(index, index + 1) for index in range(2, chips // 2, 2)]
    done = finish(early, mine, 0, lhs, merged)
    passed, done = lax.optimization_barrier((passed, done))
    rest = passed[0][None] if len(passed) == 1 else jnp.stack(passed)
    theirs = swap(jnp.concatenate([mine, rest]))
    done = finish(late, rest, 0, lhs, merged, done)
    new_feedback, new_factor = finish(early + late, theirs, 1, lhs, merged, done)
    return new_feedback[None], new_factor


def solution(mesh):
    return jax.shard_map(
        local,
        mesh=mesh,
        in_specs=(
            P(("runs", "dp"), "tp", None),
            P(("runs", "dp"), None, "tp"),
            P(("runs", "dp"), "tp", None),
            P(),
        ),
        out_specs=(P(("runs", "dp"), "tp", None), P("runs", None)),
        check_vma=False,
    )
```

```python
import functools

import jax
import jax.numpy as jnp
from jax import lax
from jax.experimental import pallas as pl
from jax.experimental.pallas import tpu as pltpu
from jax.sharding import PartitionSpec as P

F32 = jnp.float32
BF16 = jnp.bfloat16
HIGHEST = lax.Precision.HIGHEST
VMEM_LIMIT = 24 * 1024 * 1024
STEPS = 4
SMALL = 0.05
PIVOTS = 8


def split2(value):
    high = value.astype(BF16)
    return high, (value - high.astype(F32)).astype(BF16)


def fold2(stacked):
    rank = stacked.shape[0] // 2
    return stacked[:rank] + stacked[rank:]


def nn(a, b):
    return lax.dot_general(a, b, (((1,), (0,)), ((), ())), preferred_element_type=F32)


def nt(a, b):
    return lax.dot_general(a, b, (((1,), (1,)), ((), ())), preferred_element_type=F32)


def params(semantics=None, limit=VMEM_LIMIT):
    return pltpu.CompilerParams(vmem_limit_bytes=limit, dimension_semantics=semantics)


def cost(microseconds):
    return pl.CostEstimate(flops=int(microseconds * 1.15e9), bytes_accessed=0, transcendentals=0)


def whole(shape):
    return pl.BlockSpec(shape, lambda *_: (0,) * len(shape))


def halves_kernel(shard, first, second):
    size = first.shape[0]
    first[...] = shard[:size, :]
    second[...] = shard[size:, :]


def halves_of(shard):
    half = jax.ShapeDtypeStruct((shard.shape[0] // 2, shard.shape[1]), BF16)
    return pl.pallas_call(
        halves_kernel,
        in_specs=[pl.BlockSpec(memory_space=pltpu.VMEM)],
        out_specs=[pl.BlockSpec(memory_space=pltpu.VMEM)] * 2,
        out_shape=[half, half],
        compiler_params=params(),
        cost_estimate=cost(4.0),
        name="halves",
    )(shard)


def relay_kernel(first, second, first_copy, second_copy):
    first_copy[...] = first[...]
    second_copy[...] = second[...]


def relayed(halves):
    return pl.pallas_call(
        relay_kernel,
        in_specs=[pl.BlockSpec(memory_space=pltpu.VMEM)] * 2,
        out_specs=[pl.BlockSpec(memory_space=pltpu.VMEM)] * 2,
        out_shape=[jax.ShapeDtypeStruct(half.shape, BF16) for half in halves],
        compiler_params=params(),
        cost_estimate=cost(2.2),
        name="relayed",
    )(*halves)


def residue_kernel(right, feedback, terms, left_t):
    cols = right.shape[1] // STEPS
    total = None
    for step in range(STEPS):
        span = slice(step * cols, (step + 1) * cols)
        stacked = jnp.concatenate(split2(right[:, span]), axis=0)
        terms[:, span] = stacked
        part = nt(stacked, feedback[:, span])
        total = part if total is None else total + part
    left_t[...] = fold2(total)


def residue_left(right, feedback):
    rank, width = right.shape
    rows = feedback.shape[0]
    return pl.pallas_call(
        residue_kernel,
        in_specs=[pl.BlockSpec(memory_space=pltpu.VMEM)] * 2,
        out_specs=[pl.BlockSpec(memory_space=pltpu.VMEM)] * 2,
        out_shape=[
            jax.ShapeDtypeStruct((2 * rank, width), BF16),
            jax.ShapeDtypeStruct((rank, rows), F32),
        ],
        compiler_params=params(),
        cost_estimate=cost(2.2),
        name="residue_left",
    )(right, feedback)


def ring_chip(position, chips):
    if chips != 8:
        return position
    up = jnp.where(position == 0, 0, 2 * position - 1)
    return jnp.where(position < 4, up, jnp.where(position == 4, 7, 2 * (8 - position)))


def ring_position(chip, chips):
    if chips != 8:
        return chip
    return jnp.where(chip % 2 == 1, (chip + 1) // 2, jnp.where(chip == 0, 0, 8 - chip // 2))


def piece_rows(origin, size):
    shift, half = origin
    chips = lax.axis_size("tp")
    sign = 1 - 2 * lax.axis_index("dp")
    position = ring_position(lax.axis_index("tp"), chips) + sign * shift + chips
    source = ring_chip(position % chips, chips)
    return pl.ds(pl.multiple_of((2 * source + half) * size, size), size)


def early_kernel(origins, *refs):
    pieces, (terms, residue_t, hidden_t, tokens, hidden, left_t) = refs[:-6], refs[-6:]
    size = pieces[0].shape[0]
    for index, origin in enumerate(origins):
        rows = piece_rows(origin, size)
        if index < len(pieces):
            tokens[rows, :] = pieces[index][...]
        else:
            tokens[rows, :] = jnp.zeros((size, tokens.shape[1]), BF16)
    projected = fold2(nt(terms[...], tokens[...]))
    stacked = jnp.concatenate(split2(projected), axis=0)
    left_t[...] = residue_t[...] + fold2(nt(stacked, hidden_t[...]))
    hidden[...] = hidden_t[...].T


def early_left(origins, pieces, terms, residue_t, hidden_t):
    rows, count = hidden_t.shape
    width = terms.shape[1]
    operands = [*pieces, terms, residue_t, hidden_t]
    return pl.pallas_call(
        functools.partial(early_kernel, origins),
        in_specs=[pl.BlockSpec(memory_space=pltpu.VMEM)] * len(operands),
        out_specs=[pl.BlockSpec(memory_space=pltpu.VMEM)] * 3,
        out_shape=[
            jax.ShapeDtypeStruct((count, width), BF16),
            jax.ShapeDtypeStruct((count, rows), BF16),
            jax.ShapeDtypeStruct(residue_t.shape, F32),
        ],
        compiler_params=params(),
        cost_estimate=cost(2.0),
        name="early_left",
    )(*operands)


def late_kernel(origins, first, second, terms, hidden, early_t, left_t):
    size = first.shape[0]
    seen = [hidden[piece_rows(origin, size), :] for origin in origins]
    projected = fold2(nt(terms[...], jnp.concatenate([first[...], second[...]], axis=0)))
    stacked = jnp.concatenate(split2(projected), axis=0)
    left_t[...] = early_t[...] + fold2(nn(stacked, jnp.concatenate(seen, axis=0)))


def late_left(origins, pieces, terms, hidden, early_t):
    operands = [*pieces, terms, hidden, early_t]
    return pl.pallas_call(
        functools.partial(late_kernel, origins),
        in_specs=[pl.BlockSpec(memory_space=pltpu.VMEM)] * len(operands),
        out_specs=pl.BlockSpec(memory_space=pltpu.VMEM),
        out_shape=jax.ShapeDtypeStruct(early_t.shape, F32),
        compiler_params=params(),
        cost_estimate=cost(1.0),
        name="late_left",
    )(*operands)


def insert_kernel(origins, first, second, _, tokens, sems):
    copies = []
    for index, (origin, piece) in enumerate(zip(origins, (first, second))):
        rows = piece_rows(origin, piece.shape[0])
        copies.append(pltpu.make_async_copy(piece, tokens.at[rows, :], sems.at[index]))
        copies[-1].start()
    for copy in copies:
        copy.wait()


def inserted(origins, pieces, tokens):
    return pl.pallas_call(
        functools.partial(insert_kernel, origins),
        in_specs=[pl.BlockSpec(memory_space=pltpu.VMEM)] * 2 + [pl.BlockSpec(memory_space=pl.ANY)],
        out_specs=pl.BlockSpec(memory_space=pl.ANY),
        out_shape=jax.ShapeDtypeStruct(tokens.shape, BF16),
        input_output_aliases={2: 0},
        scratch_shapes=[pltpu.SemaphoreType.DMA((2,))],
        compiler_params=params(),
        cost_estimate=cost(0.4),
        name="inserted",
    )(*pieces, tokens)


def core_of(place):
    return (place >> 1) & 1


def index_of(place):
    return (place >> 2) * 2 + (place & 1)


def place_of(core, index):
    return (index >> 1) * 4 + core * 2 + (index & 1)


def columns_of(place, cols):
    shard = lax.axis_index("tp") ^ place
    return pl.ds(pl.multiple_of(shard * cols, cols), cols)


def block_sum(lhs, rhs, feedback, tokens, core, index, cols):
    span = columns_of(place_of(core, index), cols)
    return fold2(nn(lhs[...], feedback[:, span]) + nn(rhs[...], tokens[:, span]))


def give_far_kernel(here_l, other_l, hidden_t, feedback, tokens, give, left_sum, lhs, rhs):
    left_t = here_l[...] + other_l[...]
    left_sum[...] = left_t
    lhs[...] = jnp.concatenate(split2(left_t), axis=0)
    seen_t = fold2(nn(lhs[...], hidden_t[...]))
    rhs[...] = jnp.concatenate(split2(seen_t), axis=0)
    other = 1 - lax.axis_index("dp")
    for index in range(give.shape[0]):
        give[index] = block_sum(lhs, rhs, feedback, tokens, other, index + 2, give.shape[2])


def given_far(here_l, other_l, hidden_t, feedback, tokens, chips):
    rank, rows = here_l.shape
    count, width = tokens.shape
    return pl.pallas_call(
        give_far_kernel,
        in_specs=[pl.BlockSpec(memory_space=pltpu.VMEM)] * 5,
        out_specs=[pl.BlockSpec(memory_space=pltpu.VMEM)] * 4,
        out_shape=[
            jax.ShapeDtypeStruct((chips // 2 - 2, rank, width // chips), F32),
            jax.ShapeDtypeStruct((rank, rows), F32),
            jax.ShapeDtypeStruct((2 * rank, rows), BF16),
            jax.ShapeDtypeStruct((2 * rank, count), BF16),
        ],
        compiler_params=params(),
        cost_estimate=cost(SMALL),
        name="given_far",
    )(here_l, other_l, hidden_t, feedback, tokens)


def keep_far_kernel(left_sum, lhs, rhs, feedback, tokens, keep, gram):
    core = lax.axis_index("dp")
    for index in range(keep.shape[0]):
        keep[index] = block_sum(lhs, rhs, feedback, tokens, core, index + 2, keep.shape[2])
    left_t = left_sum[...]
    gram[...] = lax.dot_general(
        left_t, left_t, (((1,), (1,)), ((), ())), precision=HIGHEST, preferred_element_type=F32
    )


def kept_far(left_sum, lhs, rhs, feedback, tokens, chips):
    rank = left_sum.shape[0]
    return pl.pallas_call(
        keep_far_kernel,
        in_specs=[pl.BlockSpec(memory_space=pltpu.VMEM)] * 5,
        out_specs=[pl.BlockSpec(memory_space=pltpu.VMEM)] * 2,
        out_shape=[
            jax.ShapeDtypeStruct((chips // 2 - 2, rank, tokens.shape[1] // chips), F32),
            jax.ShapeDtypeStruct((rank, rank), F32),
        ],
        compiler_params=params(),
        cost_estimate=cost(SMALL),
        name="kept_far",
    )(left_sum, lhs, rhs, feedback, tokens)


def near_kernel(lhs, rhs, feedback, tokens, give, keep):
    core = lax.axis_index("dp")
    for target, owner in ((give, 1 - core), (keep, core)):
        for index in range(2):
            target[index] = block_sum(lhs, rhs, feedback, tokens, owner, index, target.shape[2])


def near_terms(lhs, rhs, feedback, tokens, chips):
    block = jax.ShapeDtypeStruct((2, lhs.shape[0] // 2, tokens.shape[1] // chips), F32)
    return pl.pallas_call(
        near_kernel,
        in_specs=[pl.BlockSpec(memory_space=pltpu.VMEM)] * 4,
        out_specs=[pl.BlockSpec(memory_space=pltpu.VMEM)] * 2,
        out_shape=[block, block],
        compiler_params=params(),
        cost_estimate=cost(SMALL),
        name="near_terms",
    )(lhs, rhs, feedback, tokens)


def merged_kernel(hidden_t, feedback, tokens, merged):
    cols = tokens.shape[1] // STEPS
    for step in range(STEPS):
        span = slice(step * cols, (step + 1) * cols)
        merged[:, span] = nn(hidden_t[...], tokens[:, span]) + feedback[:, span].astype(F32)


def merged_sum(hidden_t, feedback, tokens):
    return pl.pallas_call(
        merged_kernel,
        in_specs=[pl.BlockSpec(memory_space=pltpu.VMEM)] * 3,
        out_specs=pl.BlockSpec(memory_space=pltpu.VMEM),
        out_shape=jax.ShapeDtypeStruct(feedback.shape, F32),
        compiler_params=params(),
        cost_estimate=cost(SMALL),
        name="merged",
    )(hidden_t, feedback, tokens)


def put_message(message, value, gram):
    rank = gram.shape[0]
    blocks = value.shape[1] // rank
    rows = rank // blocks
    message[:rank, :] = value
    for block in range(blocks):
        message[rank:, block * rank : (block + 1) * rank] = gram[block * rows : (block + 1) * rows, :]


def begin_kernel(keep, got, gram, *messages):
    core = lax.axis_index("dp")
    for pair, message in enumerate(messages):
        index = 2 * pair + core
        put_message(message, keep[index] + got[index], gram)


def begin_messages(keep, got, gram):
    rank, cols = keep.shape[1:]
    pairs = keep.shape[0] // 2
    rows = rank + rank // (cols // rank)
    return pl.pallas_call(
        begin_kernel,
        in_specs=[pl.BlockSpec(memory_space=pltpu.VMEM)] * 3,
        out_specs=[pl.BlockSpec(memory_space=pltpu.VMEM)] * pairs,
        out_shape=[jax.ShapeDtypeStruct((rows, cols), F32)] * pairs,
        compiler_params=params(),
        cost_estimate=cost(SMALL),
        name="begin_messages",
    )(keep, got, gram)


def rest_kernel(keep_far, got_far, keep, got, gram, own, beside, *messages):
    first = lax.axis_index("dp") == 0
    put_message(own, keep[0] + got[0], gram)
    put_message(beside, keep[1] + got[1], gram)
    for pair in range(len(messages) // 2):
        direct = keep_far[2 * pair + 1] + got_far[2 * pair + 1]
        crossing = keep_far[2 * pair] + got_far[2 * pair]
        if pair == 0:
            direct = jnp.where(first, direct, keep[0] + got[0])
            crossing = jnp.where(first, keep[1] + got[1], crossing)
        put_message(messages[2 * pair], direct, gram)
        put_message(messages[2 * pair + 1], crossing, gram)


def rest_messages(keep_far, got_far, keep, got, gram):
    rank, cols = keep.shape[1:]
    count = 2 + keep_far.shape[0]
    rows = rank + rank // (cols // rank)
    own, beside, *messages = pl.pallas_call(
        rest_kernel,
        in_specs=[pl.BlockSpec(memory_space=pltpu.VMEM)] * 5,
        out_specs=[pl.BlockSpec(memory_space=pltpu.VMEM)] * count,
        out_shape=[jax.ShapeDtypeStruct((rows, cols), F32)] * count,
        compiler_params=params(),
        cost_estimate=cost(SMALL),
        name="rest_messages",
    )(keep_far, got_far, keep, got, gram)
    return own, beside, messages[::2], messages[1::2]


def cross_kernel(message, passed, total):
    total[...] = message[...] + jnp.where(lax.axis_index("dp") == 0, 0.0, passed[...])


def crossing(message, passed):
    return pl.pallas_call(
        cross_kernel,
        in_specs=[pl.BlockSpec(memory_space=pltpu.VMEM)] * 2,
        out_specs=pl.BlockSpec(memory_space=pltpu.VMEM),
        out_shape=jax.ShapeDtypeStruct(message.shape, F32),
        compiler_params=params(),
        cost_estimate=cost(SMALL),
        name="crossing",
    )(message, passed)


def core_sum_kernel(own, third, *refs):
    messages, total = refs[:-1], refs[-1]
    pairs = len(messages) // 3
    begun, direct, crossed = messages[:pairs], messages[pairs : 2 * pairs], messages[2 * pairs :]
    first = lax.axis_index("dp") == 0
    parts = [jnp.where(first, own[...] + crossed[0][...], direct[0][...] + third[...])]
    for pair in range(pairs):
        parts.append(jnp.where(first, begun[pair][...] + direct[pair][...], crossed[pair][...]))
    while len(parts) > 1:
        parts = [a + b for a, b in zip(parts[::2], parts[1::2])]
    total[...] = parts[0]


def core_sum(own, third, begun, direct, crossed):
    operands = [own, third, *begun, *direct, *crossed]
    return pl.pallas_call(
        core_sum_kernel,
        in_specs=[pl.BlockSpec(memory_space=pltpu.VMEM)] * len(operands),
        out_specs=pl.BlockSpec(memory_space=pltpu.VMEM),
        out_shape=jax.ShapeDtypeStruct(own.shape, F32),
        compiler_params=params(),
        cost_estimate=cost(SMALL),
        name="core_sum",
    )(*operands)


def choose_kernel(here, there, chosen):
    chosen[...] = jnp.where(lax.axis_index("dp") == 0, here[...], there[...])


def by_core(here, there):
    return pl.pallas_call(
        choose_kernel,
        in_specs=[pl.BlockSpec(memory_space=pltpu.VMEM)] * 2,
        out_specs=pl.BlockSpec(memory_space=pltpu.VMEM),
        out_shape=jax.ShapeDtypeStruct(here.shape, F32),
        compiler_params=params(),
        cost_estimate=cost(SMALL),
        name="by_core",
    )(here, there)


def join_kernel(share, third, *refs):
    shares, mine = refs[:-1], refs[-1]
    pairs = len(shares) // 2
    begun, direct = shares[:pairs], shares[pairs:]
    first = lax.axis_index("dp") == 0
    mine[0] = jnp.where(first, share[...], direct[0][...])
    mine[1] = jnp.where(first, begun[0][...], third[...])
    for pair in range(pairs):
        mine[pair + 2] = jnp.where(first, direct[pair][...], begun[pair][...])


def joined(share, third, begun, direct):
    operands = [share, third, *begun, *direct]
    return pl.pallas_call(
        join_kernel,
        in_specs=[pl.BlockSpec(memory_space=pltpu.VMEM)] * len(operands),
        out_specs=pl.BlockSpec(memory_space=pltpu.VMEM),
        out_shape=jax.ShapeDtypeStruct((len(begun) + 2, *share.shape), F32),
        compiler_params=params(),
        cost_estimate=cost(SMALL),
        name="joined",
    )(*operands)


def chip_sum_kernel(here, other, share, gram):
    total = here[...] + other[...]
    rank, cols = share.shape
    blocks = cols // rank
    rows = rank // blocks
    share[...] = total[:rank]
    for block in range(blocks):
        gram[block * rows : (block + 1) * rows, :] = total[rank:, block * rank : (block + 1) * rank]


def chip_sum(here, other, rank):
    return pl.pallas_call(
        chip_sum_kernel,
        in_specs=[pl.BlockSpec(memory_space=pltpu.VMEM)] * 2,
        out_specs=[pl.BlockSpec(memory_space=pltpu.VMEM)] * 2,
        out_shape=[
            jax.ShapeDtypeStruct((rank, here.shape[1]), F32),
            jax.ShapeDtypeStruct((rank, rank), F32),
        ],
        compiler_params=params(),
        cost_estimate=cost(SMALL),
        name="chip_sum",
    )(here, other)


def inverse_kernel(gram, inverse):
    rank = gram.shape[0]
    row = lax.broadcasted_iota(jnp.int32, (rank, 2 * rank), 0)
    lane = lax.broadcasted_iota(jnp.int32, (rank, 2 * rank), 1)
    eye = (lane[:, rank:] == row[:, rank:] + rank).astype(F32)
    table = jnp.concatenate([gram[...], eye], axis=1)
    done = []
    for start in range(0, rank, PIVOTS):
        below = row[start:]
        each = range(PIVOTS)
        lines = [table[k : k + 1, :] for k in each]
        columns = [jnp.broadcast_to(table[:, start + k : start + k + 1], table.shape) for k in each]
        change = None
        for k in each:
            top = columns[k][k : k + 1, :]
            reciprocal = 1.0 / top
            factor = jnp.where(below > start + k, columns[k] * reciprocal, 0.0)
            for m in range(k + 1, PIVOTS):
                entry = columns[m][k : k + 1, :]
                lines[m] = lines[m] - (entry * reciprocal) * lines[k]
                columns[m] = columns[m] - factor * entry
            done.append(lines[k] * lax.rsqrt(top))
            part = factor * lines[k]
            change = part if change is None else change + part
        table = (table - change)[PIVOTS:]
    inverse[...] = jnp.concatenate(done, axis=0)[:, rank:]


def cholesky_inverse(gram):
    return pl.pallas_call(
        inverse_kernel,
        in_specs=[pl.BlockSpec(memory_space=pltpu.VMEM)],
        out_specs=pl.BlockSpec(memory_space=pltpu.VMEM),
        out_shape=jax.ShapeDtypeStruct(gram.shape, F32),
        compiler_params=params(),
        cost_estimate=cost(5.0),
        name="cholesky_inverse",
    )(gram)


def spread(target, rows, value):
    rank = value.shape[1]
    high, low = split2(value)
    for place, term in enumerate((high, high, low, low)):
        target[rows, place * rank : (place + 1) * rank] = term


def operand_kernel(replicas, inverse, left_sum, lhs):
    rank, rows = left_sum.shape
    orth_t = jnp.dot(inverse[...], left_sum[...], precision=HIGHEST, preferred_element_type=F32)
    share = inverse[...] * (1.0 / replicas)
    weight_t = lax.dot_general(
        share, orth_t, (((0,), (0,)), ((), ())), precision=HIGHEST, preferred_element_type=F32
    )
    spread(lhs, slice(0, rows), -weight_t.T)
    spread(lhs, slice(rows, rows + rank), share)


def last_operand(inverse, left_sum, replicas):
    rank, rows = left_sum.shape
    return pl.pallas_call(
        functools.partial(operand_kernel, replicas),
        in_specs=[pl.BlockSpec(memory_space=pltpu.VMEM)] * 2,
        out_specs=pl.BlockSpec(memory_space=pltpu.VMEM),
        out_shape=jax.ShapeDtypeStruct((rows + rank, 4 * rank), BF16),
        compiler_params=params(),
        cost_estimate=cost(SMALL),
        name="last_operand",
    )(inverse, left_sum)


def final_kernel(indices, side, shares, lhs, merged, *refs):
    out, factor, rhs, out_here, factor_here, sems = refs[-6:]
    owner = lax.axis_index("dp") ^ side
    rows = merged.shape[0]
    rank, cols = shares.shape[1:]
    copies = []
    for block, (index, other) in enumerate(indices):
        place = jnp.where(owner == 0, place_of(0, index), place_of(1, other))
        span = columns_of(place, cols)
        high, low = split2(shares[block])
        for place, term in enumerate((high, low, high, low)):
            rhs[block % 2, place * rank : (place + 1) * rank, :] = term
        product = nn(lhs[...], rhs[block % 2])
        factor_here[block] = product[rows:]
        out_here[block] = (merged[:, span] + product[:rows]).astype(BF16)
        for number, (source, target) in enumerate(((out_here, out), (factor_here, factor))):
            copies.append(
                pltpu.make_async_copy(source.at[block], target.at[:, span], sems.at[block, number])
            )
            copies[-1].start()
    for copy in copies:
        copy.wait()


def finish(indices, shares, side, lhs, merged, begun=()):
    rank, cols = shares.shape[1:]
    rows, width = merged.shape
    blocks = len(indices)
    return pl.pallas_call(
        functools.partial(final_kernel, indices, side),
        in_specs=[pl.BlockSpec(memory_space=pltpu.VMEM)] * 3
        + [pl.BlockSpec(memory_space=pl.ANY)] * len(begun),
        out_specs=[pl.BlockSpec(memory_space=pl.ANY)] * 2,
        out_shape=[
            jax.ShapeDtypeStruct((rows, width), BF16),
            jax.ShapeDtypeStruct((rank, width), F32),
        ],
        input_output_aliases={3 + index: index for index in range(len(begun))},
        scratch_shapes=[
            pltpu.VMEM((2, lhs.shape[1], cols), BF16),
            pltpu.VMEM((blocks, rows, cols), BF16),
            pltpu.VMEM((blocks, rank, cols), F32),
            pltpu.SemaphoreType.DMA((blocks, 2)),
        ],
        compiler_params=params(),
        cost_estimate=cost(SMALL),
        name="finish",
    )(shares, lhs, merged, *begun)


def ring_order(chips):
    if chips == 8:
        return [0, 1, 3, 5, 7, 6, 4, 2]
    return list(range(chips))


def ring_gather(shard, chips, right_factor):
    order = ring_order(chips)

    def pairs(way):
        steps = ((0, way), (1, -way))
        return [
            (2 * order[i] + core, 2 * order[(i + step) % chips] + core)
            for i in range(chips)
            for core, step in steps
        ]

    halves = halves_of(shard)
    pieces = list(halves)
    origin = [(0, 0), (0, 1)]
    far = chips // 2
    later = relayed(halves)
    going = {(1, 0): halves[0], (-1, 1): halves[1], (1, 1): later[1], (-1, 0): later[0]}
    for hop in range(1, far + 1):
        for way, half in ((1, 0), (-1, 1), (1, 1), (-1, 0)):
            if hop == far and (half == 0) != (way == 1):
                continue
            going[way, half] = lax.ppermute(going[way, half], ("tp", "dp"), pairs(way))
            pieces.append(going[way, half])
            origin.append((-way * hop, half))
        if hop == far - 1:
            going[1, 0], right_factor = lax.optimization_barrier((going[1, 0], right_factor))
    return pieces, origin, right_factor


def swap(value):
    return lax.ppermute(value, "dp", [(0, 1), (1, 0)])


def local(grad_out, hidden, feedback, right_factor):
    shard, residue = grad_out[0], feedback[0]
    hidden_t = hidden[0].T
    chips, replicas = lax.axis_size("tp"), lax.axis_size("dp")
    rank = right_factor.shape[0]

    def send(value, first, second):
        pairs = []
        for chip in range(chips):
            for core, place in enumerate((first, second)):
                if place:
                    pairs.append((2 * chip + core, 2 * (chip ^ place) + core))
        return lax.ppermute(value, ("tp", "dp"), pairs)

    pieces, origins, right_factor = ring_gather(shard, chips, right_factor)
    terms, residue_t = residue_left(right_factor, residue)
    tokens, hidden_rows, left_t = early_left(origins, pieces[:-2], terms, residue_t, hidden_t)
    left_t = late_left(origins[-2:], pieces[-2:], terms, hidden_rows, left_t)
    left_t, tokens = lax.optimization_barrier((left_t, tokens))
    tokens = inserted(origins[-2:], pieces[-2:], tokens)
    give, left_sum, lhs, rhs = given_far(left_t, swap(left_t), hidden_t, residue, tokens, chips)
    got = swap(give)
    keep, gram = kept_far(left_sum, lhs, rhs, residue, tokens, chips)
    begin = begin_messages(keep, got, gram)
    give, keep_near = near_terms(lhs, rhs, residue, tokens, chips)
    own, beside, direct, cross = rest_messages(keep, got, keep_near, swap(give), gram)

    evens = range(4, chips, 4)
    begun = [send(value, place, 1) for value, place in zip(begin, evens)]
    direct = [send(value, place + 1, 2 * (place == 4)) for value, place in zip(direct, evens)]
    third = send(beside, 0, 3)
    cross = [crossing(value, passed) for value, passed in zip(cross, begun)]
    crossed = [send(value, int(place == 4), place + 2) for value, place in zip(cross, evens)]
    tokens, _ = lax.optimization_barrier((tokens, beside))
    merged = merged_sum(hidden_t, residue, tokens)
    third, merged = lax.optimization_barrier((third, merged))
    partial = core_sum(own, third, begun, direct, crossed)
    share, gram_matrix = chip_sum(partial, swap(partial), rank)

    begun = [send(share, int(place == 4), place + 2) for place in evens]
    direct = [send(share, place + 1, 2 * (place == 4)) for place in evens]
    third = send(share, 0, 3)
    passed = [send(by_core(share, value), place, 1) for value, place in zip(begun, evens)]
    inverse = cholesky_inverse(gram_matrix)
    inverse, begun = lax.optimization_barrier((inverse, begun))
    lhs = last_operand(inverse, left_sum, replicas)
    mine = joined(share, third, begun, direct)
    early = [(0, 0), (1, 1)] + [(index + 1, index) for index in range(2, chips // 2, 2)]
    late = [(index, index + 1) for index in range(2, chips // 2, 2)]
    done = finish(early, mine, 0, lhs, merged)
    passed, done = lax.optimization_barrier((passed, done))
    rest = passed[0][None] if len(passed) == 1 else jnp.stack(passed)
    theirs = swap(jnp.concatenate([mine, rest]))
    done = finish(late, rest, 0, lhs, merged, done)
    new_feedback, new_factor = finish(early + late, theirs, 1, lhs, merged, done)
    return new_feedback[None], new_factor


def solution(mesh):
    return jax.shard_map(
        local,
        mesh=mesh,
        in_specs=(
            P(("runs", "dp"), "tp", None),
            P(("runs", "dp"), None, "tp"),
            P(("runs", "dp"), "tp", None),
            P(),
        ),
        out_specs=(P(("runs", "dp"), "tp", None), P("runs", None)),
        check_vma=False,
    )
```
